32 devices in a mesh: dp: 4 (over y, x), graph: 8 (over z, core).
Axes of the slice: x: 2, y: 2, z: 4, core: 2. Of those that a mesh axis runs over, the one named last changes fastest.
Arguments:
- edge_emb: bfloat16 [4, 4096, 512], P('dp', 'graph'), may hold values from -6 to 6
- atom_emb: bfloat16 [4, 256, 512], P('dp', 'graph'), may hold values from -6 to 6
- edge_target: int32 [4, 4096], P('dp', 'graph'), may hold values from 0 to 255, as said below
- trip_in: int32 [4, 131072], P('dp', 'graph'), may hold values from 0 to 4095, as said below
- trip_out: int32 [4, 131072], P('dp', 'graph'), may hold values from 0 to 511
- trip_count: int32 [4, 8], P('dp', 'graph'), may hold values from 8192 to 16384, as said below
- trip_basis: bfloat16 [4, 16, 131072], P('dp', None, 'graph'), may hold values from -3 to 3
- grad_edge: bfloat16 [4, 4096, 512], P('dp', 'graph'), may hold values from -6 to 6
- grad_atom: bfloat16 [4, 256, 512], P('dp', 'graph'), may hold values from -6 to 6
- w_down: bfloat16 [512, 64], replicated, may hold values from -0.25 to 0.25
- w_bil: bfloat16 [1024, 64], replicated, may hold values from -0.1875 to 0.1875
- w_up: bfloat16 [64, 512], replicated, may hold values from -0.75 to 0.75
- w_atom: bfloat16 [512, 512], replicated, may hold values from -0.25 to 0.25
Outputs:
- edge_new: bfloat16 [4, 4096, 512], P('dp', 'graph')
- atom_new: bfloat16 [4, 256, 512], P('dp', 'graph')
- grad_edge_in: float32 [4, 4096, 512], P('dp', 'graph')
- grad_wdown: float32 [512, 64], replicated
- grad_wbil: float32 [1024, 64], replicated
- grad_wup: float32 [64, 512], replicated
- grad_watom: float32 [512, 512], replicated
The draws below stay inside these ranges and needn't reach their ends.
Inputs may be any that keep to these rules, and one draw needn't show every extreme that they name: `trip_in`: among the 16384 slots of one device, the incoming edges held by any one device of the batch number at most 128 distinct ones; on every device some one device gives exactly 128. `trip_count`: every batch has a device with all 16384 slots used. `edge_target`: among the 512 edges of one device, those whose target atom is held by any one device (target // 32) number at most 128; on every device some one holder gets exactly 128.
All inputs are finite; a program needn't handle non-finite values.
Results may differ from the reference program's by a relative error of at most 0.0077.
Values may be sent and summed in bfloat16 or wider, within the bound.
No kernel may reach another device: no remote copies, remote signals or barrier semaphores. Data moves between devices by JAX's collectives and lax.ppermute only.
A program may use at most 64 MiB of HBM per device.

```python
import math
import jax
import jax.numpy as jnp
from jax import lax

D = 512
DT = 64
NB = 16
EDGE_DEV = 512
ATOM_DEV = 32
TRIP_DEV = 16384
CAP = 128
GROUPS = 4
GROUP = 8
ACAP = 128
EDGES_G = 4096
ATOMS_G = 256
TRIPLETS_G = 131072


def triplet_plan(key):
    base = jax.random.fold_in(key, 4242)
    subkeys = jax.random.split(base, 7)
    members = jnp.arange(GROUP, dtype=jnp.int32)
    counts = jax.random.randint(subkeys[0], (GROUPS, GROUP), TRIP_DEV // 2, TRIP_DEV + 1)
    fullest = jax.random.randint(subkeys[1], (GROUPS, 1), 0, GROUP)
    counts = jnp.where(members[None, :] == fullest, TRIP_DEV, counts)
    demand = jax.random.randint(subkeys[2], (GROUPS, GROUP, GROUP), 1, CAP + 1)
    busiest = jax.random.randint(subkeys[3], (GROUPS, GROUP, 1), 0, GROUP)
    demand = jnp.where(members[None, None, :] == busiest, CAP, demand)
    shuffles = jax.vmap(lambda subkey: jax.random.permutation(subkey, EDGE_DEV))(jax.random.split(subkeys[4], GROUPS * GROUP * GROUP))
    shuffles = shuffles.reshape(GROUPS, GROUP, GROUP, EDGE_DEV).astype(jnp.int32)
    bounds_end = jnp.cumsum(demand, axis=2)
    starts = bounds_end - demand
    totals = bounds_end[:, :, -1:]
    slot_ids = jnp.arange(TRIP_DEV, dtype=jnp.int32)[None, None, :]
    spare_pick = jax.random.randint(subkeys[5], (GROUPS, GROUP, TRIP_DEV), 0, 1 << 30) % totals
    wanted = jnp.where(slot_ids < totals, slot_ids, spare_pick)
    source = jax.vmap(lambda limits, picks: jnp.searchsorted(limits, picks, side='right'))(bounds_end.reshape(GROUPS * GROUP, GROUP), wanted.reshape(GROUPS * GROUP, TRIP_DEV))
    source = source.reshape(GROUPS, GROUP, TRIP_DEV).astype(jnp.int32)
    offsets = wanted - jnp.take_along_axis(starts, source, axis=2)
    group_axis = jnp.arange(GROUPS, dtype=jnp.int32)[:, None, None]
    device_axis = jnp.arange(GROUP, dtype=jnp.int32)[None, :, None]
    row_ids = shuffles[group_axis, device_axis, source, offsets]
    edge_ids = source * EDGE_DEV + row_ids
    scores = jax.random.randint(subkeys[6], (GROUPS, GROUP, TRIP_DEV), 0, TRIP_DEV)
    sort_key = jnp.where(slot_ids < counts[:, :, None], scores, TRIP_DEV + slot_ids)
    shuffle = jnp.argsort(sort_key, axis=2, stable=True)
    edge_ids = jnp.take_along_axis(edge_ids, shuffle, axis=2)
    return (edge_ids.reshape(GROUPS, GROUP * TRIP_DEV).astype(jnp.int32), counts.astype(jnp.int32))


def draw_trip_in(key, part):
    return triplet_plan(key)[0]


def draw_trip_count(key, part):
    return triplet_plan(key)[1]


def draw_edge_target(key, part):
    base = jax.random.fold_in(key, 7171)
    subkeys = jax.random.split(base, 4)
    lower = (EDGE_DEV + GROUP - 1) // GROUP
    demand = jax.random.randint(subkeys[0], (GROUPS, GROUP, GROUP), lower, ACAP + 1)
    demand = demand.at[:, :, 0].set(ACAP)
    ends = jnp.cumsum(demand, axis=2)
    slot_ids = jnp.arange(EDGE_DEV, dtype=jnp.int32)
    order_pos = jnp.sum((slot_ids[None, None, :, None] >= ends[:, :, None, :]).astype(jnp.int32), axis=3)
    first_owner = jax.random.randint(subkeys[1], (GROUPS, GROUP, 1), 0, GROUP)
    owner = (first_owner + order_pos) % GROUP
    local_atom = jax.random.randint(subkeys[2], (GROUPS, GROUP, EDGE_DEV), 0, ATOM_DEV)
    targets = owner * ATOM_DEV + local_atom
    shuffles = jax.vmap(lambda subkey: jax.random.permutation(subkey, EDGE_DEV))(jax.random.split(subkeys[3], GROUPS * GROUP)).reshape(GROUPS, GROUP, EDGE_DEV).astype(jnp.int32)
    targets = jnp.take_along_axis(targets, shuffles, axis=2)
    return targets.reshape(GROUPS, GROUP * EDGE_DEV).astype(jnp.int32)


def set_ends(entries, stream_key, least, top_value):
    longest = entries.shape.index(max(entries.shape))
    spots = []
    for shift in (0, 1):
        where = [jax.random.randint(jax.random.fold_in(stream_key, axis), (), 0, length) for axis, length in enumerate(entries.shape)]
        where[longest] = (where[longest] + shift) % entries.shape[longest]
        spots.append(tuple(where))
    return entries.at[spots[0]].set(least).at[spots[1]].set(top_value)


def shard_levels(key, extent, shards, smallest, high):
    factor_of, own = 1.0, jax.random.fold_in(key, 6)
    for axis_at, blocks in shards:
        draws = jnp.exp(jax.random.uniform(jax.random.fold_in(own, axis_at), (blocks,), jnp.float32, smallest / len(shards), high / len(shards)))
        factor_of = factor_of * jnp.repeat(draws, extent[axis_at] // blocks).reshape([-1 if axis == axis_at else 1 for axis in range(len(extent))])
    return factor_of


def bell_draw(own_key, dims, scale, most, shards=(), kind=jnp.bfloat16):
    entries = jax.random.normal(own_key, dims, jnp.float32) * scale
    if len(shards) > 0:
        entries = shard_levels(own_key, dims, shards, -0.22, 0.18) * entries
    return jnp.clip(entries, min=-most, max=most).astype(kind)


def setup_inputs(seed: int = 0) -> dict:
    splits = jax.random.split(jax.random.key(seed), 14)
    edge_emb = bell_draw(splits[0], (GROUPS, EDGES_G, D), 1.0, 6.0, ((0, 4), (1, 8)))
    atom_emb = bell_draw(splits[1], (GROUPS, ATOMS_G, D), 1.0, 6.0, ((0, 4), (1, 8)))
    edge_target = draw_edge_target(jax.random.fold_in(splits[13], 71), 0)
    trip_in = draw_trip_in(jax.random.fold_in(splits[13], 71), 0)
    trip_out = set_ends(jax.random.randint(splits[4], (GROUPS, TRIPLETS_G), 0, EDGE_DEV), jax.random.fold_in(splits[4], 1), 0, EDGE_DEV - 1).astype(jnp.int32)
    trip_count = draw_trip_count(jax.random.fold_in(splits[13], 71), 0)
    trip_basis = bell_draw(splits[6], (GROUPS, NB, TRIPLETS_G), 0.5, 3.0, ((0, 4), (2, 8)))
    grad_edge = bell_draw(splits[7], (GROUPS, EDGES_G, D), 1.0, 6.0, ((0, 4), (1, 8)))
    grad_atom = bell_draw(splits[8], (GROUPS, ATOMS_G, D), 1.0, 6.0, ((0, 4), (1, 8)))
    w_down = bell_draw(splits[9], (D, DT), D ** -0.5, 0.25)
    w_bil = bell_draw(splits[10], (NB * DT, DT), (NB * DT) ** -0.5, 0.1875)
    w_up = bell_draw(splits[11], (DT, D), DT ** -0.5, 0.75)
    w_atom = bell_draw(splits[12], (D, D), D ** -0.5, 0.25)
    return dict(edge_emb=edge_emb, atom_emb=atom_emb, edge_target=edge_target, trip_in=trip_in, trip_out=trip_out, trip_count=trip_count, trip_basis=trip_basis, grad_edge=grad_edge, grad_atom=grad_atom, w_down=w_down, w_bil=w_bil, w_up=w_up, w_atom=w_atom)


ATOM_SCALE = 0.25

def silu_slope(value):
    logistic = jax.nn.sigmoid(value)
    return logistic * (1.0 + value * (1.0 - logistic))

def spread_rows(basis_rows, feat_rows):
    outer = basis_rows.astype(jnp.float32)[:, :, None] * feat_rows.astype(jnp.float32)[:, None, :]
    return outer.reshape(basis_rows.shape[0], -1).astype(jnp.bfloat16)

def one_group(edge_emb, atom_emb, edge_target, trip_in, trip_out, trip_count, trip_basis, grad_edge, grad_atom, w_down, w_bil, w_up, w_atom):
    projected = jnp.dot(edge_emb, w_down, preferred_element_type=jnp.float32)
    edge_feat = jax.nn.silu(projected).astype(jnp.bfloat16)
    slot_ids = jnp.arange(TRIPLETS_G, dtype=jnp.int32)
    device = (slot_ids // TRIP_DEV).astype(jnp.int32)
    usable = slot_ids % TRIP_DEV < trip_count[device]
    out_edge = (device * EDGE_DEV + trip_out).astype(jnp.int32)
    feat_in = edge_feat[trip_in]
    basis_rows = trip_basis.T
    block_rows = math.gcd(TRIPLETS_G, 8192)
    feat_blocks = feat_in.reshape(-1, block_rows, DT)
    basis_blocks = basis_rows.reshape(-1, block_rows, NB)

    def forward_block(pair):
        return jnp.dot(spread_rows(pair[0], pair[1]), w_bil, preferred_element_type=jnp.float32)
    mixed = lax.map(forward_block, (basis_blocks, feat_blocks)).reshape(TRIPLETS_G, DT)
    mixed = jnp.where(usable[:, None], mixed, jnp.zeros((), jnp.float32))
    gathered = jax.ops.segment_sum(mixed, out_edge, num_segments=EDGES_G).astype(jnp.bfloat16)
    update = jnp.dot(gathered, w_up, preferred_element_type=jnp.float32)
    edge_new = (edge_emb.astype(jnp.float32) + jax.nn.silu(update)).astype(jnp.bfloat16)
    atom_sum = jax.ops.segment_sum(edge_new.astype(jnp.float32), edge_target, num_segments=ATOMS_G).astype(jnp.bfloat16)
    atom_pre = ATOM_SCALE * jnp.dot(atom_sum, w_atom, preferred_element_type=jnp.float32)
    atom_new = (atom_emb.astype(jnp.float32) + jax.nn.silu(atom_pre)).astype(jnp.bfloat16)
    grad_pre = (grad_atom.astype(jnp.float32) * silu_slope(atom_pre)).astype(jnp.bfloat16)
    watom_term = ATOM_SCALE * jnp.dot(atom_sum.T, grad_pre, preferred_element_type=jnp.float32)
    grad_sum = (ATOM_SCALE * jnp.dot(grad_pre, w_atom.T, preferred_element_type=jnp.float32)).astype(jnp.bfloat16)
    grad_new = grad_edge.astype(jnp.float32) + grad_sum[edge_target].astype(jnp.float32)
    grad_update = (grad_new * silu_slope(update)).astype(jnp.bfloat16)
    wup_term = jnp.dot(gathered.T, grad_update, preferred_element_type=jnp.float32)
    grad_gathered = jnp.dot(grad_update, w_up.T, preferred_element_type=jnp.float32).astype(jnp.bfloat16)
    grad_mixed = jnp.where(usable[:, None], grad_gathered[out_edge], jnp.zeros((), jnp.bfloat16))

    def backward_block(running, triple):
        basis_part, feat_part, grad_part = triple
        spread = spread_rows(basis_part, feat_part)
        running = running + jnp.dot(spread.T, grad_part, preferred_element_type=jnp.float32)
        backed = jnp.dot(grad_part, w_bil.T, preferred_element_type=jnp.float32).reshape(-1, NB, DT)
        feat_grad = lax.optimization_barrier(jnp.sum(basis_part.astype(jnp.float32)[:, :, None] * backed, axis=1))
        return (running, feat_grad)
    wbil_term, grad_feat = lax.scan(backward_block, jnp.zeros((NB * DT, DT), jnp.float32), (basis_blocks, feat_blocks, grad_mixed.reshape(-1, block_rows, DT)))
    grad_feat = grad_feat.reshape(TRIPLETS_G, DT)
    grad_edge_feat = jax.ops.segment_sum(grad_feat, trip_in, num_segments=EDGES_G)
    grad_project = (grad_edge_feat * silu_slope(projected)).astype(jnp.bfloat16)
    grad_edge_in = grad_new + jnp.dot(grad_project, w_down.T, preferred_element_type=jnp.float32)
    wdown_term = jnp.dot(edge_emb.T, grad_project, preferred_element_type=jnp.float32)
    return (edge_new, atom_new, grad_edge_in, wdown_term, wbil_term, wup_term, watom_term)

def reference(edge_emb, atom_emb, edge_target, trip_in, trip_out, trip_count, trip_basis, grad_edge, grad_atom, w_down, w_bil, w_up, w_atom):
    edge_list = []
    atom_list = []
    input_list = []
    sums = None
    for group in range(GROUPS):
        result = one_group(edge_emb[group], atom_emb[group], edge_target[group], trip_in[group], trip_out[group], trip_count[group], trip_basis[group], grad_edge[group], grad_atom[group], w_down, w_bil, w_up, w_atom)
        edge_list.append(result[0])
        atom_list.append(result[1])
        input_list.append(result[2])
        terms = result[3:]
        sums = terms if sums is None else tuple((left + right for left, right in zip(sums, terms)))
    factor = 1.0 / math.sqrt(GROUPS * EDGES_G)
    return (jnp.stack(edge_list), jnp.stack(atom_list), jnp.stack(input_list), sums[0] * factor, sums[1] * factor, sums[2] * factor, sums[3] * factor)
```

```python
import functools
import math

import jax
import jax.numpy as jnp
from jax import lax
from jax.experimental import pallas as pl
from jax.experimental.pallas import tpu as pltpu
from jax.sharding import PartitionSpec as P

ATOM_SCALE = 0.25
BLOCK = 256
TILE_LIMIT = 1024
VMEM_BYTES = 48 * 1024 * 1024

FIRST_FIRST = (((0,), (0,)), ((), ()))
FIRST_LAST = (((0,), (1,)), ((), ()))
LAST_LAST = (((1,), (1,)), ((), ()))


def dot32(left, right, dims=(((1,), (0,)), ((), ()))):
    return lax.dot_general(left, right, dims, preferred_element_type=jnp.float32)


def silu(value):
    return value / (1.0 + jnp.exp(-value))


def silu_slope(value):
    logistic = 1.0 / (1.0 + jnp.exp(-value))
    return logistic * (1.0 + value * (1.0 - logistic))


def row_hot(rows, index):
    iota = lax.broadcasted_iota(jnp.int32, (rows, index.shape[1]), 0)
    return (iota == index).astype(jnp.float32).astype(jnp.bfloat16)


def feature_kernel(emb_ref, down_ref, projected_ref, table_ref):
    projected = dot32(down_ref[...], emb_ref[...], FIRST_LAST)
    projected_ref[...] = projected
    feat = silu(projected).astype(jnp.bfloat16)
    width = feat.shape[0]
    for part in range(feat.shape[1] // BLOCK):
        table_ref[part * width : (part + 1) * width, :] = feat[:, part * BLOCK : (part + 1) * BLOCK]


def forward_kernel(
    count_ref,
    in_ref,
    out_ref,
    basis_ref,
    table_ref,
    bil_ref,
    up_ref,
    emb_ref,
    target_ref,
    new_ref,
    atoms_ref,
    gathered_ref,
    moment_ref,
    total,
    spread,
):
    step = pl.program_id(0)
    tile = in_ref.shape[1]
    width = bil_ref.shape[1]
    edges = emb_ref.shape[0]
    groups = table_ref.shape[0] // width

    @pl.when(step == 0)
    def _():
        total[...] = jnp.zeros_like(total)

    incoming = in_ref[...]
    low = incoming & (BLOCK - 1)
    high = incoming // BLOCK
    hot = row_hot(BLOCK, low)
    feat = jnp.zeros((width, tile), jnp.float32)
    per = BLOCK // width
    for chunk in range(groups // per):
        picked = dot32(table_ref[chunk * BLOCK : (chunk + 1) * BLOCK, :], hot)
        for part in range(per):
            feat = jnp.where(
                high == chunk * per + part, picked[part * width : (part + 1) * width, :], feat
            )
    feat = feat.astype(jnp.bfloat16)
    for row in range(basis_ref.shape[0]):
        spread[row * width : (row + 1) * width, :] = feat * basis_ref[row : row + 1, :]
    place = step * tile + lax.broadcasted_iota(jnp.int32, (1, tile), 1)
    outgoing = jnp.where(place < count_ref[0, 0], out_ref[...], -1)
    total[...] += dot32(spread[...], row_hot(edges, outgoing), LAST_LAST)

    @pl.when(step == pl.num_programs(0) - 1)
    def _():
        summed = total[...]
        head = summed.astype(jnp.bfloat16)
        rest = (summed - head.astype(jnp.float32)).astype(jnp.bfloat16)
        moment_ref[...] = head
        gathered = (
            dot32(bil_ref[...], head, FIRST_FIRST) + dot32(bil_ref[...], rest, FIRST_FIRST)
        ).astype(jnp.bfloat16)
        gathered_ref[...] = gathered
        update = dot32(gathered, up_ref[...], FIRST_FIRST)
        fresh = (emb_ref[...].astype(jnp.float32) + silu(update)).astype(jnp.bfloat16)
        new_ref[...] = fresh
        atoms_ref[...] = dot32(row_hot(atoms_ref.shape[0], target_ref[...]), fresh).astype(
            jnp.bfloat16
        )


def atom_kernel(parts_ref, emb_ref, grad_ref, weight_ref, new_ref, pair_ref, weight_grad_ref):
    total = parts_ref[0].astype(jnp.float32)
    for part in range(1, parts_ref.shape[0]):
        total = total + parts_ref[part].astype(jnp.float32)
    total = total.astype(jnp.bfloat16)
    pre = ATOM_SCALE * dot32(total, weight_ref[...])
    new_ref[...] = (emb_ref[...].astype(jnp.float32) + silu(pre)).astype(jnp.bfloat16)
    grad_pre = (grad_ref[...].astype(jnp.float32) * silu_slope(pre)).astype(jnp.bfloat16)
    pair_ref[...] = (ATOM_SCALE * dot32(grad_pre, weight_ref[...], LAST_LAST)).astype(jnp.bfloat16)
    weight_grad_ref[...] = (ATOM_SCALE * dot32(total, grad_pre, FIRST_FIRST)).astype(jnp.bfloat16)


def backward_kernel(
    count_ref,
    in_ref,
    out_ref,
    basis_ref,
    bil_ref,
    up_ref,
    gathered_ref,
    moment_ref,
    grad_edge_ref,
    grad_sum_ref,
    target_ref,
    grad_new_ref,
    up_grad_ref,
    bil_grad_ref,
    parts_ref,
    table,
    spread,
    total,
):
    step = pl.program_id(0)
    tile = in_ref.shape[1]
    width = bil_ref.shape[1]
    edges = grad_edge_ref.shape[0]
    groups = total.shape[0] // width

    @pl.when(step == 0)
    def _():
        total[...] = jnp.zeros_like(total)
        update = dot32(gathered_ref[...], up_ref[...], FIRST_FIRST)
        hot = row_hot(grad_sum_ref.shape[0], target_ref[...])
        grad_new = grad_edge_ref[...].astype(jnp.float32) + dot32(
            hot, grad_sum_ref[...], FIRST_FIRST
        )
        grad_new_ref[...] = grad_new
        grad_update = (grad_new * silu_slope(update)).astype(jnp.bfloat16)
        up_grad_ref[...] = dot32(gathered_ref[...], grad_update).astype(jnp.bfloat16)
        grad_gathered = dot32(up_ref[...], grad_update, LAST_LAST).astype(jnp.bfloat16)
        bil_grad_ref[...] = dot32(grad_gathered, moment_ref[...], LAST_LAST).astype(jnp.bfloat16)
        for part in range(edges // BLOCK):
            table[part * width : (part + 1) * width, :] = grad_gathered[
                :, part * BLOCK : (part + 1) * BLOCK
            ]

    place = step * tile + lax.broadcasted_iota(jnp.int32, (1, tile), 1)
    outgoing = jnp.where(place < count_ref[0, 0], out_ref[...], -1)
    picked = dot32(table[...], row_hot(BLOCK, outgoing & (BLOCK - 1)))
    high = outgoing // BLOCK
    grad = jnp.zeros((width, tile), jnp.float32)
    for part in range(edges // BLOCK):
        grad = jnp.where(
            (high == part) & (outgoing >= 0), picked[part * width : (part + 1) * width, :], grad
        )
    grad = grad.astype(jnp.bfloat16)
    for row in range(basis_ref.shape[0]):
        spread[row * width : (row + 1) * width, :] = grad * basis_ref[row : row + 1, :]
    feat_grad = dot32(bil_ref[...], spread[...], FIRST_FIRST)
    incoming = in_ref[...]
    hot_in = row_hot(BLOCK, incoming & (BLOCK - 1))
    high_in = incoming // BLOCK
    for part in range(groups):
        masked = jnp.where(high_in == part, feat_grad, 0.0).astype(jnp.bfloat16)
        total[part * width : (part + 1) * width, :] += dot32(masked, hot_in, LAST_LAST)

    @pl.when(step == pl.num_programs(0) - 1)
    def _():
        parts_ref[...] = total[...].astype(jnp.bfloat16)


def edge_kernel(
    parts_ref, projected_ref, emb_ref, down_ref, grad_new_ref, grad_in_ref, down_grad_ref
):
    total = parts_ref[0].astype(jnp.float32)
    for part in range(1, parts_ref.shape[0]):
        total = total + parts_ref[part].astype(jnp.float32)
    width = projected_ref.shape[0]
    grad_feat = jnp.concatenate(
        [total[at : at + width, :] for at in range(0, total.shape[0], width)], axis=1
    )
    grad_project = (grad_feat * silu_slope(projected_ref[...])).astype(jnp.bfloat16)
    grad_in_ref[...] = grad_new_ref[...] + dot32(grad_project, down_ref[...], FIRST_LAST)
    down_grad_ref[...] = dot32(grad_project, emb_ref[...]).astype(jnp.bfloat16)


def whole(shape):
    return pl.BlockSpec(shape, lambda step: (0,) * len(shape))


def params():
    return pltpu.CompilerParams(vmem_limit_bytes=VMEM_BYTES)


def body(
    edge_emb,
    atom_emb,
    edge_target,
    trip_in,
    trip_out,
    trip_count,
    trip_basis,
    grad_edge,
    grad_atom,
    w_down,
    w_bil,
    w_up,
    w_atom,
):
    members = lax.axis_size("graph")
    devices = members * lax.axis_size("dp")
    edge_rows = edge_emb[0]
    edge_dev, model = edge_rows.shape
    atom_dev = atom_emb.shape[1]
    trips = trip_in.shape[1]
    width = w_down.shape[1]
    basis_width = trip_basis.shape[1]
    tile = math.gcd(trips, TILE_LIMIT)
    rows_dev = edge_dev // BLOCK * width
    f32, b16 = jnp.float32, jnp.bfloat16
    shaped = jax.ShapeDtypeStruct

    projected, table = pl.pallas_call(
        feature_kernel,
        out_shape=(shaped((width, edge_dev), f32), shaped((rows_dev, BLOCK), b16)),
        compiler_params=params(),
        name="features",
    )(edge_rows, w_down)
    table_all = lax.all_gather(table, "graph", axis=0, tiled=True)

    along = lambda rows: pl.BlockSpec((rows, tile), lambda step: (0, step))
    smem = pl.BlockSpec(memory_space=pltpu.SMEM)
    atoms_all = atom_dev * members
    edge_new, atom_parts, gathered, moment = pl.pallas_call(
        forward_kernel,
        grid=(trips // tile,),
        in_specs=[
            smem,
            along(1),
            along(1),
            along(basis_width),
            whole(table_all.shape),
            whole(w_bil.shape),
            whole(w_up.shape),
            whole(edge_rows.shape),
            whole(edge_target.shape),
        ],
        out_specs=(
            whole(edge_rows.shape),
            whole((atoms_all, model)),
            whole((width, edge_dev)),
            whole((w_bil.shape[0], edge_dev)),
        ),
        out_shape=(
            shaped(edge_rows.shape, b16),
            shaped((atoms_all, model), b16),
            shaped((width, edge_dev), b16),
            shaped((w_bil.shape[0], edge_dev), b16),
        ),
        scratch_shapes=[
            pltpu.VMEM((w_bil.shape[0], edge_dev), f32),
            pltpu.VMEM((w_bil.shape[0], tile), b16),
        ],
        compiler_params=params(),
        name="forward_triplets",
    )(trip_count, trip_in, trip_out, trip_basis[0], table_all, w_bil, w_up, edge_rows, edge_target)

    atom_parts = lax.all_to_all(
        atom_parts.reshape(members, atom_dev, model), "graph", 0, 0, tiled=True
    )
    atom_new, grad_sum, watom_term = pl.pallas_call(
        atom_kernel,
        out_shape=(
            shaped((atom_dev, model), b16),
            shaped((atom_dev, model), b16),
            shaped((model, model), b16),
        ),
        compiler_params=params(),
        name="atoms",
    )(atom_parts, atom_emb[0], grad_atom[0], w_atom)
    grad_sum_all = lax.all_gather(grad_sum, "graph", axis=0, tiled=True)

    grad_new, wup_term, wbil_term, feat_parts = pl.pallas_call(
        backward_kernel,
        grid=(trips // tile,),
        in_specs=[
            smem,
            along(1),
            along(1),
            along(basis_width),
            whole(w_bil.shape),
            whole(w_up.shape),
            whole(gathered.shape),
            whole(moment.shape),
            whole(edge_rows.shape),
            whole(grad_sum_all.shape),
            whole(edge_target.shape),
        ],
        out_specs=(
            whole(edge_rows.shape),
            whole(w_up.shape),
            whole((width, w_bil.shape[0])),
            whole((members * rows_dev, BLOCK)),
        ),
        out_shape=(
            shaped(edge_rows.shape, f32),
            shaped(w_up.shape, b16),
            shaped((width, w_bil.shape[0]), b16),
            shaped((members * rows_dev, BLOCK), b16),
        ),
        scratch_shapes=[
            pltpu.VMEM((rows_dev, BLOCK), b16),
            pltpu.VMEM((w_bil.shape[0], tile), b16),
            pltpu.VMEM((members * rows_dev, BLOCK), f32),
        ],
        compiler_params=params(),
        name="backward_triplets",
    )(
        trip_count,
        trip_in,
        trip_out,
        trip_basis[0],
        jnp.transpose(w_bil.reshape(basis_width, width, width), (0, 2, 1)).reshape(w_bil.shape),
        w_up,
        gathered,
        moment,
        grad_edge[0],
        grad_sum_all,
        edge_target,
    )
    feat_parts = lax.all_to_all(
        feat_parts.reshape(members, rows_dev, BLOCK), "graph", 0, 0, tiled=True
    )
    grad_in, wdown_term = pl.pallas_call(
        edge_kernel,
        out_shape=(shaped(edge_rows.shape, f32), shaped((width, model), b16)),
        compiler_params=params(),
        name="edges",
    )(feat_parts, projected, edge_rows, w_down, grad_new)

    factor = 1.0 / math.sqrt(lax.axis_size("dp") * members * edge_dev)
    terms = (wdown_term, wbil_term, wup_term, watom_term)
    lanes = 128
    packed = jnp.concatenate([term.reshape(-1, lanes) for term in terms], axis=0)
    packed = lax.all_to_all(
        packed.reshape(devices, -1, lanes), ("dp", "graph"), 0, 0, tiled=True
    )
    share = (jnp.sum(packed.astype(f32), axis=0) * factor).astype(b16)
    totals = lax.all_to_all(
        jnp.broadcast_to(share[None], packed.shape), ("dp", "graph"), 0, 0, tiled=True
    ).reshape(-1, lanes)
    sums, at = [], 0
    for term in terms:
        rows = term.size // lanes
        sums.append(totals[at : at + rows].reshape(term.shape).astype(f32))
        at += rows
    return (
        edge_new[None],
        atom_new[None],
        grad_in[None],
        sums[0].T,
        sums[1].T,
        sums[2],
        sums[3],
    )


def solution(mesh):
    return jax.shard_map(
        body,
        mesh=mesh,
        in_specs=(
            P("dp", "graph", None),
            P("dp", "graph", None),
            P("dp", "graph"),
            P("dp", "graph"),
            P("dp", "graph"),
            P("dp", "graph"),
            P("dp", None, "graph"),
            P("dp", "graph", None),
            P("dp", "graph", None),
            P(),
            P(),
            P(),
            P(),
        ),
        out_specs=(
            P("dp", "graph", None),
            P("dp", "graph", None),
            P("dp", "graph", None),
            P(),
            P(),
            P(),
            P(),
        ),
        check_vma=False,
    )
```

```python
import functools
import math

import jax
import jax.numpy as jnp
from jax import lax
from jax.experimental import pallas as pl
from jax.experimental.pallas import tpu as pltpu
from jax.sharding import PartitionSpec as P

ATOM_SCALE = 0.25
BLOCK = 256
CAP = 128
TILE_LIMIT = 1024
INDEX_TILE = 2048
VMEM_BYTES = 48 * 1024 * 1024

FIRST_FIRST = (((0,), (0,)), ((), ()))
LAST_LAST = (((1,), (1,)), ((), ()))


def dot32(left, right, dims=(((1,), (0,)), ((), ()))):
    return lax.dot_general(left, right, dims, preferred_element_type=jnp.float32)


def silu(value):
    return value / (1.0 + jnp.exp(-value))


def silu_slope(value):
    logistic = 1.0 / (1.0 + jnp.exp(-value))
    return logistic * (1.0 + value * (1.0 - logistic))


def row_hot(rows, index):
    iota = lax.broadcasted_iota(jnp.int32, (rows, index.shape[1]), 0)
    return (iota == index).astype(jnp.float32).astype(jnp.bfloat16)


def feature_kernel(emb_ref, down_ref, bil_ref, projected_ref, feat_ref, back_ref):
    projected = dot32(down_ref[...], emb_ref[...], LAST_LAST)
    projected_ref[...] = projected
    feat_ref[...] = silu(projected).astype(jnp.bfloat16)
    width = down_ref.shape[0]
    turned = bil_ref[...].astype(jnp.float32).T
    back_ref[...] = jnp.concatenate(
        [turned[at : at + width] for at in range(0, turned.shape[0], width)], axis=1
    ).astype(jnp.bfloat16)


def index_kernel(members, in_ref, slot_ref, rank_ref, hots, counts):
    trips = in_ref.shape[1]
    rows = rank_ref.shape[0]
    tile = math.gcd(trips, INDEX_TILE)
    spans = [slice(at, at + tile) for at in range(0, trips, tile)]
    counts[...] = jnp.zeros_like(counts)
    for span in spans:
        incoming = in_ref[:, span]
        hot = row_hot(CAP, incoming & (CAP - 1))
        hots[:, span] = hot
        counts[...] += dot32(row_hot(rows, incoming // CAP), hot, LAST_LAST)
    named = (counts[...] > 0.0).astype(jnp.float32)
    per = rows // members
    ahead = (
        lax.broadcasted_iota(jnp.int32, (CAP, CAP), 0)
        < lax.broadcasted_iota(jnp.int32, (CAP, CAP), 1)
    ).astype(jnp.bfloat16)
    row = lax.broadcasted_iota(jnp.int32, (rows, rows), 0)
    other = lax.broadcasted_iota(jnp.int32, (rows, rows), 1)
    above = ((other < row) & (other // per == row // per)).astype(jnp.bfloat16)
    sums = dot32(above, named.astype(jnp.bfloat16))
    before = jnp.sum(sums, axis=1, keepdims=True)
    rank = dot32(named.astype(jnp.bfloat16), ahead) + before
    rank = jnp.where(named > 0.0, rank, -1.0)
    rank_ref[...] = rank
    lookup = rank.astype(jnp.bfloat16)
    for span in spans:
        incoming = in_ref[:, span]
        place = incoming // CAP
        found = dot32(lookup, hots[:, span])
        iota = lax.broadcasted_iota(jnp.int32, found.shape, 0)
        found = jnp.sum(jnp.where(iota == place, found, 0.0), axis=0, keepdims=True)
        slot_ref[:, span] = (place // per) * CAP + found.astype(jnp.int32)


def rank_row(rank_ref, source, per):
    return jnp.concatenate(
        [rank_ref[source * per + part : source * per + part + 1, :] for part in range(per)], axis=1
    )


def rank_hot(row):
    iota = lax.broadcasted_iota(jnp.int32, (CAP, row.shape[1]), 0).astype(jnp.float32)
    return (iota == row).astype(jnp.float32).astype(jnp.bfloat16)


def forward_kernel(
    count_ref,
    slot_ref,
    out_ref,
    basis_ref,
    feat_ref,
    rank_ref,
    bil_ref,
    up_ref,
    emb_ref,
    target_ref,
    new_ref,
    atoms_ref,
    gathered_ref,
    moment_ref,
    table,
    total,
    spread,
):
    step = pl.program_id(0)
    tile = slot_ref.shape[1]
    width = bil_ref.shape[0]
    edges = emb_ref.shape[0]
    members = feat_ref.shape[0] // width
    groups = table.shape[0] // width

    @pl.when(step == 0)
    def _():
        total[...] = jnp.zeros_like(total)
        for source in range(members):
            row = rank_row(rank_ref, source, edges // CAP)
            chosen = dot32(
                feat_ref[source * width : (source + 1) * width, :], rank_hot(row), LAST_LAST
            )
            group, lane = divmod(source * CAP, BLOCK)
            table[group * width : (group + 1) * width, lane : lane + CAP] = chosen.astype(
                jnp.bfloat16
            )

    slot = slot_ref[...]
    high = slot // BLOCK
    hot = row_hot(BLOCK, slot & (BLOCK - 1))
    feat = jnp.zeros((width, tile), jnp.float32)
    per = BLOCK // width
    for chunk in range(groups // per):
        picked = dot32(table[chunk * BLOCK : (chunk + 1) * BLOCK, :], hot)
        for part in range(per):
            feat = jnp.where(
                high == chunk * per + part, picked[part * width : (part + 1) * width, :], feat
            )
    feat = feat.astype(jnp.bfloat16)
    basis = basis_ref[...]
    for row in range(basis.shape[0]):
        spread[row * width : (row + 1) * width, :] = feat * basis[row : row + 1, :]
    place = step * tile + lax.broadcasted_iota(jnp.int32, (1, tile), 1)
    outgoing = jnp.where(place < count_ref[0, 0], out_ref[...], -1)
    total[...] += dot32(spread[...], row_hot(edges, outgoing), LAST_LAST)

    @pl.when(step == pl.num_programs(0) - 1)
    def _():
        summed = total[...]
        head = summed.astype(jnp.bfloat16)
        rest = (summed - head.astype(jnp.float32)).astype(jnp.bfloat16)
        moment_ref[...] = head
        gathered = (dot32(bil_ref[...], head) + dot32(bil_ref[...], rest)).astype(jnp.bfloat16)
        gathered_ref[...] = gathered
        update = dot32(gathered, up_ref[...], FIRST_FIRST)
        fresh = (emb_ref[...].astype(jnp.float32) + silu(update)).astype(jnp.bfloat16)
        new_ref[...] = fresh
        atoms_ref[...] = dot32(row_hot(atoms_ref.shape[0], target_ref[...]), fresh).astype(
            jnp.bfloat16
        )


def atom_kernel(parts_ref, emb_ref, grad_ref, weight_ref, new_ref, grad_sum_ref, pair_ref):
    total = parts_ref[0].astype(jnp.float32)
    for part in range(1, parts_ref.shape[0]):
        total = total + parts_ref[part].astype(jnp.float32)
    total = total.astype(jnp.bfloat16)
    pre = ATOM_SCALE * dot32(total, weight_ref[...])
    new_ref[...] = (emb_ref[...].astype(jnp.float32) + silu(pre)).astype(jnp.bfloat16)
    grad_pre = (grad_ref[...].astype(jnp.float32) * silu_slope(pre)).astype(jnp.bfloat16)
    grad_sum_ref[...] = (ATOM_SCALE * dot32(grad_pre, weight_ref[...], LAST_LAST)).astype(
        jnp.bfloat16
    )
    pair_ref[0] = total
    pair_ref[1] = grad_pre


def atom_weight_kernel(factor, pairs_ref, out_ref):
    devices, _, rows, model = pairs_ref.shape
    sums = pairs_ref[:, 0].reshape(devices * rows, model)
    grads = pairs_ref[:, 1].reshape(devices * rows, model)
    out_ref[...] = dot32(sums, grads, FIRST_FIRST) * (ATOM_SCALE * factor)


def backward_kernel(
    count_ref,
    slot_ref,
    out_ref,
    basis_ref,
    rank_ref,
    back_ref,
    up_ref,
    gathered_ref,
    moment_ref,
    grad_edge_ref,
    grad_sum_ref,
    target_ref,
    grad_new_ref,
    up_grad_ref,
    bil_grad_ref,
    parts_ref,
    table,
    spread,
    masked,
    total,
):
    step = pl.program_id(0)
    tile = slot_ref.shape[1]
    width = back_ref.shape[0]
    edges = grad_edge_ref.shape[0]
    groups = total.shape[0] // width

    @pl.when(step == 0)
    def _():
        total[...] = jnp.zeros_like(total)
        update = dot32(gathered_ref[...], up_ref[...], FIRST_FIRST)
        hot = row_hot(grad_sum_ref.shape[0], target_ref[...])
        grad_new = grad_edge_ref[...].astype(jnp.float32) + dot32(
            hot, grad_sum_ref[...], FIRST_FIRST
        )
        grad_new_ref[...] = grad_new
        grad_update = (grad_new * silu_slope(update)).astype(jnp.bfloat16)
        up_grad_ref[...] = dot32(gathered_ref[...], grad_update).astype(jnp.bfloat16)
        grad_gathered = dot32(up_ref[...], grad_update, LAST_LAST).astype(jnp.bfloat16)
        bil_grad_ref[...] = dot32(grad_gathered, moment_ref[...], LAST_LAST).astype(jnp.bfloat16)
        for part in range(edges // BLOCK):
            table[part * width : (part + 1) * width, :] = grad_gathered[
                :, part * BLOCK : (part + 1) * BLOCK
            ]

    place = step * tile + lax.broadcasted_iota(jnp.int32, (1, tile), 1)
    outgoing = jnp.where(place < count_ref[0, 0], out_ref[...], -1)
    picked = dot32(table[...], row_hot(BLOCK, outgoing & (BLOCK - 1)))
    high = jnp.where(outgoing >= 0, outgoing // BLOCK, -1)
    grad = jnp.zeros((width, tile), jnp.float32)
    for part in range(edges // BLOCK):
        grad = jnp.where(high == part, picked[part * width : (part + 1) * width, :], grad)
    grad = grad.astype(jnp.bfloat16)
    basis = basis_ref[...]
    for row in range(basis.shape[0]):
        spread[row * width : (row + 1) * width, :] = grad * basis[row : row + 1, :]
    feat_grad = dot32(back_ref[...], spread[...])
    slot = slot_ref[...]
    high_in = slot // BLOCK
    for part in range(groups):
        masked[part * width : (part + 1) * width, :] = jnp.where(
            high_in == part, feat_grad, 0.0
        ).astype(jnp.bfloat16)
    total[...] += dot32(masked[...], row_hot(BLOCK, slot & (BLOCK - 1)), LAST_LAST)

    @pl.when(step == pl.num_programs(0) - 1)
    def _():
        members = parts_ref.shape[0]
        per = rank_ref.shape[0] // members
        for source in range(members):
            group, lane = divmod(source * CAP, BLOCK)
            piece = total[group * width : (group + 1) * width, lane : lane + CAP]
            ranks = rank_ref[source * per : (source + 1) * per, :]
            spare = jnp.zeros((parts_ref.shape[1] - width - per, CAP), jnp.float32)
            parts_ref[source] = jnp.concatenate([piece, ranks, spare], axis=0).astype(jnp.bfloat16)


def edge_kernel(
    parts_ref,
    projected_ref,
    emb_ref,
    down_ref,
    grad_new_ref,
    bil_grad_ref,
    up_grad_ref,
    grad_in_ref,
    packed_ref,
):
    members = parts_ref.shape[0]
    width, edges = projected_ref.shape
    per = edges // CAP
    grad_feat = jnp.zeros((width, edges), jnp.float32)
    for source in range(members):
        part = parts_ref[source].astype(jnp.float32)
        row = jnp.concatenate([part[width + at : width + at + 1] for at in range(per)], axis=1)
        grad_feat = grad_feat + dot32(part[:width].astype(jnp.bfloat16), rank_hot(row))
    grad_project = (grad_feat * silu_slope(projected_ref[...])).astype(jnp.bfloat16)
    grad_in_ref[...] = grad_new_ref[...] + dot32(grad_project, down_ref[...], FIRST_FIRST)
    down_grad = dot32(grad_project, emb_ref[...])
    devices, rows, lanes = packed_ref.shape
    at = 0
    for term in (down_grad, bil_grad_ref[...].astype(jnp.float32), up_grad_ref[...].astype(jnp.float32)):
        for column in range(0, term.shape[1], lanes):
            for first in range(0, width, rows):
                packed_ref[at] = term[first : first + rows, column : column + lanes].astype(
                    jnp.bfloat16
                )
                at += 1


def share_kernel(factor, parts_ref, out_ref):
    total = parts_ref[0].astype(jnp.float32)
    for part in range(1, parts_ref.shape[0]):
        total = total + parts_ref[part].astype(jnp.float32)
    total = (total * factor).astype(jnp.bfloat16)
    for part in range(out_ref.shape[0]):
        out_ref[part] = total


def unpack_kernel(parts_ref, down_ref, bil_ref, up_ref):
    devices, rows, lanes = parts_ref.shape
    at = 0
    for out in (down_ref, bil_ref, up_ref):
        for column in range(0, out.shape[1], lanes):
            for first in range(0, out.shape[0], rows):
                out[first : first + rows, column : column + lanes] = parts_ref[at].astype(
                    jnp.float32
                )
                at += 1


def whole(shape):
    return pl.BlockSpec(shape, lambda step: (0,) * len(shape))


def params():
    return pltpu.CompilerParams(vmem_limit_bytes=VMEM_BYTES)


def body(
    edge_emb,
    atom_emb,
    edge_target,
    trip_in,
    trip_out,
    trip_count,
    trip_basis,
    grad_edge,
    grad_atom,
    w_down,
    w_bil,
    w_up,
    w_atom,
):
    members = lax.axis_size("graph")
    devices = members * lax.axis_size("dp")
    edge_rows = edge_emb[0]
    edge_dev, model = edge_rows.shape
    atom_dev = atom_emb.shape[1]
    trips = trip_in.shape[1]
    width = w_down.shape[1]
    basis_width = trip_basis.shape[1]
    tile = math.gcd(trips, TILE_LIMIT)
    f32, b16 = jnp.float32, jnp.bfloat16
    shaped = jax.ShapeDtypeStruct

    down_rows = w_down.T
    bil_rows = w_bil.T
    projected, feat, back = pl.pallas_call(
        feature_kernel,
        out_shape=(
            shaped((width, edge_dev), f32),
            shaped((width, edge_dev), b16),
            shaped((width, w_bil.shape[0]), b16),
        ),
        compiler_params=params(),
        name="features",
    )(edge_rows, down_rows, bil_rows)
    feat_all = lax.all_gather(feat, "graph", axis=0, tiled=True)
    rank_rows = members * edge_dev // CAP
    slot, rank = pl.pallas_call(
        functools.partial(index_kernel, members),
        out_shape=(shaped(trip_in.shape, jnp.int32), shaped((rank_rows, CAP), f32)),
        scratch_shapes=[pltpu.VMEM((CAP, trips), b16), pltpu.VMEM((rank_rows, CAP), f32)],
        compiler_params=params(),
        name="slots",
    )(trip_in)

    along = lambda rows: pl.BlockSpec((rows, tile), lambda step: (0, step))
    smem = pl.BlockSpec(memory_space=pltpu.SMEM)
    atoms_all = atom_dev * members
    named_rows = members * CAP // BLOCK * width
    edge_new, atom_parts, gathered, moment = pl.pallas_call(
        forward_kernel,
        grid=(trips // tile,),
        in_specs=[
            smem,
            along(1),
            along(1),
            along(basis_width),
            whole(feat_all.shape),
            whole(rank.shape),
            whole(bil_rows.shape),
            whole(w_up.shape),
            whole(edge_rows.shape),
            whole(edge_target.shape),
        ],
        out_specs=(
            whole(edge_rows.shape),
            whole((atoms_all, model)),
            whole((width, edge_dev)),
            whole((w_bil.shape[0], edge_dev)),
        ),
        out_shape=(
            shaped(edge_rows.shape, b16),
            shaped((atoms_all, model), b16),
            shaped((width, edge_dev), b16),
            shaped((w_bil.shape[0], edge_dev), b16),
        ),
        scratch_shapes=[
            pltpu.VMEM((named_rows, BLOCK), b16),
            pltpu.VMEM((w_bil.shape[0], edge_dev), f32),
            pltpu.VMEM((w_bil.shape[0], tile), b16),
        ],
        compiler_params=params(),
        name="forward_triplets",
    )(
        trip_count,
        slot,
        trip_out,
        trip_basis[0],
        feat_all,
        rank,
        bil_rows,
        w_up,
        edge_rows,
        edge_target,
    )

    atom_parts = lax.all_to_all(
        atom_parts.reshape(members, atom_dev, model), "graph", 0, 0, tiled=True
    )
    atom_new, grad_sum, pair = pl.pallas_call(
        atom_kernel,
        out_shape=(
            shaped((atom_dev, model), b16),
            shaped((atom_dev, model), b16),
            shaped((2, atom_dev, model), b16),
        ),
        compiler_params=params(),
        name="atoms",
    )(atom_parts, atom_emb[0], grad_atom[0], w_atom)
    grad_sum_all = lax.all_gather(grad_sum, "graph", axis=0, tiled=True)
    pairs = lax.all_gather(pair, ("dp", "graph"), axis=0)

    piece_rows = width + -(-(edge_dev // CAP) // 16) * 16
    grad_new, wup_term, wbil_term, feat_parts = pl.pallas_call(
        backward_kernel,
        grid=(trips // tile,),
        in_specs=[
            smem,
            along(1),
            along(1),
            along(basis_width),
            whole(rank.shape),
            whole(back.shape),
            whole(w_up.shape),
            whole(gathered.shape),
            whole(moment.shape),
            whole(edge_rows.shape),
            whole(grad_sum_all.shape),
            whole(edge_target.shape),
        ],
        out_specs=(
            whole(edge_rows.shape),
            whole(w_up.shape),
            whole((width, w_bil.shape[0])),
            whole((members, piece_rows, CAP)),
        ),
        out_shape=(
            shaped(edge_rows.shape, f32),
            shaped(w_up.shape, b16),
            shaped((width, w_bil.shape[0]), b16),
            shaped((members, piece_rows, CAP), b16),
        ),
        scratch_shapes=[
            pltpu.VMEM((edge_dev // BLOCK * width, BLOCK), b16),
            pltpu.VMEM((w_bil.shape[0], tile), b16),
            pltpu.VMEM((named_rows, tile), b16),
            pltpu.VMEM((named_rows, BLOCK), f32),
        ],
        compiler_params=params(),
        name="backward_triplets",
    )(
        trip_count,
        slot,
        trip_out,
        trip_basis[0],
        rank,
        back,
        w_up,
        gathered,
        moment,
        grad_edge[0],
        grad_sum_all,
        edge_target,
    )
    feat_parts = lax.all_to_all(feat_parts, "graph", 0, 0, tiled=True)
    lanes = CAP
    weights = width * (2 * model + w_bil.shape[0])
    packed_shape = (devices, weights // devices // lanes, lanes)
    grad_in, packed = pl.pallas_call(
        edge_kernel,
        out_shape=(shaped(edge_rows.shape, f32), shaped(packed_shape, b16)),
        compiler_params=params(),
        name="edges",
    )(feat_parts, projected, edge_rows, down_rows, grad_new, wbil_term, wup_term)

    factor = 1.0 / math.sqrt(lax.axis_size("dp") * members * edge_dev)
    packed = lax.all_to_all(packed, ("dp", "graph"), 0, 0, tiled=True)
    share = pl.pallas_call(
        functools.partial(share_kernel, factor),
        out_shape=shaped(packed_shape, b16),
        compiler_params=params(),
        name="share",
    )(packed)
    totals = lax.all_to_all(share, ("dp", "graph"), 0, 0, tiled=True)
    grad_watom = pl.pallas_call(
        functools.partial(atom_weight_kernel, factor),
        out_shape=shaped((model, model), f32),
        compiler_params=params(),
        name="atom_weights",
    )(pairs)
    grad_wdown, grad_wbil, grad_wup = pl.pallas_call(
        unpack_kernel,
        out_shape=(
            shaped((width, model), f32),
            shaped((width, w_bil.shape[0]), f32),
            shaped(w_up.shape, f32),
        ),
        compiler_params=params(),
        name="unpack",
    )(totals)
    return (
        edge_new[None],
        atom_new[None],
        grad_in[None],
        grad_wdown.T,
        grad_wbil.T,
        grad_wup,
        grad_watom,
    )


def solution(mesh):
    return jax.shard_map(
        body,
        mesh=mesh,
        in_specs=(
            P("dp", "graph", None),
            P("dp", "graph", None),
            P("dp", "graph"),
            P("dp", "graph"),
            P("dp", "graph"),
            P("dp", "graph"),
            P("dp", None, "graph"),
            P("dp", "graph", None),
            P("dp", "graph", None),
            P(),
            P(),
            P(),
            P(),
        ),
        out_specs=(
            P("dp", "graph", None),
            P("dp", "graph", None),
            P("dp", "graph", None),
            P(),
            P(),
            P(),
            P(),
        ),
        check_vma=False,
    )
```

```python
import functools
import math

import jax
import jax.numpy as jnp
from jax import lax
from jax.experimental import pallas as pl
from jax.experimental.pallas import tpu as pltpu
from jax.sharding import PartitionSpec as P

ATOM_SCALE = 0.25
BLOCK = 256
CAP = 128
TILE_LIMIT = 2048
INDEX_TILE = 2048
VMEM_BYTES = 24 * 1024 * 1024
VMEM_MOST = 60 * 1024 * 1024

FIRST_FIRST = (((0,), (0,)), ((), ()))
LAST_LAST = (((1,), (1,)), ((), ()))


def dot32(left, right, dims=(((1,), (0,)), ((), ()))):
    return lax.dot_general(left, right, dims, preferred_element_type=jnp.float32)


def silu(value):
    return value / (1.0 + jnp.exp(-value))


def silu_slope(value):
    logistic = 1.0 / (1.0 + jnp.exp(-value))
    return logistic * (1.0 + value * (1.0 - logistic))


def row_hot(rows, index):
    iota = lax.broadcasted_iota(jnp.int32, (rows, index.shape[1]), 0)
    return (iota == index).astype(jnp.float32).astype(jnp.bfloat16)


def start_copies(pairs, sems):
    copies = [
        pltpu.make_async_copy(source, target, sems.at[place])
        for place, (source, target) in enumerate(pairs)
    ]
    for copy in copies:
        copy.start()
    return copies


def feature_kernel(emb_hbm, down_hbm, projected_ref, feat_ref, emb_ref, down_ref, sems):
    for copy in start_copies(((emb_hbm, emb_ref), (down_hbm, down_ref)), sems):
        copy.wait()
    projected = dot32(down_ref[...], emb_ref[...], LAST_LAST)
    projected_ref[...] = projected
    feat_ref[...] = silu(projected).astype(jnp.bfloat16)


def index_kernel(members, in_ref, *refs):
    slot_ref, rank_ref, hots, counts = refs[-4:]
    trips = in_ref.shape[1]
    rows = rank_ref.shape[0]
    turn = lax.axis_index("graph") * (rows // members * CAP)
    tile = math.gcd(trips, INDEX_TILE)
    spans = [slice(at, at + tile) for at in range(0, trips, tile)]
    counts[...] = jnp.zeros_like(counts)
    for span in spans:
        incoming = in_ref[:, span] ^ turn
        hot = row_hot(CAP, incoming & (CAP - 1))
        hots[:, span] = hot
        counts[...] += dot32(row_hot(rows, incoming // CAP), hot, LAST_LAST)
    named = (counts[...] > 0.0).astype(jnp.float32)
    per = rows // members
    ahead = (
        lax.broadcasted_iota(jnp.int32, (CAP, CAP), 0)
        < lax.broadcasted_iota(jnp.int32, (CAP, CAP), 1)
    ).astype(jnp.bfloat16)
    row = lax.broadcasted_iota(jnp.int32, (rows, rows), 0)
    other = lax.broadcasted_iota(jnp.int32, (rows, rows), 1)
    above = ((other < row) & (other // per == row // per)).astype(jnp.bfloat16)
    sums = dot32(above, named.astype(jnp.bfloat16))
    before = jnp.sum(sums, axis=1, keepdims=True)
    rank = dot32(named.astype(jnp.bfloat16), ahead) + before
    rank = jnp.where(named > 0.0, rank, -1.0)
    rank_ref[...] = rank
    lookup = rank.astype(jnp.bfloat16)
    for span in spans:
        incoming = in_ref[:, span] ^ turn
        place = incoming // CAP
        found = dot32(lookup, hots[:, span])
        iota = lax.broadcasted_iota(jnp.int32, found.shape, 0)
        found = jnp.sum(jnp.where(iota == place, found, 0.0), axis=0, keepdims=True)
        slot_ref[:, span] = (place // per) * CAP + found.astype(jnp.int32)


def rank_row(rank_ref, source, per):
    return jnp.concatenate(
        [rank_ref[source * per + part : source * per + part + 1, :] for part in range(per)], axis=1
    )


def rank_hot(row):
    iota = lax.broadcasted_iota(jnp.int32, (CAP, row.shape[1]), 0).astype(jnp.float32)
    return (iota == row).astype(jnp.float32).astype(jnp.bfloat16)


def forward_kernel(
    members,
    count_ref,
    slot_ref,
    rank_ref,
    out_ref,
    basis_ref,
    bil_ref,
    up_ref,
    emb_ref,
    target_ref,
    *refs,
):
    feat_refs, refs = refs[:members], refs[members:]
    new_ref, near_ref, far_ref, gathered_ref, moment_ref, back_ref, *refs = refs
    table, total, spread = refs
    trips = slot_ref.shape[1]
    tile = spread.shape[1]
    width = bil_ref.shape[0]
    edges = emb_ref.shape[0]
    groups = table.shape[0] // width
    per = BLOCK // width
    count = count_ref[0, 0]
    total[...] = jnp.zeros_like(total)
    for source in range(members):
        row = rank_row(rank_ref, source, edges // CAP)
        chosen = dot32(feat_refs[source][...], rank_hot(row), LAST_LAST)
        group, lane = divmod(source * CAP, BLOCK)
        table[group * width : (group + 1) * width, lane : lane + CAP] = chosen.astype(jnp.bfloat16)

    def one_tile(step, carry):
        span = pl.ds(pl.multiple_of(step * tile, tile), tile)
        slot = slot_ref[:, span]
        high = slot // BLOCK
        hot = row_hot(BLOCK, slot & (BLOCK - 1))
        feat = jnp.zeros((width, tile), jnp.float32)
        for chunk in range(groups // per):
            picked = dot32(table[chunk * BLOCK : (chunk + 1) * BLOCK, :], hot)
            for part in range(per):
                feat = jnp.where(
                    high == chunk * per + part, picked[part * width : (part + 1) * width, :], feat
                )
        feat = feat.astype(jnp.bfloat16)
        basis = basis_ref[:, span]
        for row in range(basis.shape[0]):
            spread[row * width : (row + 1) * width, :] = feat * basis[row : row + 1, :]
        place = step * tile + lax.broadcasted_iota(jnp.int32, (1, tile), 1)
        outgoing = jnp.where(place < count, out_ref[:, span], -1)
        total[...] += dot32(spread[...], row_hot(edges, outgoing), LAST_LAST)
        return carry

    lax.fori_loop(0, trips // tile, one_tile, 0)
    turned = bil_ref[...].astype(jnp.float32).T
    back_ref[...] = jnp.concatenate(
        [turned[at : at + width] for at in range(0, turned.shape[0], width)], axis=1
    ).astype(jnp.bfloat16)
    summed = total[...]
    head = summed.astype(jnp.bfloat16)
    rest = (summed - head.astype(jnp.float32)).astype(jnp.bfloat16)
    moment_ref[...] = head
    gathered = (dot32(bil_ref[...], head) + dot32(bil_ref[...], rest)).astype(jnp.bfloat16)
    gathered_ref[...] = gathered
    update = dot32(gathered, up_ref[...], FIRST_FIRST)
    fresh = (emb_ref[...].astype(jnp.float32) + silu(update)).astype(jnp.bfloat16)
    new_ref[...] = fresh
    held = near_ref.shape[1]
    turn = lax.axis_index("graph") * held
    sums = dot32(row_hot(members * held, target_ref[...] ^ turn), fresh)
    for pair in range(members // 2):
        near_ref[pair] = sums[2 * pair * held : (2 * pair + 1) * held].astype(jnp.bfloat16)
        far_ref[pair] = sums[(2 * pair + 1) * held : (2 * pair + 2) * held].astype(jnp.bfloat16)


def chip_kernel(near_ref, far_ref, *out_refs):
    for pair, out_ref in enumerate(out_refs):
        out_ref[...] = (
            near_ref[pair].astype(jnp.float32) + far_ref[pair].astype(jnp.float32)
        ).astype(jnp.bfloat16)


def atom_kernel(emb_ref, grad_ref, weight_ref, *refs):
    part_refs, (new_ref, pair_ref) = refs[:-2], refs[-2:]
    total = part_refs[0][...].astype(jnp.float32)
    for part_ref in part_refs[1:]:
        total = total + part_ref[...].astype(jnp.float32)
    total = total.astype(jnp.bfloat16)
    pre = ATOM_SCALE * dot32(total, weight_ref[...])
    new_ref[...] = (emb_ref[...].astype(jnp.float32) + silu(pre)).astype(jnp.bfloat16)
    grad_pre = (grad_ref[...].astype(jnp.float32) * silu_slope(pre)).astype(jnp.bfloat16)
    pair_ref[0] = total
    pair_ref[1] = grad_pre


def backward_kernel(
    members,
    count_ref,
    slot_ref,
    out_ref,
    basis_ref,
    rank_ref,
    back_ref,
    up_ref,
    gathered_ref,
    moment_ref,
    grad_edge_ref,
    target_ref,
    atom_weight_ref,
    *refs,
):
    pair_refs, refs = refs[:members], refs[members:]
    grad_new_ref, up_grad_ref, bil_grad_ref, slab_ref, parts_ref, *refs = refs
    table, spread, masked, total, sums, grads, atom_grad = refs
    trips = slot_ref.shape[1]
    tile = spread.shape[1]
    width = back_ref.shape[0]
    edges = grad_edge_ref.shape[0]
    groups = total.shape[0] // width
    count = count_ref[0, 0]
    me = lax.axis_index("graph")
    held, model = pair_refs[0].shape[1:]
    for source, pair_ref in enumerate(pair_refs):
        sums[source * held : (source + 1) * held, :] = pair_ref[0]
        grads[source * held : (source + 1) * held, :] = pair_ref[1]
    grad_sum = (ATOM_SCALE * dot32(grads[...], atom_weight_ref[...], LAST_LAST)).astype(
        jnp.bfloat16
    )
    atom_grad[...] = ATOM_SCALE * dot32(sums[...], grads[...], FIRST_FIRST)
    share = model // members
    mine = atom_grad[pl.ds(pl.multiple_of(me * share, share), share), :]
    for column in range(0, model, CAP):
        slab_ref[column // CAP] = mine[:, column : column + CAP].astype(jnp.bfloat16)
    total[...] = jnp.zeros_like(total)
    update = dot32(gathered_ref[...], up_ref[...], FIRST_FIRST)
    hot = row_hot(members * held, target_ref[...] ^ (me * held))
    grad_new = grad_edge_ref[...].astype(jnp.float32) + dot32(hot, grad_sum, FIRST_FIRST)
    grad_new_ref[...] = grad_new
    grad_update = (grad_new * silu_slope(update)).astype(jnp.bfloat16)
    up_grad_ref[...] = dot32(gathered_ref[...], grad_update).astype(jnp.bfloat16)
    grad_gathered = dot32(up_ref[...], grad_update, LAST_LAST).astype(jnp.bfloat16)
    bil_grad_ref[...] = dot32(grad_gathered, moment_ref[...], LAST_LAST).astype(jnp.bfloat16)
    for part in range(edges // BLOCK):
        table[part * width : (part + 1) * width, :] = grad_gathered[
            :, part * BLOCK : (part + 1) * BLOCK
        ]

    def one_tile(step, carry):
        span = pl.ds(pl.multiple_of(step * tile, tile), tile)
        place = step * tile + lax.broadcasted_iota(jnp.int32, (1, tile), 1)
        outgoing = jnp.where(place < count, out_ref[:, span], -1)
        picked = dot32(table[...], row_hot(BLOCK, outgoing & (BLOCK - 1)))
        high = jnp.where(outgoing >= 0, outgoing // BLOCK, -1)
        grad = jnp.zeros((width, tile), jnp.float32)
        for part in range(edges // BLOCK):
            grad = jnp.where(high == part, picked[part * width : (part + 1) * width, :], grad)
        grad = grad.astype(jnp.bfloat16)
        basis = basis_ref[:, span]
        for row in range(basis.shape[0]):
            spread[row * width : (row + 1) * width, :] = grad * basis[row : row + 1, :]
        feat_grad = dot32(back_ref[...], spread[...])
        slot = slot_ref[:, span]
        high_in = slot // BLOCK
        for part in range(groups):
            masked[part * width : (part + 1) * width, :] = jnp.where(
                high_in == part, feat_grad, 0.0
            ).astype(jnp.bfloat16)
        total[...] += dot32(masked[...], row_hot(BLOCK, slot & (BLOCK - 1)), LAST_LAST)
        return carry

    lax.fori_loop(0, trips // tile, one_tile, 0)
    per = rank_ref.shape[0] // members
    for source in range(members):
        group, lane = divmod(source * CAP, BLOCK)
        piece = total[group * width : (group + 1) * width, lane : lane + CAP]
        ranks = rank_ref[source * per : (source + 1) * per, :]
        spare = jnp.zeros((parts_ref.shape[1] - width - per, CAP), jnp.float32)
        parts_ref[me ^ source] = jnp.concatenate([piece, ranks, spare], axis=0).astype(jnp.bfloat16)


def edge_kernel(
    parts_ref,
    projected_ref,
    emb_ref,
    down_ref,
    grad_new_ref,
    bil_grad_ref,
    up_grad_ref,
    grad_in_ref,
    near_ref,
    far_ref,
    flat,
):
    members = parts_ref.shape[0]
    width, edges = projected_ref.shape
    per = edges // CAP
    grad_feat = jnp.zeros((width, edges), jnp.float32)
    for source in range(members):
        part = parts_ref[source].astype(jnp.float32)
        row = jnp.concatenate([part[width + at : width + at + 1] for at in range(per)], axis=1)
        grad_feat = grad_feat + dot32(part[:width].astype(jnp.bfloat16), rank_hot(row))
    grad_project = (grad_feat * silu_slope(projected_ref[...])).astype(jnp.bfloat16)
    grad_in_ref[...] = grad_new_ref[...] + dot32(grad_project, down_ref[...], FIRST_FIRST)
    down_grad = dot32(grad_project, emb_ref[...]).astype(jnp.bfloat16)
    at = 0
    for term in (down_grad, bil_grad_ref[...], up_grad_ref[...]):
        for column in range(0, term.shape[1], CAP):
            flat[at : at + width, :] = term[:, column : column + CAP]
            at += width
    me = lax.axis_index("graph")
    rows = near_ref.shape[1]
    for pair in range(members // 2):
        near_ref[pair] = flat[pl.ds(pl.multiple_of((me ^ (2 * pair)) * rows, rows), rows), :]
        far_ref[pair] = flat[pl.ds(pl.multiple_of((me ^ (2 * pair + 1)) * rows, rows), rows), :]


def share_kernel(slab_ref, *refs):
    part_refs, out_ref = refs[:-1], refs[-1]
    total = part_refs[0][...].astype(jnp.float32)
    for part_ref in part_refs[1:]:
        total = total + part_ref[...].astype(jnp.float32)
    rows = total.shape[0]
    out_ref[:rows, :] = total.astype(jnp.bfloat16)
    slab = slab_ref[...]
    out_ref[rows:, :] = slab.reshape(slab.shape[0] * slab.shape[1], CAP)


def total_kernel(factor, *refs):
    part_refs, out_ref = refs[:-1], refs[-1]
    total = part_refs[0][...].astype(jnp.float32)
    for part_ref in part_refs[1:]:
        total = total + part_ref[...].astype(jnp.float32)
    out_ref[...] = (total * factor).astype(jnp.bfloat16)


def last_kernel(members, *refs):
    part_refs, (down_ref, bil_ref, up_ref, atom_ref, flat) = refs[:members], refs[members:]
    me = lax.axis_index("graph")
    model = atom_ref.shape[1]
    rows = flat.shape[0] // members
    held = model // members
    for place, part_ref in enumerate(part_refs):
        source = me ^ place
        flat[pl.ds(pl.multiple_of(source * rows, rows), rows), :] = part_ref[:rows, :]
        for block in range(model // CAP):
            first = rows + block * held
            atom_ref[
                pl.ds(pl.multiple_of(source * held, held), held), block * CAP : (block + 1) * CAP
            ] = part_ref[first : first + held, :].astype(jnp.float32)
    at = 0
    for out in (down_ref, bil_ref, up_ref):
        width = out.shape[0]
        for column in range(0, out.shape[1], CAP):
            out[:, column : column + CAP] = flat[at : at + width, :].astype(jnp.float32)
            at += width


HBM = pl.BlockSpec(memory_space=pltpu.HBM)
VMEM = pl.BlockSpec(memory_space=pltpu.VMEM)
SMEM = pl.BlockSpec(memory_space=pltpu.SMEM)


def swap(value, members, mask, axis="graph"):
    return lax.ppermute(value, axis, [(at, at ^ mask) for at in range(members)])


def scatter_near(near, far, members):
    shape = jax.ShapeDtypeStruct(near.shape[1:], near.dtype)
    sums = pl.pallas_call(
        chip_kernel,
        out_shape=[shape] * (members // 2),
        compiler_params=params(),
        name="chip_sums",
    )(near, swap(far, members, 1))
    return [sums[0]] + [swap(part, members, 2 * at) for at, part in enumerate(sums) if at > 0]


def gather_near(value, members, beside=None):
    even = [value] + [swap(value, members, mask) for mask in range(2, members, 2)]
    if beside is not None:
        even, beside = lax.optimization_barrier((even, beside))
    odd = [swap(piece, members, 1) for piece in even]
    return [piece for pair in zip(even, odd) for piece in pair], beside


def params(limit=VMEM_BYTES):
    return pltpu.CompilerParams(vmem_limit_bytes=limit)


def body(
    edge_emb,
    atom_emb,
    edge_target,
    trip_in,
    trip_out,
    trip_count,
    trip_basis,
    grad_edge,
    grad_atom,
    w_down,
    w_bil,
    w_up,
    w_atom,
):
    members = lax.axis_size("graph")
    edge_rows = edge_emb[0]
    edge_dev, model = edge_rows.shape
    atom_dev = atom_emb.shape[1]
    trips = trip_in.shape[1]
    width = w_down.shape[1]
    tile = math.gcd(trips, TILE_LIMIT)
    f32, b16 = jnp.float32, jnp.bfloat16
    shaped = jax.ShapeDtypeStruct

    down_rows = w_down.T
    bil_rows = w_bil.T
    basis = trip_basis[0]
    projected, feat = pl.pallas_call(
        feature_kernel,
        in_specs=[HBM] * 2,
        out_shape=(
            shaped((width, edge_dev), f32),
            shaped((width, edge_dev), b16),
        ),
        scratch_shapes=[
            pltpu.VMEM(edge_rows.shape, b16),
            pltpu.VMEM(down_rows.shape, b16),
            pltpu.SemaphoreType.DMA((2,)),
        ],
        compiler_params=params(VMEM_MOST),
        name="features",
    )(edge_rows, down_rows)
    rank_rows = members * edge_dev // CAP
    staged = (trip_out, basis, bil_rows, w_up, edge_rows, edge_target)
    slot, rank = pl.pallas_call(
        functools.partial(index_kernel, members),
        in_specs=[VMEM] + [pl.BlockSpec(memory_space=pl.ANY)] * len(staged),
        out_shape=(shaped(trip_in.shape, jnp.int32), shaped((rank_rows, CAP), f32)),
        scratch_shapes=[
            pltpu.VMEM((CAP, trips), b16),
            pltpu.VMEM((rank_rows, CAP), f32),
        ],
        compiler_params=params(),
        cost_estimate=pl.CostEstimate(
            flops=8 * CAP * CAP * trips, bytes_accessed=8 * trips, transcendentals=0
        ),
        name="slots",
    )(trip_in, *staged)
    feats, (slot, rank) = gather_near(feat, members, (slot, rank))

    named_rows = members * CAP // BLOCK * width
    half = shaped((members // 2, atom_dev, model), b16)
    edge_new, near, far, gathered, moment, back = pl.pallas_call(
        functools.partial(forward_kernel, members),
        in_specs=[SMEM] + [VMEM] * (8 + members),
        out_shape=(
            shaped(edge_rows.shape, b16),
            half,
            half,
            shaped((width, edge_dev), b16),
            shaped((w_bil.shape[0], edge_dev), b16),
            shaped((width, w_bil.shape[0]), b16),
        ),
        scratch_shapes=[
            pltpu.VMEM((named_rows, BLOCK), b16),
            pltpu.VMEM((w_bil.shape[0], edge_dev), f32),
            pltpu.VMEM((w_bil.shape[0], tile), b16),
        ],
        compiler_params=params(),
        name="forward_triplets",
    )(
        trip_count,
        slot,
        rank,
        trip_out,
        basis,
        bil_rows,
        w_up,
        edge_rows,
        edge_target,
        *feats,
    )

    atom_block = shaped((atom_dev, model), b16)
    sums = scatter_near(near, far, members)
    atom_new, pair = pl.pallas_call(
        atom_kernel,
        out_shape=(atom_block, shaped((2, atom_dev, model), b16)),
        compiler_params=params(),
        name="atoms",
    )(atom_emb[0], grad_atom[0], w_atom, *sums)
    pairs, _ = gather_near(pair, members)

    piece_rows = width + -(-(edge_dev // CAP) // 16) * 16
    grad_new, wup_term, wbil_term, slab, feat_parts = pl.pallas_call(
        functools.partial(backward_kernel, members),
        in_specs=[SMEM] + [VMEM] * (11 + members),
        out_shape=(
            shaped(edge_rows.shape, f32),
            shaped(w_up.shape, b16),
            shaped((width, w_bil.shape[0]), b16),
            shaped((model // CAP, model // members, CAP), b16),
            shaped((members, piece_rows, CAP), b16),
        ),
        scratch_shapes=[
            pltpu.VMEM((edge_dev // BLOCK * width, BLOCK), b16),
            pltpu.VMEM((w_bil.shape[0], tile), b16),
            pltpu.VMEM((named_rows, tile), b16),
            pltpu.VMEM((named_rows, BLOCK), f32),
            pltpu.VMEM((members * atom_dev, model), b16),
            pltpu.VMEM((members * atom_dev, model), b16),
            pltpu.VMEM((model, model), f32),
        ],
        compiler_params=params(),
        name="backward_triplets",
    )(
        trip_count,
        slot,
        trip_out,
        basis,
        rank,
        back,
        w_up,
        gathered,
        moment,
        grad_edge[0],
        edge_target,
        w_atom,
        *pairs,
    )
    feat_parts = lax.all_to_all(feat_parts, "graph", 0, 0, tiled=True)
    flat_rows = width * (2 * model + w_bil.shape[0]) // CAP
    piece = shaped((members // 2, flat_rows // members, CAP), b16)
    grad_in, near, far = pl.pallas_call(
        edge_kernel,
        out_shape=(shaped(edge_rows.shape, f32), piece, piece),
        scratch_shapes=[pltpu.VMEM((flat_rows, CAP), b16)],
        compiler_params=params(),
        name="edges",
    )(feat_parts, projected, edge_rows, down_rows, grad_new, wbil_term, wup_term)

    batches = lax.axis_size("dp")
    factor = 1.0 / math.sqrt(batches * members * edge_dev)
    share_rows = (flat_rows + model * model // CAP) // members
    share = pl.pallas_call(
        share_kernel,
        out_shape=shaped((share_rows, CAP), b16),
        compiler_params=params(),
        name="share",
    )(slab, *scatter_near(near, far, members))
    share = pl.pallas_call(
        functools.partial(total_kernel, factor),
        out_shape=shaped((share_rows, CAP), b16),
        compiler_params=params(),
        name="total",
    )(share, *[swap(share, batches, mask, "dp") for mask in range(1, batches)])
    shares, _ = gather_near(share, members)
    grad_wdown, grad_wbil, grad_wup, grad_watom = pl.pallas_call(
        functools.partial(last_kernel, members),
        out_shape=(
            shaped((width, model), f32),
            shaped((width, w_bil.shape[0]), f32),
            shaped(w_up.shape, f32),
            shaped((model, model), f32),
        ),
        scratch_shapes=[pltpu.VMEM((flat_rows, CAP), b16)],
        compiler_params=params(),
        name="weights",
    )(*shares)
    return (
        edge_new[None],
        atom_new[None],
        grad_in[None],
        grad_wdown.T,
        grad_wbil.T,
        grad_wup,
        grad_watom,
    )


def solution(mesh):
    return jax.shard_map(
        body,
        mesh=mesh,
        in_specs=(
            P("dp", "graph", None),
            P("dp", "graph", None),
            P("dp", "graph"),
            P("dp", "graph"),
            P("dp", "graph"),
            P("dp", "graph"),
            P("dp", None, "graph"),
            P("dp", "graph", None),
            P("dp", "graph", None),
            P(),
            P(),
            P(),
            P(),
        ),
        out_specs=(
            P("dp", "graph", None),
            P("dp", "graph", None),
            P("dp", "graph", None),
            P(),
            P(),
            P(),
            P(),
        ),
        check_vma=False,
    )
```

```python
import functools
import math

import jax
import jax.numpy as jnp
from jax import lax
from jax.experimental import pallas as pl
from jax.experimental.pallas import tpu as pltpu
from jax.sharding import PartitionSpec as P

ATOM_SCALE = 0.25
BLOCK = 256
CAP = 128
TILE_LIMIT = 2048
INDEX_TILE = 2048
VMEM_BYTES = 24 * 1024 * 1024

FIRST_FIRST = (((0,), (0,)), ((), ()))
LAST_LAST = (((1,), (1,)), ((), ()))


def dot32(left, right, dims=(((1,), (0,)), ((), ()))):
    return lax.dot_general(left, right, dims, preferred_element_type=jnp.float32)


def silu(value):
    return value / (1.0 + jnp.exp(-value))


def silu_slope(value):
    logistic = 1.0 / (1.0 + jnp.exp(-value))
    return logistic * (1.0 + value * (1.0 - logistic))


def row_hot(rows, index):
    iota = lax.broadcasted_iota(jnp.int32, (rows, index.shape[1]), 0)
    if rows > BLOCK:
        return (iota == index).astype(jnp.float32).astype(jnp.bfloat16)
    match = iota.astype(jnp.bfloat16) == index.astype(jnp.bfloat16)
    return jnp.where(match, jnp.bfloat16(1), jnp.bfloat16(0))


def start_copies(pairs, sems):
    copies = [
        pltpu.make_async_copy(source, target, sems.at[place])
        for place, (source, target) in enumerate(pairs)
    ]
    for copy in copies:
        copy.start()
    return copies


def tile_copy(source, target, sems, step, tile):
    span = pl.ds(pl.multiple_of(step * tile, tile), tile)
    return pltpu.make_async_copy(source.at[:, span], target.at[:, span], sems.at[step])


def feature_kernel(emb_hbm, down_hbm, projected_ref, feat_ref, emb_ref, down_ref, sems):
    for copy in start_copies(((emb_hbm, emb_ref), (down_hbm, down_ref)), sems):
        copy.wait()
    projected = dot32(down_ref[...], emb_ref[...], LAST_LAST)
    projected_ref[...] = projected
    feat_ref[...] = silu(projected).astype(jnp.bfloat16)


def index_kernel(members, in_hbm, *refs):
    held = (len(refs) - 6) // 2
    staged, (slot_ref, rank_ref), kept = refs[:held], refs[held : held + 2], refs[held + 2 : -4]
    in_ref, hots, counts, sems = refs[-4:]
    copy, *copies = start_copies(((in_hbm, in_ref), *zip(staged, kept)), sems)
    trips = in_ref.shape[1]
    rows = rank_ref.shape[0]
    turn = lax.axis_index("graph") * (rows // members * CAP)
    tile = math.gcd(trips, INDEX_TILE)
    spans = [slice(at, at + tile) for at in range(0, trips, tile)]
    counts[...] = jnp.zeros_like(counts)
    copy.wait()
    for span in spans:
        incoming = in_ref[:, span] ^ turn
        hot = row_hot(CAP, incoming & (CAP - 1))
        hots[:, span] = hot
        counts[...] += dot32(row_hot(rows, incoming // CAP), hot, LAST_LAST)
    named = (counts[...] > 0.0).astype(jnp.float32)
    per = rows // members
    ahead = (
        lax.broadcasted_iota(jnp.int32, (CAP, CAP), 0)
        < lax.broadcasted_iota(jnp.int32, (CAP, CAP), 1)
    ).astype(jnp.bfloat16)
    row = lax.broadcasted_iota(jnp.int32, (rows, rows), 0)
    other = lax.broadcasted_iota(jnp.int32, (rows, rows), 1)
    above = ((other < row) & (other // per == row // per)).astype(jnp.bfloat16)
    sums = dot32(above, named.astype(jnp.bfloat16))
    before = jnp.sum(sums, axis=1, keepdims=True)
    rank = dot32(named.astype(jnp.bfloat16), ahead) + before
    rank = jnp.where(named > 0.0, rank, -1.0)
    rank_ref[...] = rank
    lookup = rank.astype(jnp.bfloat16)
    for span in spans:
        incoming = in_ref[:, span] ^ turn
        place = incoming // CAP
        found = dot32(lookup, hots[:, span])
        iota = lax.broadcasted_iota(jnp.int32, found.shape, 0)
        found = jnp.sum(jnp.where(iota == place, found, 0.0), axis=0, keepdims=True)
        slot_ref[:, span] = (place // per) * CAP + found.astype(jnp.int32)
    for copy in copies:
        copy.wait()


def rank_row(rank_ref, source, per):
    return jnp.concatenate(
        [rank_ref[source * per + part : source * per + part + 1, :] for part in range(per)], axis=1
    )


def rank_hot(row):
    iota = lax.broadcasted_iota(jnp.int32, (CAP, row.shape[1]), 0).astype(jnp.float32)
    return (iota == row).astype(jnp.float32).astype(jnp.bfloat16)


def forward_kernel(
    members,
    count_ref,
    slot_ref,
    rank_ref,
    *refs,
):
    out_ref, basis_ref, bil_ref, up_ref, emb_ref, target_ref, *refs = refs
    feat_refs, refs = refs[:members], refs[members:]
    new_ref, near_ref, far_ref, gathered_ref, picked_hbm, back_ref, *refs = refs
    table, total, spread, masked, picked_ref, sems = refs
    trips = slot_ref.shape[1]
    tile = spread.shape[1]
    width = bil_ref.shape[0]
    edges = emb_ref.shape[0]
    groups = table.shape[0] // width
    per = BLOCK // width
    count = count_ref[0, 0]
    total[...] = jnp.zeros_like(total)
    for source in range(members):
        row = rank_row(rank_ref, source, edges // CAP)
        chosen = dot32(feat_refs[source][...], rank_hot(row), LAST_LAST)
        group, lane = divmod(source * CAP, BLOCK)
        table[group * width : (group + 1) * width, lane : lane + CAP] = chosen.astype(jnp.bfloat16)

    def one_tile(step, carry):
        span = pl.ds(pl.multiple_of(step * tile, tile), tile)
        slot = slot_ref[:, span]
        high = slot // BLOCK
        hot = row_hot(BLOCK, slot & (BLOCK - 1))
        feat = jnp.zeros((width, tile), jnp.float32)
        for chunk in range(groups // per):
            picked = dot32(table[chunk * BLOCK : (chunk + 1) * BLOCK, :], hot)
            for part in range(per):
                feat = jnp.where(
                    high == chunk * per + part, picked[part * width : (part + 1) * width, :], feat
                )
        feat = feat.astype(jnp.bfloat16)
        picked_ref[:, span] = feat
        tile_copy(picked_ref, picked_hbm, sems, step, tile).start()
        basis = basis_ref[:, span]
        for row in range(basis.shape[0]):
            spread[row * width : (row + 1) * width, :] = feat * basis[row : row + 1, :]
        place = step * tile + lax.broadcasted_iota(jnp.int32, (1, tile), 1)
        outgoing = out_ref[:, span]
        high = jnp.where(place < count, outgoing // BLOCK, -1)
        mixed = dot32(bil_ref[...], spread[...])
        for part in range(edges // BLOCK):
            masked[part * width : (part + 1) * width, :] = jnp.where(
                high == part, mixed, 0.0
            ).astype(jnp.bfloat16)
        total[...] += dot32(masked[...], row_hot(BLOCK, outgoing & (BLOCK - 1)), LAST_LAST)
        return carry

    lax.fori_loop(0, trips // tile, one_tile, 0)
    for step in range(trips // tile):
        tile_copy(picked_ref, picked_hbm, sems, step, tile).wait()
    turned = bil_ref[...].astype(jnp.float32).T
    back_ref[...] = jnp.concatenate(
        [turned[at : at + width] for at in range(0, turned.shape[0], width)], axis=1
    ).astype(jnp.bfloat16)
    gathered = jnp.concatenate(
        [total[at : at + width, :] for at in range(0, total.shape[0], width)], axis=1
    ).astype(jnp.bfloat16)
    gathered_ref[...] = gathered
    update = dot32(gathered, up_ref[...], FIRST_FIRST)
    fresh = (emb_ref[...].astype(jnp.float32) + silu(update)).astype(jnp.bfloat16)
    new_ref[...] = fresh
    held = near_ref.shape[1]
    turn = lax.axis_index("graph") * held
    sums = dot32(row_hot(members * held, target_ref[...] ^ turn), fresh)
    for pair in range(members // 2):
        near_ref[pair] = sums[2 * pair * held : (2 * pair + 1) * held].astype(jnp.bfloat16)
        far_ref[pair] = sums[(2 * pair + 1) * held : (2 * pair + 2) * held].astype(jnp.bfloat16)


def chip_kernel(near_ref, far_ref, *out_refs):
    for pair, out_ref in enumerate(out_refs):
        out_ref[...] = (
            near_ref[pair].astype(jnp.float32) + far_ref[pair].astype(jnp.float32)
        ).astype(jnp.bfloat16)


def atom_kernel(emb_ref, grad_ref, weight_ref, *refs):
    part_refs, (new_ref, pair_ref) = refs[:-2], refs[-2:]
    total = part_refs[0][...].astype(jnp.float32)
    for part_ref in part_refs[1:]:
        total = total + part_ref[...].astype(jnp.float32)
    total = total.astype(jnp.bfloat16)
    pre = ATOM_SCALE * dot32(total, weight_ref[...])
    new_ref[...] = (emb_ref[...].astype(jnp.float32) + silu(pre)).astype(jnp.bfloat16)
    grad_pre = (grad_ref[...].astype(jnp.float32) * silu_slope(pre)).astype(jnp.bfloat16)
    pair_ref[0] = total
    pair_ref[1] = grad_pre


def backward_kernel(
    members,
    count_ref,
    slot_ref,
    out_ref,
    basis_ref,
    rank_ref,
    back_ref,
    up_ref,
    gathered_ref,
    grad_edge_ref,
    target_ref,
    atom_weight_ref,
    *refs,
):
    pair_refs, refs = refs[:members], refs[members:]
    grad_new_ref, up_grad_ref, mixed_hbm, slab_ref, parts_ref, *refs = refs
    table, spread, masked, total, sums, grads, atom_grad, mixed_ref, sems = refs
    trips = slot_ref.shape[1]
    tile = spread.shape[1]
    width = back_ref.shape[0]
    edges = grad_edge_ref.shape[0]
    groups = total.shape[0] // width
    count = count_ref[0, 0]
    me = lax.axis_index("graph")
    held, model = pair_refs[0].shape[1:]
    for source, pair_ref in enumerate(pair_refs):
        sums[source * held : (source + 1) * held, :] = pair_ref[0]
        grads[source * held : (source + 1) * held, :] = pair_ref[1]
    grad_sum = (ATOM_SCALE * dot32(grads[...], atom_weight_ref[...], LAST_LAST)).astype(
        jnp.bfloat16
    )
    atom_grad[...] = ATOM_SCALE * dot32(sums[...], grads[...], FIRST_FIRST)
    share = model // members
    mine = atom_grad[pl.ds(pl.multiple_of(me * share, share), share), :]
    for column in range(0, model, CAP):
        slab_ref[column // CAP] = mine[:, column : column + CAP].astype(jnp.bfloat16)
    total[...] = jnp.zeros_like(total)
    update = dot32(gathered_ref[...], up_ref[...], FIRST_FIRST)
    hot = row_hot(members * held, target_ref[...] ^ (me * held))
    grad_new = grad_edge_ref[...].astype(jnp.float32) + dot32(hot, grad_sum, FIRST_FIRST)
    grad_new_ref[...] = grad_new
    grad_update = (grad_new * silu_slope(update)).astype(jnp.bfloat16)
    up_grad_ref[...] = dot32(gathered_ref[...], grad_update).astype(jnp.bfloat16)
    grad_gathered = dot32(up_ref[...], grad_update, LAST_LAST).astype(jnp.bfloat16)
    for part in range(edges // BLOCK):
        table[part * width : (part + 1) * width, :] = grad_gathered[
            :, part * BLOCK : (part + 1) * BLOCK
        ]

    def one_tile(step, carry):
        span = pl.ds(pl.multiple_of(step * tile, tile), tile)
        place = step * tile + lax.broadcasted_iota(jnp.int32, (1, tile), 1)
        outgoing = jnp.where(place < count, out_ref[:, span], -1)
        picked = dot32(table[...], row_hot(BLOCK, outgoing & (BLOCK - 1)))
        high = jnp.where(outgoing >= 0, outgoing // BLOCK, -1)
        grad = jnp.zeros((width, tile), jnp.float32)
        for part in range(edges // BLOCK):
            grad = jnp.where(high == part, picked[part * width : (part + 1) * width, :], grad)
        grad = grad.astype(jnp.bfloat16)
        mixed_ref[:, span] = grad
        tile_copy(mixed_ref, mixed_hbm, sems, step, tile).start()
        basis = basis_ref[:, span]
        for row in range(basis.shape[0]):
            spread[row * width : (row + 1) * width, :] = grad * basis[row : row + 1, :]
        feat_grad = dot32(back_ref[...], spread[...])
        slot = slot_ref[:, span]
        high_in = slot // BLOCK
        for part in range(groups):
            masked[part * width : (part + 1) * width, :] = jnp.where(
                high_in == part, feat_grad, 0.0
            ).astype(jnp.bfloat16)
        total[...] += dot32(masked[...], row_hot(BLOCK, slot & (BLOCK - 1)), LAST_LAST)
        return carry

    lax.fori_loop(0, trips // tile, one_tile, 0)
    for step in range(trips // tile):
        tile_copy(mixed_ref, mixed_hbm, sems, step, tile).wait()
    per = rank_ref.shape[0] // members
    for source in range(members):
        group, lane = divmod(source * CAP, BLOCK)
        piece = total[group * width : (group + 1) * width, lane : lane + CAP]
        ranks = rank_ref[source * per : (source + 1) * per, :]
        spare = jnp.zeros((parts_ref.shape[1] - width - per, CAP), jnp.float32)
        parts_ref[me ^ source] = jnp.concatenate([piece, ranks, spare], axis=0).astype(jnp.bfloat16)


def weight_kernel(basis_ref, picked_hbm, mixed_hbm, out_ref, picked, mixed, spread, total, sems):
    width, trips = picked.shape
    tile = spread.shape[1]
    steps = trips // tile
    for step in range(steps):
        tile_copy(picked_hbm, picked, sems.at[0], step, tile).start()
        tile_copy(mixed_hbm, mixed, sems.at[1], step, tile).start()
    total[...] = jnp.zeros_like(total)

    def one_tile(step, carry):
        span = pl.ds(pl.multiple_of(step * tile, tile), tile)
        tile_copy(picked_hbm, picked, sems.at[0], step, tile).wait()
        tile_copy(mixed_hbm, mixed, sems.at[1], step, tile).wait()
        feat = picked[:, span]
        basis = basis_ref[:, span]
        for row in range(basis.shape[0]):
            spread[row * width : (row + 1) * width, :] = feat * basis[row : row + 1, :]
        total[...] += dot32(spread[...], mixed[:, span], LAST_LAST)
        return carry

    lax.fori_loop(0, steps, one_tile, 0)
    out_ref[...] = total[...].T.astype(jnp.bfloat16)


def edge_kernel(
    parts_ref,
    projected_ref,
    emb_ref,
    down_ref,
    grad_new_ref,
    bil_grad_ref,
    up_grad_ref,
    grad_in_ref,
    near_ref,
    far_ref,
    flat,
):
    members = parts_ref.shape[0]
    width, edges = projected_ref.shape
    per = edges // CAP
    grad_feat = jnp.zeros((width, edges), jnp.float32)
    for source in range(members):
        part = parts_ref[source].astype(jnp.float32)
        row = jnp.concatenate([part[width + at : width + at + 1] for at in range(per)], axis=1)
        grad_feat = grad_feat + dot32(part[:width].astype(jnp.bfloat16), rank_hot(row))
    grad_project = (grad_feat * silu_slope(projected_ref[...])).astype(jnp.bfloat16)
    grad_in_ref[...] = grad_new_ref[...] + dot32(grad_project, down_ref[...], FIRST_FIRST)
    down_grad = dot32(grad_project, emb_ref[...]).astype(jnp.bfloat16)
    at = 0
    for term in (down_grad, bil_grad_ref[...], up_grad_ref[...]):
        for column in range(0, term.shape[1], CAP):
            flat[at : at + width, :] = term[:, column : column + CAP]
            at += width
    me = lax.axis_index("graph")
    rows = near_ref.shape[1]
    for pair in range(members // 2):
        near_ref[pair] = flat[pl.ds(pl.multiple_of((me ^ (2 * pair)) * rows, rows), rows), :]
        far_ref[pair] = flat[pl.ds(pl.multiple_of((me ^ (2 * pair + 1)) * rows, rows), rows), :]


def share_kernel(slab_ref, *refs):
    part_refs, out_ref = refs[:-1], refs[-1]
    total = part_refs[0][...].astype(jnp.float32)
    for part_ref in part_refs[1:]:
        total = total + part_ref[...].astype(jnp.float32)
    rows = total.shape[0]
    out_ref[:rows, :] = total.astype(jnp.bfloat16)
    slab = slab_ref[...]
    out_ref[rows:, :] = slab.reshape(slab.shape[0] * slab.shape[1], CAP)


def total_kernel(factor, *refs):
    part_refs, out_ref = refs[:-1], refs[-1]
    total = part_refs[0][...].astype(jnp.float32)
    for part_ref in part_refs[1:]:
        total = total + part_ref[...].astype(jnp.float32)
    out_ref[...] = (total * factor).astype(jnp.bfloat16)


def last_kernel(members, *refs):
    part_refs, (down_ref, bil_ref, up_ref, atom_ref, flat) = refs[:members], refs[members:]
    me = lax.axis_index("graph")
    model = atom_ref.shape[1]
    rows = flat.shape[0] // members
    held = model // members
    for place, part_ref in enumerate(part_refs):
        source = me ^ place
        flat[pl.ds(pl.multiple_of(source * rows, rows), rows), :] = part_ref[:rows, :]
        for block in range(model // CAP):
            first = rows + block * held
            atom_ref[
                pl.ds(pl.multiple_of(source * held, held), held), block * CAP : (block + 1) * CAP
            ] = part_ref[first : first + held, :].astype(jnp.float32)
    at = 0
    for out in (down_ref, bil_ref, up_ref):
        width = out.shape[0]
        for column in range(0, out.shape[1], CAP):
            out[:, column : column + CAP] = flat[at : at + width, :].astype(jnp.float32)
            at += width


HBM = pl.BlockSpec(memory_space=pltpu.HBM)
VMEM = pl.BlockSpec(memory_space=pltpu.VMEM)
SMEM = pl.BlockSpec(memory_space=pltpu.SMEM)


def hbm(value):
    return pltpu.with_memory_space_constraint(value, pltpu.HBM)


def swap(value, members, mask, axis="graph"):
    return lax.ppermute(value, axis, [(at, at ^ mask) for at in range(members)])


def scatter_near(near, far, members):
    shape = jax.ShapeDtypeStruct(near.shape[1:], near.dtype)
    sums = pl.pallas_call(
        chip_kernel,
        out_shape=[shape] * (members // 2),
        compiler_params=params(),
        name="chip_sums",
    )(near, swap(far, members, 1))
    return [sums[0]] + [swap(part, members, 2 * at) for at, part in enumerate(sums) if at > 0]


def gather_near(value, members, beside=None):
    even = [value] + [swap(value, members, mask) for mask in range(2, members, 2)]
    if beside is not None:
        even, beside = lax.optimization_barrier((even, beside))
    odd = [swap(piece, members, 1) for piece in even]
    return [piece for pair in zip(even, odd) for piece in pair], beside


def params(limit=VMEM_BYTES):
    return pltpu.CompilerParams(vmem_limit_bytes=limit)


def cost(flops):
    return pl.CostEstimate(flops=flops, bytes_accessed=1 << 20, transcendentals=0)


def body(
    edge_emb,
    atom_emb,
    edge_target,
    trip_in,
    trip_out,
    trip_count,
    trip_basis,
    grad_edge,
    grad_atom,
    w_down,
    w_bil,
    w_up,
    w_atom,
):
    members = lax.axis_size("graph")
    edge_rows = edge_emb[0]
    edge_dev, model = edge_rows.shape
    atom_dev = atom_emb.shape[1]
    trips = trip_in.shape[1]
    width = w_down.shape[1]
    tile = math.gcd(trips, TILE_LIMIT)
    f32, b16 = jnp.float32, jnp.bfloat16
    shaped = jax.ShapeDtypeStruct

    down_rows = w_down.T
    bil_rows = w_bil.T
    basis = trip_basis[0]
    projected, feat = pl.pallas_call(
        feature_kernel,
        in_specs=[HBM] * 2,
        out_shape=(
            shaped((width, edge_dev), f32),
            shaped((width, edge_dev), b16),
        ),
        scratch_shapes=[
            pltpu.VMEM(edge_rows.shape, b16),
            pltpu.VMEM(down_rows.shape, b16),
            pltpu.SemaphoreType.DMA((2,)),
        ],
        compiler_params=params(),
        cost_estimate=cost(16 * edge_rows.size * width),
        name="features",
    )(hbm(edge_rows), hbm(down_rows))
    rank_rows = members * edge_dev // CAP
    staged = (trip_out, basis, bil_rows, w_up, edge_rows, edge_target)
    slot, rank, *kept = pl.pallas_call(
        functools.partial(index_kernel, members),
        in_specs=[HBM] * (1 + len(staged)),
        out_shape=(
            shaped(trip_in.shape, jnp.int32),
            shaped((rank_rows, CAP), f32),
            *[shaped(value.shape, value.dtype) for value in staged],
        ),
        scratch_shapes=[
            pltpu.VMEM(trip_in.shape, jnp.int32),
            pltpu.VMEM((CAP, trips), b16),
            pltpu.VMEM((rank_rows, CAP), f32),
            pltpu.SemaphoreType.DMA((1 + len(staged),)),
        ],
        compiler_params=params(),
        cost_estimate=cost(8 * CAP * CAP * trips),
        name="slots",
    )(*[hbm(value) for value in (trip_in, *staged)])
    feats, (slot, rank, *kept) = gather_near(feat, members, (slot, rank, *kept))

    named_rows = members * CAP // BLOCK * width
    half = shaped((members // 2, atom_dev, model), b16)
    edge_new, near, far, gathered, picked, back = pl.pallas_call(
        functools.partial(forward_kernel, members),
        in_specs=[SMEM] + [VMEM] * (2 + len(kept) + members),
        out_specs=(VMEM, VMEM, VMEM, VMEM, HBM, VMEM),
        out_shape=(
            shaped(edge_rows.shape, b16),
            half,
            half,
            shaped((width, edge_dev), b16),
            pltpu.HBM((width, trips), b16),
            shaped((width, w_bil.shape[0]), b16),
        ),
        scratch_shapes=[
            pltpu.VMEM((named_rows, BLOCK), b16),
            pltpu.VMEM((edge_dev // BLOCK * width, BLOCK), f32),
            pltpu.VMEM((w_bil.shape[0], tile), b16),
            pltpu.VMEM((edge_dev // BLOCK * width, tile), b16),
            pltpu.VMEM((width, trips), b16),
            pltpu.SemaphoreType.DMA((trips // tile,)),
        ],
        compiler_params=params(),
        cost_estimate=cost(12 * w_bil.size * trips),
        name="forward_triplets",
    )(
        trip_count,
        slot,
        rank,
        *kept,
        *feats,
    )

    atom_block = shaped((atom_dev, model), b16)
    sums = scatter_near(near, far, members)
    atom_new, pair = pl.pallas_call(
        atom_kernel,
        out_shape=(atom_block, shaped((2, atom_dev, model), b16)),
        compiler_params=params(),
        cost_estimate=cost(16 * atom_dev * w_atom.size),
        name="atoms",
    )(atom_emb[0], grad_atom[0], w_atom, *sums)
    pairs, _ = gather_near(pair, members)

    piece_rows = width + -(-(edge_dev // CAP) // 16) * 16
    grad_new, wup_term, mixed, slab, feat_parts = pl.pallas_call(
        functools.partial(backward_kernel, members),
        in_specs=[SMEM] + [VMEM] * (10 + members),
        out_specs=(VMEM, VMEM, HBM, VMEM, VMEM),
        out_shape=(
            shaped(edge_rows.shape, f32),
            shaped(w_up.shape, b16),
            pltpu.HBM((width, trips), b16),
            shaped((model // CAP, model // members, CAP), b16),
            shaped((members, piece_rows, CAP), b16),
        ),
        scratch_shapes=[
            pltpu.VMEM((edge_dev // BLOCK * width, BLOCK), b16),
            pltpu.VMEM((w_bil.shape[0], tile), b16),
            pltpu.VMEM((named_rows, tile), b16),
            pltpu.VMEM((named_rows, BLOCK), f32),
            pltpu.VMEM((members * atom_dev, model), b16),
            pltpu.VMEM((members * atom_dev, model), b16),
            pltpu.VMEM((model, model), f32),
            pltpu.VMEM((width, trips), b16),
            pltpu.SemaphoreType.DMA((trips // tile,)),
        ],
        compiler_params=params(),
        cost_estimate=cost(12 * w_bil.size * trips),
        name="backward_triplets",
    )(
        trip_count,
        slot,
        kept[0],
        kept[1],
        rank,
        back,
        kept[3],
        gathered,
        grad_edge[0],
        kept[5],
        w_atom,
        *pairs,
    )
    feat_parts = lax.all_to_all(feat_parts, "graph", 0, 0, tiled=True)
    wide = math.gcd(trips, 2 * tile)
    wbil_term = pl.pallas_call(
        weight_kernel,
        in_specs=[VMEM, HBM, HBM],
        out_shape=shaped((width, w_bil.shape[0]), b16),
        scratch_shapes=[
            pltpu.VMEM((width, trips), b16),
            pltpu.VMEM((width, trips), b16),
            pltpu.VMEM((w_bil.shape[0], wide), b16),
            pltpu.VMEM((w_bil.shape[0], width), f32),
            pltpu.SemaphoreType.DMA((2, trips // wide)),
        ],
        compiler_params=params(),
        cost_estimate=cost(8 * w_bil.size * trips),
        name="bilinear_weights",
    )(kept[1], hbm(picked), hbm(mixed))
    flat_rows = width * (2 * model + w_bil.shape[0]) // CAP
    piece = shaped((members // 2, flat_rows // members, CAP), b16)
    grad_in, near, far = pl.pallas_call(
        edge_kernel,
        out_shape=(shaped(edge_rows.shape, f32), piece, piece),
        scratch_shapes=[pltpu.VMEM((flat_rows, CAP), b16)],
        compiler_params=params(),
        cost_estimate=cost(64 * edge_rows.size * width),
        name="edges",
    )(feat_parts, projected, edge_rows, down_rows, grad_new, wbil_term, wup_term)

    batches = lax.axis_size("dp")
    factor = 1.0 / math.sqrt(batches * members * edge_dev)
    share_rows = (flat_rows + model * model // CAP) // members
    share = pl.pallas_call(
        share_kernel,
        out_shape=shaped((share_rows, CAP), b16),
        compiler_params=params(),
        name="share",
    )(slab, *scatter_near(near, far, members))
    share = pl.pallas_call(
        functools.partial(total_kernel, factor),
        out_shape=shaped((share_rows, CAP), b16),
        compiler_params=params(),
        name="total",
    )(share, *[swap(share, batches, mask, "dp") for mask in range(1, batches)])
    shares, _ = gather_near(share, members)
    grad_wdown, grad_wbil, grad_wup, grad_watom = pl.pallas_call(
        functools.partial(last_kernel, members),
        out_shape=(
            shaped((width, model), f32),
            shaped((width, w_bil.shape[0]), f32),
            shaped(w_up.shape, f32),
            shaped((model, model), f32),
        ),
        scratch_shapes=[pltpu.VMEM((flat_rows, CAP), b16)],
        compiler_params=params(),
        name="weights",
    )(*shares)
    return (
        edge_new[None],
        atom_new[None],
        grad_in[None],
        grad_wdown.T,
        grad_wbil.T,
        grad_wup,
        grad_watom,
    )


def solution(mesh):
    return jax.shard_map(
        body,
        mesh=mesh,
        in_specs=(
            P("dp", "graph", None),
            P("dp", "graph", None),
            P("dp", "graph"),
            P("dp", "graph"),
            P("dp", "graph"),
            P("dp", "graph"),
            P("dp", None, "graph"),
            P("dp", "graph", None),
            P("dp", "graph", None),
            P(),
            P(),
            P(),
            P(),
        ),
        out_specs=(
            P("dp", "graph", None),
            P("dp", "graph", None),
            P("dp", "graph", None),
            P(),
            P(),
            P(),
            P(),
        ),
        check_vma=False,
    )
```

```python
import functools
import math

import jax
import jax.numpy as jnp
from jax import lax
from jax.experimental import pallas as pl
from jax.experimental.pallas import tpu as pltpu
from jax.sharding import PartitionSpec as P

ATOM_SCALE = 0.25
BLOCK = 256
CAP = 128
TILE_LIMIT = 4096
FORWARD_LIMIT = 8192
INDEX_TILE = 2048
VMEM_BYTES = 32 * 1024 * 1024

FIRST_FIRST = (((0,), (0,)), ((), ()))
LAST_LAST = (((1,), (1,)), ((), ()))


def dot32(left, right, dims=(((1,), (0,)), ((), ()))):
    return lax.dot_general(left, right, dims, preferred_element_type=jnp.float32)


def silu(value):
    return value / (1.0 + jnp.exp(-value))


def silu_slope(value):
    logistic = 1.0 / (1.0 + jnp.exp(-value))
    return logistic * (1.0 + value * (1.0 - logistic))


def row_hot(rows, index):
    iota = lax.broadcasted_iota(jnp.int32, (rows, index.shape[1]), 0)
    if rows > BLOCK:
        return (iota == index).astype(jnp.float32).astype(jnp.bfloat16)
    match = iota.astype(jnp.bfloat16) == index.astype(jnp.bfloat16)
    return jnp.where(match, jnp.bfloat16(1), jnp.bfloat16(0))


def start_copies(pairs, sems):
    copies = [
        pltpu.make_async_copy(source, target, sems.at[place])
        for place, (source, target) in enumerate(pairs)
    ]
    for copy in copies:
        copy.start()
    return copies


def tile_copy(source, target, sems, step, tile):
    span = pl.ds(pl.multiple_of(step * tile, tile), tile)
    return pltpu.make_async_copy(source.at[:, span], target.at[:, span], sems.at[step])


def feature_kernel(emb_hbm, down_hbm, projected_ref, feat_ref, emb_ref, down_ref, sems):
    for copy in start_copies(((emb_hbm, emb_ref), (down_hbm, down_ref)), sems):
        copy.wait()
    projected = dot32(down_ref[...], emb_ref[...], LAST_LAST)
    projected_ref[...] = projected
    feat_ref[...] = silu(projected).astype(jnp.bfloat16)


def index_kernel(members, in_hbm, *refs):
    held = (len(refs) - 7) // 2
    staged, (slot_ref, rank_ref, back_ref) = refs[:held], refs[held : held + 3]
    kept = refs[held + 3 : -4]
    in_ref, hots, counts, sems = refs[-4:]
    copy, *copies = start_copies(((in_hbm, in_ref), *zip(staged, kept)), sems)
    trips = in_ref.shape[1]
    rows = rank_ref.shape[0]
    turn = lax.axis_index("graph") * (rows // members * CAP)
    tile = math.gcd(trips, INDEX_TILE)
    spans = [slice(at, at + tile) for at in range(0, trips, tile)]
    counts[...] = jnp.zeros_like(counts)
    copy.wait()
    for span in spans:
        incoming = in_ref[:, span] ^ turn
        hot = row_hot(CAP, incoming & (CAP - 1))
        hots[:, span] = hot
        counts[...] += dot32(row_hot(rows, incoming // CAP), hot, LAST_LAST)
    named = (counts[...] > 0.0).astype(jnp.float32)
    per = rows // members
    ahead = (
        lax.broadcasted_iota(jnp.int32, (CAP, CAP), 0)
        < lax.broadcasted_iota(jnp.int32, (CAP, CAP), 1)
    ).astype(jnp.bfloat16)
    row = lax.broadcasted_iota(jnp.int32, (rows, rows), 0)
    other = lax.broadcasted_iota(jnp.int32, (rows, rows), 1)
    above = ((other < row) & (other // per == row // per)).astype(jnp.bfloat16)
    sums = dot32(above, named.astype(jnp.bfloat16))
    before = jnp.sum(sums, axis=1, keepdims=True)
    rank = dot32(named.astype(jnp.bfloat16), ahead) + before
    rank = jnp.where(named > 0.0, rank, -1.0)
    rank_ref[...] = rank
    lookup = rank.astype(jnp.bfloat16)
    for span in spans:
        incoming = in_ref[:, span] ^ turn
        place = incoming // CAP
        found = dot32(lookup, hots[:, span])
        iota = lax.broadcasted_iota(jnp.int32, found.shape, 0)
        found = jnp.sum(jnp.where(iota == place, found, 0.0), axis=0, keepdims=True)
        slot_ref[:, span] = (place // per) * CAP + found.astype(jnp.int32)
    for copy in copies:
        copy.wait()
    bil_ref = kept[2]
    width = bil_ref.shape[0]
    turned = bil_ref[...].astype(jnp.float32).T
    back_ref[...] = jnp.concatenate(
        [turned[at : at + width] for at in range(0, turned.shape[0], width)], axis=1
    ).astype(jnp.bfloat16)


def rank_row(rank_ref, source, per):
    return jnp.concatenate(
        [rank_ref[source * per + part : source * per + part + 1, :] for part in range(per)], axis=1
    )


def rank_hot(row):
    iota = lax.broadcasted_iota(jnp.int32, (CAP, row.shape[1]), 0).astype(jnp.float32)
    return (iota == row).astype(jnp.float32).astype(jnp.bfloat16)


def forward_kernel(
    members,
    count_ref,
    slot_ref,
    rank_ref,
    *refs,
):
    out_ref, basis_ref, bil_ref, up_ref, emb_ref, target_ref, *refs = refs
    feat_refs, refs = refs[:members][::-1], refs[members:]
    new_ref, near_ref, far_ref, gathered_ref, picked_hbm, *refs = refs
    table, total, spread, masked, picked_ref, sems = refs
    trips = slot_ref.shape[1]
    tile = spread.shape[1]
    width = bil_ref.shape[0]
    edges = emb_ref.shape[0]
    groups = table.shape[0] // width
    per = BLOCK // width
    count = count_ref[0, 0]
    total[...] = jnp.zeros_like(total)
    for source in range(members):
        row = rank_row(rank_ref, source, edges // CAP)
        chosen = dot32(feat_refs[source][...], rank_hot(row), LAST_LAST)
        group, lane = divmod(source * CAP, BLOCK)
        table[group * width : (group + 1) * width, lane : lane + CAP] = chosen.astype(jnp.bfloat16)

    def one_tile(step, carry):
        span = pl.ds(pl.multiple_of(step * tile, tile), tile)
        slot = slot_ref[:, span]
        high = slot // BLOCK
        hot = row_hot(BLOCK, slot & (BLOCK - 1))
        feat = jnp.zeros((width, tile), jnp.float32)
        for chunk in range(groups // per):
            picked = dot32(table[chunk * BLOCK : (chunk + 1) * BLOCK, :], hot)
            for part in range(per):
                feat = jnp.where(
                    high == chunk * per + part, picked[part * width : (part + 1) * width, :], feat
                )
        feat = feat.astype(jnp.bfloat16)
        picked_ref[:, span] = feat
        tile_copy(picked_ref, picked_hbm, sems, step, tile).start()
        basis = basis_ref[:, span]
        for row in range(basis.shape[0]):
            spread[row * width : (row + 1) * width, :] = feat * basis[row : row + 1, :]
        place = step * tile + lax.broadcasted_iota(jnp.int32, (1, tile), 1)
        outgoing = out_ref[:, span]
        high = jnp.where(place < count, outgoing // BLOCK, -1)
        mixed = dot32(bil_ref[...], spread[...])
        for part in range(edges // BLOCK):
            masked[part * width : (part + 1) * width, :] = jnp.where(
                high == part, mixed, 0.0
            ).astype(jnp.bfloat16)
        total[...] += dot32(masked[...], row_hot(BLOCK, outgoing & (BLOCK - 1)), LAST_LAST)
        return carry

    lax.fori_loop(0, trips // tile, one_tile, 0)
    for step in range(trips // tile):
        tile_copy(picked_ref, picked_hbm, sems, step, tile).wait()
    gathered = jnp.concatenate(
        [total[at : at + width, :] for at in range(0, total.shape[0], width)], axis=1
    ).astype(jnp.bfloat16)
    gathered_ref[...] = gathered
    update = dot32(gathered, up_ref[...], FIRST_FIRST)
    fresh = (emb_ref[...].astype(jnp.float32) + silu(update)).astype(jnp.bfloat16)
    new_ref[...] = fresh
    held = near_ref.shape[1]
    turn = lax.axis_index("graph") * held
    sums = dot32(row_hot(members * held, target_ref[...] ^ turn), fresh)
    for pair in range(members // 2):
        near_ref[pair] = sums[2 * pair * held : (2 * pair + 1) * held].astype(jnp.bfloat16)
        far_ref[pair] = sums[(2 * pair + 1) * held : (2 * pair + 2) * held].astype(jnp.bfloat16)


def chip_kernel(near_ref, far_ref, *out_refs):
    for pair, out_ref in enumerate(out_refs):
        out_ref[...] = (
            near_ref[pair].astype(jnp.float32) + far_ref[pair].astype(jnp.float32)
        ).astype(jnp.bfloat16)


def atom_kernel(emb_ref, grad_ref, weight_ref, *refs):
    part_refs, (new_ref, pair_ref) = refs[:-2], refs[-2:]
    total = part_refs[0][...].astype(jnp.float32)
    for part_ref in part_refs[1:]:
        total = total + part_ref[...].astype(jnp.float32)
    total = total.astype(jnp.bfloat16)
    pre = ATOM_SCALE * dot32(total, weight_ref[...])
    new_ref[...] = (emb_ref[...].astype(jnp.float32) + silu(pre)).astype(jnp.bfloat16)
    grad_pre = (grad_ref[...].astype(jnp.float32) * silu_slope(pre)).astype(jnp.bfloat16)
    pair_ref[0] = total
    pair_ref[1] = grad_pre


def slope_kernel(gathered_ref, up_ref, slope_ref):
    slope_ref[...] = silu_slope(dot32(gathered_ref[...], up_ref[...], FIRST_FIRST))


def slab_kernel(members, *refs):
    pair_refs, (slab_ref, sums, grads, atom_grad) = refs[:members], refs[members:]
    me = lax.axis_index("graph")
    held, model = pair_refs[0].shape[1:]
    for source, pair_ref in enumerate(pair_refs):
        sums[source * held : (source + 1) * held, :] = pair_ref[0]
        grads[source * held : (source + 1) * held, :] = pair_ref[1]
    atom_grad[...] = ATOM_SCALE * dot32(sums[...], grads[...], FIRST_FIRST)
    share = model // members
    mine = atom_grad[pl.ds(pl.multiple_of(me * share, share), share), :]
    for column in range(0, model, CAP):
        slab_ref[column // CAP] = mine[:, column : column + CAP].astype(jnp.bfloat16)


def backward_kernel(
    members,
    count_ref,
    slot_ref,
    out_ref,
    basis_ref,
    rank_ref,
    back_ref,
    up_ref,
    gathered_ref,
    slope_ref,
    grad_edge_ref,
    target_ref,
    atom_weight_ref,
    *refs,
):
    pair_refs, refs = refs[:members][::-1], refs[members:]
    grad_new_ref, up_grad_ref, mixed_hbm, parts_ref, *refs = refs
    table, spread, masked, total, grads, mixed_ref, sems = refs
    trips = slot_ref.shape[1]
    tile = spread.shape[1]
    width = back_ref.shape[0]
    edges = grad_edge_ref.shape[0]
    groups = total.shape[0] // width
    count = count_ref[0, 0]
    me = lax.axis_index("graph")
    held = pair_refs[0].shape[1]
    for source, pair_ref in enumerate(pair_refs):
        grads[source * held : (source + 1) * held, :] = pair_ref[1]
    grad_sum = (ATOM_SCALE * dot32(grads[...], atom_weight_ref[...], LAST_LAST)).astype(
        jnp.bfloat16
    )
    total[...] = jnp.zeros_like(total)
    hot = row_hot(members * held, target_ref[...] ^ (me * held))
    grad_new = grad_edge_ref[...].astype(jnp.float32) + dot32(hot, grad_sum, FIRST_FIRST)
    grad_new_ref[...] = grad_new
    grad_update = (grad_new * slope_ref[...]).astype(jnp.bfloat16)
    up_grad_ref[...] = dot32(gathered_ref[...], grad_update).astype(jnp.bfloat16)
    grad_gathered = dot32(up_ref[...], grad_update, LAST_LAST).astype(jnp.bfloat16)
    for part in range(edges // BLOCK):
        table[part * width : (part + 1) * width, :] = grad_gathered[
            :, part * BLOCK : (part + 1) * BLOCK
        ]

    def one_tile(step, carry):
        span = pl.ds(pl.multiple_of(step * tile, tile), tile)
        place = step * tile + lax.broadcasted_iota(jnp.int32, (1, tile), 1)
        outgoing = jnp.where(place < count, out_ref[:, span], -1)
        picked = dot32(table[...], row_hot(BLOCK, outgoing & (BLOCK - 1)))
        high = jnp.where(outgoing >= 0, outgoing // BLOCK, -1)
        grad = jnp.zeros((width, tile), jnp.float32)
        for part in range(edges // BLOCK):
            grad = jnp.where(high == part, picked[part * width : (part + 1) * width, :], grad)
        grad = grad.astype(jnp.bfloat16)
        mixed_ref[:, span] = grad
        tile_copy(mixed_ref, mixed_hbm, sems, step, tile).start()
        basis = basis_ref[:, span]
        for row in range(basis.shape[0]):
            spread[row * width : (row + 1) * width, :] = grad * basis[row : row + 1, :]
        feat_grad = dot32(back_ref[...], spread[...])
        slot = slot_ref[:, span]
        high_in = slot // BLOCK
        for part in range(groups):
            masked[part * width : (part + 1) * width, :] = jnp.where(
                high_in == part, feat_grad, 0.0
            ).astype(jnp.bfloat16)
        total[...] += dot32(masked[...], row_hot(BLOCK, slot & (BLOCK - 1)), LAST_LAST)
        return carry

    lax.fori_loop(0, trips // tile, one_tile, 0)
    for step in range(trips // tile):
        tile_copy(mixed_ref, mixed_hbm, sems, step, tile).wait()
    per = rank_ref.shape[0] // members
    for source in range(members):
        group, lane = divmod(source * CAP, BLOCK)
        piece = total[group * width : (group + 1) * width, lane : lane + CAP]
        ranks = rank_ref[source * per : (source + 1) * per, :]
        spare = jnp.zeros((parts_ref.shape[1] - width - per, CAP), jnp.float32)
        parts_ref[me ^ source] = jnp.concatenate([piece, ranks, spare], axis=0).astype(jnp.bfloat16)


def weight_kernel(basis_ref, picked_hbm, mixed_hbm, out_ref, picked, mixed, spread, total, sems):
    width, trips = picked.shape
    tile = spread.shape[1]
    steps = trips // tile
    for step in range(steps):
        tile_copy(picked_hbm, picked, sems.at[0], step, tile).start()
        tile_copy(mixed_hbm, mixed, sems.at[1], step, tile).start()
    total[...] = jnp.zeros_like(total)

    def one_tile(step, carry):
        span = pl.ds(pl.multiple_of(step * tile, tile), tile)
        tile_copy(picked_hbm, picked, sems.at[0], step, tile).wait()
        tile_copy(mixed_hbm, mixed, sems.at[1], step, tile).wait()
        feat = picked[:, span]
        basis = basis_ref[:, span]
        for row in range(basis.shape[0]):
            spread[row * width : (row + 1) * width, :] = feat * basis[row : row + 1, :]
        total[...] += dot32(spread[...], mixed[:, span], LAST_LAST)
        return carry

    lax.fori_loop(0, steps, one_tile, 0)
    out_ref[...] = total[...].T.astype(jnp.bfloat16)


def input_kernel(grad_project_ref, down_ref, grad_new_ref, grad_in_ref):
    grad_in_ref[...] = grad_new_ref[...] + dot32(
        grad_project_ref[...], down_ref[...], FIRST_FIRST
    )


def edge_kernel(
    parts_ref,
    projected_ref,
    emb_ref,
    bil_grad_ref,
    up_grad_ref,
    grad_project_ref,
    near_ref,
    far_ref,
    flat,
):
    members = parts_ref.shape[0]
    width, edges = projected_ref.shape
    per = edges // CAP
    grad_feat = jnp.zeros((width, edges), jnp.float32)
    for source in range(members):
        part = parts_ref[source].astype(jnp.float32)
        row = jnp.concatenate([part[width + at : width + at + 1] for at in range(per)], axis=1)
        grad_feat = grad_feat + dot32(part[:width].astype(jnp.bfloat16), rank_hot(row))
    grad_project = (grad_feat * silu_slope(projected_ref[...])).astype(jnp.bfloat16)
    grad_project_ref[...] = grad_project
    down_grad = dot32(grad_project, emb_ref[...]).astype(jnp.bfloat16)
    at = 0
    for term in (down_grad, bil_grad_ref[...], up_grad_ref[...]):
        for column in range(0, term.shape[1], CAP):
            flat[at : at + width, :] = term[:, column : column + CAP]
            at += width
    me = lax.axis_index("graph")
    rows = near_ref.shape[1]
    for pair in range(members // 2):
        near_ref[pair] = flat[pl.ds(pl.multiple_of((me ^ (2 * pair)) * rows, rows), rows), :]
        far_ref[pair] = flat[pl.ds(pl.multiple_of((me ^ (2 * pair + 1)) * rows, rows), rows), :]


def share_kernel(slab_ref, *refs):
    part_refs, out_ref = refs[:-1], refs[-1]
    total = part_refs[0][...].astype(jnp.float32)
    for part_ref in part_refs[1:]:
        total = total + part_ref[...].astype(jnp.float32)
    rows = total.shape[0]
    out_ref[:rows, :] = total.astype(jnp.bfloat16)
    slab = slab_ref[...]
    out_ref[rows:, :] = slab.reshape(slab.shape[0] * slab.shape[1], CAP)


def total_kernel(factor, *refs):
    parts = [part_ref[...].astype(jnp.float32) for part_ref in refs[:-1]]
    while len(parts) > 1:
        parts = [left + right for left, right in zip(parts[::2], parts[1::2])]
    refs[-1][...] = (parts[0] * factor).astype(jnp.bfloat16)


def last_kernel(members, *refs):
    part_refs, (down_ref, bil_ref, up_ref, atom_ref, flat) = refs[:members][::-1], refs[members:]
    me = lax.axis_index("graph")
    model = atom_ref.shape[1]
    rows = flat.shape[0] // members
    held = model // members
    for place, part_ref in enumerate(part_refs):
        source = me ^ place
        flat[pl.ds(pl.multiple_of(source * rows, rows), rows), :] = part_ref[:rows, :]
        for block in range(model // CAP):
            first = rows + block * held
            atom_ref[
                pl.ds(pl.multiple_of(source * held, held), held), block * CAP : (block + 1) * CAP
            ] = part_ref[first : first + held, :].astype(jnp.float32)
    at = 0
    for out in (down_ref, bil_ref, up_ref):
        width = out.shape[0]
        for column in range(0, out.shape[1], CAP):
            out[:, column : column + CAP] = flat[at : at + width, :].astype(jnp.float32)
            at += width


HBM = pl.BlockSpec(memory_space=pltpu.HBM)
VMEM = pl.BlockSpec(memory_space=pltpu.VMEM)
SMEM = pl.BlockSpec(memory_space=pltpu.SMEM)


def hbm(value):
    return pltpu.with_memory_space_constraint(value, pltpu.HBM)


def swap(value, members, mask, axis="graph"):
    return lax.ppermute(value, axis, [(at, at ^ mask) for at in range(members)])


def scatter_near(near, far, members):
    shape = jax.ShapeDtypeStruct(near.shape[1:], near.dtype)
    sums = pl.pallas_call(
        chip_kernel,
        out_shape=[shape] * (members // 2),
        compiler_params=params(),
        name="chip_sums",
    )(near, swap(far, members, 1))
    return [sums[0]] + [swap(part, members, 2 * at) for at, part in enumerate(sums) if at > 0]


def gather_near(value, members, beside=None):
    even = [value] + [swap(value, members, mask) for mask in range(2, members, 2)]
    if beside is not None:
        back_even, beside = lax.optimization_barrier((even[::-1], beside))
        even = back_even[::-1]
    odd = [swap(piece, members, 1) for piece in even]
    return [piece for pair in zip(even, odd) for piece in pair], beside


def params(limit=VMEM_BYTES):
    return pltpu.CompilerParams(vmem_limit_bytes=limit)


def cost(flops):
    return pl.CostEstimate(flops=flops, bytes_accessed=1 << 20, transcendentals=0)


def body(
    edge_emb,
    atom_emb,
    edge_target,
    trip_in,
    trip_out,
    trip_count,
    trip_basis,
    grad_edge,
    grad_atom,
    w_down,
    w_bil,
    w_up,
    w_atom,
):
    members = lax.axis_size("graph")
    edge_rows = edge_emb[0]
    edge_dev, model = edge_rows.shape
    atom_dev = atom_emb.shape[1]
    trips = trip_in.shape[1]
    width = w_down.shape[1]
    tile = math.gcd(trips, TILE_LIMIT)
    long = math.gcd(trips, FORWARD_LIMIT)
    f32, b16 = jnp.float32, jnp.bfloat16
    shaped = jax.ShapeDtypeStruct

    down_rows = w_down.T
    bil_rows = w_bil.T
    basis = trip_basis[0]
    projected, feat = pl.pallas_call(
        feature_kernel,
        in_specs=[HBM] * 2,
        out_shape=(
            shaped((width, edge_dev), f32),
            shaped((width, edge_dev), b16),
        ),
        scratch_shapes=[
            pltpu.VMEM(edge_rows.shape, b16),
            pltpu.VMEM(down_rows.shape, b16),
            pltpu.SemaphoreType.DMA((2,)),
        ],
        compiler_params=params(),
        cost_estimate=cost(16 * edge_rows.size * width),
        name="features",
    )(hbm(edge_rows), hbm(down_rows))
    rank_rows = members * edge_dev // CAP
    staged = (trip_out, basis, bil_rows, w_up, edge_rows, edge_target)
    slot, rank, back, *kept = pl.pallas_call(
        functools.partial(index_kernel, members),
        in_specs=[HBM] * (1 + len(staged)),
        out_shape=(
            shaped(trip_in.shape, jnp.int32),
            shaped((rank_rows, CAP), f32),
            shaped(bil_rows.shape, b16),
            *[shaped(value.shape, value.dtype) for value in staged],
        ),
        scratch_shapes=[
            pltpu.VMEM(trip_in.shape, jnp.int32),
            pltpu.VMEM((CAP, trips), b16),
            pltpu.VMEM((rank_rows, CAP), f32),
            pltpu.SemaphoreType.DMA((1 + len(staged),)),
        ],
        compiler_params=params(),
        cost_estimate=cost(8 * CAP * CAP * trips),
        name="slots",
    )(*[hbm(value) for value in (trip_in, *staged)])
    feats, (slot, rank, back, *kept) = gather_near(feat, members, (slot, rank, back, *kept))

    named_rows = members * CAP // BLOCK * width
    half = shaped((members // 2, atom_dev, model), b16)
    edge_new, near, far, gathered, picked = pl.pallas_call(
        functools.partial(forward_kernel, members),
        in_specs=[SMEM] + [VMEM] * (2 + len(kept) + members),
        out_specs=(VMEM, VMEM, VMEM, VMEM, HBM),
        out_shape=(
            shaped(edge_rows.shape, b16),
            half,
            half,
            shaped((width, edge_dev), b16),
            pltpu.HBM((width, trips), b16),
        ),
        scratch_shapes=[
            pltpu.VMEM((named_rows, BLOCK), b16),
            pltpu.VMEM((edge_dev // BLOCK * width, BLOCK), f32),
            pltpu.VMEM((w_bil.shape[0], long), b16),
            pltpu.VMEM((edge_dev // BLOCK * width, long), b16),
            pltpu.VMEM((width, trips), b16),
            pltpu.SemaphoreType.DMA((trips // long,)),
        ],
        compiler_params=params(),
        cost_estimate=cost(12 * w_bil.size * trips),
        name="forward_triplets",
    )(
        trip_count,
        slot,
        rank,
        *kept,
        *feats[::-1],
    )

    atom_block = shaped((atom_dev, model), b16)
    slope = pl.pallas_call(
        slope_kernel,
        out_shape=shaped(edge_rows.shape, f32),
        compiler_params=params(),
        cost_estimate=cost(64 * edge_rows.size * width),
        name="slopes",
    )(gathered, kept[3])
    sums = scatter_near(near, far, members)
    sums, slope = lax.optimization_barrier((sums[::-1], slope))
    sums = sums[::-1]
    atom_new, pair = pl.pallas_call(
        atom_kernel,
        out_shape=(atom_block, shaped((2, atom_dev, model), b16)),
        compiler_params=params(),
        cost_estimate=cost(16 * atom_dev * w_atom.size),
        name="atoms",
    )(atom_emb[0], grad_atom[0], w_atom, *sums[::-1])
    pairs, _ = gather_near(pair, members)

    piece_rows = width + -(-(edge_dev // CAP) // 16) * 16
    grad_new, wup_term, mixed, feat_parts = pl.pallas_call(
        functools.partial(backward_kernel, members),
        in_specs=[SMEM] + [VMEM] * (11 + members),
        out_specs=(VMEM, VMEM, HBM, VMEM),
        out_shape=(
            shaped(edge_rows.shape, f32),
            shaped(w_up.shape, b16),
            pltpu.HBM((width, trips), b16),
            shaped((members, piece_rows, CAP), b16),
        ),
        scratch_shapes=[
            pltpu.VMEM((edge_dev // BLOCK * width, BLOCK), b16),
            pltpu.VMEM((w_bil.shape[0], tile), b16),
            pltpu.VMEM((named_rows, tile), b16),
            pltpu.VMEM((named_rows, BLOCK), f32),
            pltpu.VMEM((members * atom_dev, model), b16),
            pltpu.VMEM((width, trips), b16),
            pltpu.SemaphoreType.DMA((trips // tile,)),
        ],
        compiler_params=params(),
        cost_estimate=cost(12 * w_bil.size * trips),
        name="backward_triplets",
    )(
        trip_count,
        slot,
        kept[0],
        kept[1],
        rank,
        back,
        kept[3],
        gathered,
        slope,
        grad_edge[0],
        kept[5],
        w_atom,
        *pairs[::-1],
    )
    feat_parts = lax.all_to_all(feat_parts, "graph", 0, 0, tiled=True)
    wide = math.gcd(trips, tile)
    wbil_term = pl.pallas_call(
        weight_kernel,
        in_specs=[VMEM, HBM, HBM],
        out_shape=shaped((width, w_bil.shape[0]), b16),
        scratch_shapes=[
            pltpu.VMEM((width, trips), b16),
            pltpu.VMEM((width, trips), b16),
            pltpu.VMEM((w_bil.shape[0], wide), b16),
            pltpu.VMEM((w_bil.shape[0], width), f32),
            pltpu.SemaphoreType.DMA((2, trips // wide)),
        ],
        compiler_params=params(),
        cost_estimate=cost(8 * w_bil.size * trips),
        name="bilinear_weights",
    )(kept[1], hbm(picked), hbm(mixed))
    flat_rows = width * (2 * model + w_bil.shape[0]) // CAP
    piece = shaped((members // 2, flat_rows // members, CAP), b16)
    grad_project, near, far = pl.pallas_call(
        edge_kernel,
        out_shape=(shaped((width, edge_dev), b16), piece, piece),
        scratch_shapes=[pltpu.VMEM((flat_rows, CAP), b16)],
        compiler_params=params(),
        cost_estimate=cost(64 * edge_rows.size * width),
        name="edges",
    )(feat_parts, projected, edge_rows, wbil_term, wup_term)
    grad_in = pl.pallas_call(
        input_kernel,
        out_shape=shaped(edge_rows.shape, f32),
        compiler_params=params(),
        cost_estimate=cost(64 * edge_rows.size * width),
        name="input_grads",
    )(grad_project, down_rows, grad_new)

    slab = pl.pallas_call(
        functools.partial(slab_kernel, members),
        out_shape=shaped((model // CAP, model // members, CAP), b16),
        scratch_shapes=[
            pltpu.VMEM((members * atom_dev, model), b16),
            pltpu.VMEM((members * atom_dev, model), b16),
            pltpu.VMEM((model, model), f32),
        ],
        compiler_params=params(),
        cost_estimate=cost(16 * members * atom_dev * w_atom.size),
        name="atom_slab",
    )(*pairs)
    batches = lax.axis_size("dp")
    factor = 1.0 / math.sqrt(batches * members * edge_dev)
    share_rows = (flat_rows + model * model // CAP) // members
    flat_sums = scatter_near(near, far, members)
    flat_sums, slab, grad_in = lax.optimization_barrier((flat_sums[::-1], slab, grad_in))
    flat_sums = flat_sums[::-1]
    share = pl.pallas_call(
        share_kernel,
        out_shape=shaped((share_rows, CAP), b16),
        compiler_params=params(),
        name="share",
    )(slab, *flat_sums[::-1])
    share = pl.pallas_call(
        functools.partial(total_kernel, factor),
        out_shape=shaped((share_rows, CAP), b16),
        compiler_params=params(),
        name="total",
    )(*[swap(share, batches, mask, "dp") for mask in range(batches - 1, 0, -1)], share)
    shares, _ = gather_near(share, members)
    grad_wdown, grad_wbil, grad_wup, grad_watom = pl.pallas_call(
        functools.partial(last_kernel, members),
        out_shape=(
            shaped((width, model), f32),
            shaped((width, w_bil.shape[0]), f32),
            shaped(w_up.shape, f32),
            shaped((model, model), f32),
        ),
        scratch_shapes=[pltpu.VMEM((flat_rows, CAP), b16)],
        compiler_params=params(),
        name="weights",
    )(*shares[::-1])
    return (
        edge_new[None],
        atom_new[None],
        grad_in[None],
        grad_wdown.T,
        grad_wbil.T,
        grad_wup,
        grad_watom,
    )


def solution(mesh):
    return jax.shard_map(
        body,
        mesh=mesh,
        in_specs=(
            P("dp", "graph", None),
            P("dp", "graph", None),
            P("dp", "graph"),
            P("dp", "graph"),
            P("dp", "graph"),
            P("dp", "graph"),
            P("dp", None, "graph"),
            P("dp", "graph", None),
            P("dp", "graph", None),
            P(),
            P(),
            P(),
            P(),
        ),
        out_specs=(
            P("dp", "graph", None),
            P("dp", "graph", None),
            P("dp", "graph", None),
            P(),
            P(),
            P(),
            P(),
        ),
        check_vma=False,
    )
```

```python
import functools
import math

import jax
import jax.numpy as jnp
from jax import lax
from jax.experimental import pallas as pl
from jax.experimental.pallas import tpu as pltpu
from jax.sharding import PartitionSpec as P

ATOM_SCALE = 0.25
BLOCK = 256
CAP = 128
TILE_LIMIT = 4096
FORWARD_LIMIT = 8192
INDEX_TILE = 2048
VMEM_BYTES = 32 * 1024 * 1024

FIRST_FIRST = (((0,), (0,)), ((), ()))
LAST_LAST = (((1,), (1,)), ((), ()))


def dot32(left, right, dims=(((1,), (0,)), ((), ()))):
    return lax.dot_general(left, right, dims, preferred_element_type=jnp.float32)


def silu(value):
    return value / (1.0 + jnp.exp(-value))


def silu_slope(value):
    logistic = 1.0 / (1.0 + jnp.exp(-value))
    return logistic * (1.0 + value * (1.0 - logistic))


def row_hot(rows, index):
    iota = lax.broadcasted_iota(jnp.int32, (rows, index.shape[1]), 0)
    if rows > BLOCK:
        return (iota == index).astype(jnp.float32).astype(jnp.bfloat16)
    match = iota.astype(jnp.bfloat16) == index.astype(jnp.bfloat16)
    return jnp.where(match, jnp.bfloat16(1), jnp.bfloat16(0))


def start_copies(pairs, sems):
    copies = [
        pltpu.make_async_copy(source, target, sems.at[place])
        for place, (source, target) in enumerate(pairs)
    ]
    for copy in copies:
        copy.start()
    return copies


def tile_copy(source, target, sems, step, tile):
    span = pl.ds(pl.multiple_of(step * tile, tile), tile)
    return pltpu.make_async_copy(source.at[:, span], target.at[:, span], sems.at[step])


def feature_kernel(emb_hbm, down_hbm, projected_ref, feat_ref, emb_ref, down_ref, sems):
    for copy in start_copies(((emb_hbm, emb_ref), (down_hbm, down_ref)), sems):
        copy.wait()
    projected = dot32(down_ref[...], emb_ref[...], LAST_LAST)
    projected_ref[...] = projected
    feat_ref[...] = silu(projected).astype(jnp.bfloat16)


def index_kernel(members, in_hbm, *refs):
    held = (len(refs) - 7) // 2
    staged, (slot_ref, rank_ref, back_ref) = refs[:held], refs[held : held + 3]
    kept = refs[held + 3 : -4]
    in_ref, hots, counts, sems = refs[-4:]
    copy, *copies = start_copies(((in_hbm, in_ref), *zip(staged, kept)), sems)
    trips = in_ref.shape[1]
    rows = rank_ref.shape[0]
    turn = lax.axis_index("graph") * (rows // members * CAP)
    tile = math.gcd(trips, INDEX_TILE)
    spans = [slice(at, at + tile) for at in range(0, trips, tile)]
    counts[...] = jnp.zeros_like(counts)
    copy.wait()
    for span in spans:
        incoming = in_ref[:, span] ^ turn
        hot = row_hot(CAP, incoming & (CAP - 1))
        hots[:, span] = hot
        counts[...] += dot32(row_hot(rows, incoming // CAP), hot, LAST_LAST)
    named = (counts[...] > 0.0).astype(jnp.float32)
    per = rows // members
    ahead = (
        lax.broadcasted_iota(jnp.int32, (CAP, CAP), 0)
        < lax.broadcasted_iota(jnp.int32, (CAP, CAP), 1)
    ).astype(jnp.bfloat16)
    row = lax.broadcasted_iota(jnp.int32, (rows, rows), 0)
    other = lax.broadcasted_iota(jnp.int32, (rows, rows), 1)
    above = ((other < row) & (other // per == row // per)).astype(jnp.bfloat16)
    sums = dot32(above, named.astype(jnp.bfloat16))
    before = jnp.sum(sums, axis=1, keepdims=True)
    rank = dot32(named.astype(jnp.bfloat16), ahead) + before
    rank = jnp.where(named > 0.0, rank, -1.0)
    rank_ref[...] = rank
    lookup = rank.astype(jnp.bfloat16)
    for span in spans:
        incoming = in_ref[:, span] ^ turn
        place = incoming // CAP
        found = dot32(lookup, hots[:, span])
        iota = lax.broadcasted_iota(jnp.int32, found.shape, 0)
        found = jnp.sum(jnp.where(iota == place, found, 0.0), axis=0, keepdims=True)
        slot_ref[:, span] = (place // per) * CAP + found.astype(jnp.int32)
    for copy in copies:
        copy.wait()
    bil_ref = kept[2]
    width = bil_ref.shape[0]
    turned = bil_ref[...].astype(jnp.float32).T
    back_ref[...] = jnp.concatenate(
        [turned[at : at + width] for at in range(0, turned.shape[0], width)], axis=1
    ).astype(jnp.bfloat16)


def rank_row(rank_ref, source, per):
    return jnp.concatenate(
        [rank_ref[source * per + part : source * per + part + 1, :] for part in range(per)], axis=1
    )


def rank_hot(row):
    iota = lax.broadcasted_iota(jnp.int32, (CAP, row.shape[1]), 0).astype(jnp.float32)
    return (iota == row).astype(jnp.float32).astype(jnp.bfloat16)


def forward_kernel(
    members,
    count_ref,
    slot_ref,
    rank_ref,
    *refs,
):
    out_ref, basis_ref, bil_ref, up_ref, emb_ref, target_ref, *refs = refs
    feat_refs, refs = refs[:members][::-1], refs[members:]
    new_ref, near_ref, far_ref, gathered_ref, picked_hbm, *refs = refs
    table, total, spread, masked, picked_ref, sems = refs
    trips = slot_ref.shape[1]
    tile = spread.shape[1]
    width = bil_ref.shape[0]
    edges = emb_ref.shape[0]
    groups = table.shape[0] // width
    per = BLOCK // width
    count = count_ref[0, 0]
    total[...] = jnp.zeros_like(total)
    for source in range(members):
        row = rank_row(rank_ref, source, edges // CAP)
        chosen = dot32(feat_refs[source][...], rank_hot(row), LAST_LAST)
        group, lane = divmod(source * CAP, BLOCK)
        table[group * width : (group + 1) * width, lane : lane + CAP] = chosen.astype(jnp.bfloat16)

    def one_tile(step, carry):
        span = pl.ds(pl.multiple_of(step * tile, tile), tile)
        slot = slot_ref[:, span]
        high = slot // BLOCK
        hot = row_hot(BLOCK, slot & (BLOCK - 1))
        feat = jnp.zeros((width, tile), jnp.float32)
        for chunk in range(groups // per):
            picked = dot32(table[chunk * BLOCK : (chunk + 1) * BLOCK, :], hot)
            for part in range(per):
                feat = jnp.where(
                    high == chunk * per + part, picked[part * width : (part + 1) * width, :], feat
                )
        feat = feat.astype(jnp.bfloat16)
        picked_ref[:, span] = feat
        tile_copy(picked_ref, picked_hbm, sems, step, tile).start()
        basis = basis_ref[:, span]
        for row in range(basis.shape[0]):
            spread[row * width : (row + 1) * width, :] = feat * basis[row : row + 1, :]
        place = step * tile + lax.broadcasted_iota(jnp.int32, (1, tile), 1)
        outgoing = out_ref[:, span]
        high = jnp.where(place < count, outgoing // BLOCK, -1)
        mixed = dot32(bil_ref[...], spread[...])
        for part in range(edges // BLOCK):
            masked[part * width : (part + 1) * width, :] = jnp.where(
                high == part, mixed, 0.0
            ).astype(jnp.bfloat16)
        total[...] += dot32(masked[...], row_hot(BLOCK, outgoing & (BLOCK - 1)), LAST_LAST)
        return carry

    lax.fori_loop(0, trips // tile, one_tile, 0)
    for step in range(trips // tile):
        tile_copy(picked_ref, picked_hbm, sems, step, tile).wait()
    gathered = jnp.concatenate(
        [total[at : at + width, :] for at in range(0, total.shape[0], width)], axis=1
    ).astype(jnp.bfloat16)
    gathered_ref[...] = gathered
    update = dot32(gathered, up_ref[...], FIRST_FIRST)
    fresh = (emb_ref[...].astype(jnp.float32) + silu(update)).astype(jnp.bfloat16)
    new_ref[...] = fresh
    held = near_ref.shape[1]
    turn = lax.axis_index("graph") * held
    sums = dot32(row_hot(members * held, target_ref[...] ^ turn), fresh)
    for pair in range(members // 2):
        near_ref[pair] = sums[2 * pair * held : (2 * pair + 1) * held].astype(jnp.bfloat16)
        far_ref[pair] = sums[(2 * pair + 1) * held : (2 * pair + 2) * held].astype(jnp.bfloat16)


def chip_kernel(near_ref, far_ref, *out_refs):
    for pair, out_ref in enumerate(out_refs):
        out_ref[...] = (
            near_ref[pair].astype(jnp.float32) + far_ref[pair].astype(jnp.float32)
        ).astype(jnp.bfloat16)


def atom_kernel(emb_ref, grad_ref, weight_ref, *refs):
    part_refs, (new_ref, pair_ref) = refs[:-2], refs[-2:]
    total = part_refs[0][...].astype(jnp.float32)
    for part_ref in part_refs[1:]:
        total = total + part_ref[...].astype(jnp.float32)
    total = total.astype(jnp.bfloat16)
    pre = ATOM_SCALE * dot32(total, weight_ref[...])
    new_ref[...] = (emb_ref[...].astype(jnp.float32) + silu(pre)).astype(jnp.bfloat16)
    grad_pre = (grad_ref[...].astype(jnp.float32) * silu_slope(pre)).astype(jnp.bfloat16)
    pair_ref[0] = total
    pair_ref[1] = grad_pre


def slope_kernel(gathered_ref, up_ref, slope_ref):
    slope_ref[...] = silu_slope(dot32(gathered_ref[...], up_ref[...], FIRST_FIRST))


def slab_kernel(members, *refs):
    pair_refs, (slab_ref, sums, grads, atom_grad) = refs[:members], refs[members:]
    me = lax.axis_index("graph")
    held, model = pair_refs[0].shape[1:]
    for source, pair_ref in enumerate(pair_refs):
        sums[source * held : (source + 1) * held, :] = pair_ref[0]
        grads[source * held : (source + 1) * held, :] = pair_ref[1]
    atom_grad[...] = ATOM_SCALE * dot32(sums[...], grads[...], FIRST_FIRST)
    share = model // members
    mine = atom_grad[pl.ds(pl.multiple_of(me * share, share), share), :]
    for column in range(0, model, CAP):
        slab_ref[column // CAP] = mine[:, column : column + CAP].astype(jnp.bfloat16)


def backward_kernel(
    members,
    count_ref,
    slot_ref,
    out_ref,
    basis_ref,
    rank_ref,
    back_ref,
    up_ref,
    gathered_ref,
    slope_ref,
    grad_edge_ref,
    target_ref,
    atom_weight_ref,
    *refs,
):
    pair_refs, refs = refs[:members][::-1], refs[members:]
    grad_new_ref, up_grad_ref, mixed_hbm, parts_ref, *refs = refs
    table, spread, masked, total, grads, mixed_ref, sems = refs
    trips = slot_ref.shape[1]
    tile = spread.shape[1]
    width = back_ref.shape[0]
    edges = grad_edge_ref.shape[0]
    groups = total.shape[0] // width
    count = count_ref[0, 0]
    me = lax.axis_index("graph")
    held = pair_refs[0].shape[1]
    for source, pair_ref in enumerate(pair_refs):
        grads[source * held : (source + 1) * held, :] = pair_ref[1]
    grad_sum = (ATOM_SCALE * dot32(grads[...], atom_weight_ref[...], LAST_LAST)).astype(
        jnp.bfloat16
    )
    total[...] = jnp.zeros_like(total)
    hot = row_hot(members * held, target_ref[...] ^ (me * held))
    grad_new = grad_edge_ref[...].astype(jnp.float32) + dot32(hot, grad_sum, FIRST_FIRST)
    grad_new_ref[...] = grad_new
    grad_update = (grad_new * slope_ref[...]).astype(jnp.bfloat16)
    up_grad_ref[...] = dot32(gathered_ref[...], grad_update).astype(jnp.bfloat16)
    grad_gathered = dot32(up_ref[...], grad_update, LAST_LAST).astype(jnp.bfloat16)
    for part in range(edges // BLOCK):
        table[part * width : (part + 1) * width, :] = grad_gathered[
            :, part * BLOCK : (part + 1) * BLOCK
        ]

    def one_tile(step, carry):
        span = pl.ds(pl.multiple_of(step * tile, tile), tile)
        place = step * tile + lax.broadcasted_iota(jnp.int32, (1, tile), 1)
        outgoing = jnp.where(place < count, out_ref[:, span], -1)
        picked = dot32(table[...], row_hot(BLOCK, outgoing & (BLOCK - 1)))
        high = jnp.where(outgoing >= 0, outgoing // BLOCK, -1)
        grad = jnp.zeros((width, tile), jnp.float32)
        for part in range(edges // BLOCK):
            grad = jnp.where(high == part, picked[part * width : (part + 1) * width, :], grad)
        grad = grad.astype(jnp.bfloat16)
        mixed_ref[:, span] = grad
        tile_copy(mixed_ref, mixed_hbm, sems, step, tile).start()
        basis = basis_ref[:, span]
        for row in range(basis.shape[0]):
            spread[row * width : (row + 1) * width, :] = grad * basis[row : row + 1, :]
        feat_grad = dot32(back_ref[...], spread[...])
        slot = slot_ref[:, span]
        high_in = slot // BLOCK
        for part in range(groups):
            masked[part * width : (part + 1) * width, :] = jnp.where(
                high_in == part, feat_grad, 0.0
            ).astype(jnp.bfloat16)
        total[...] += dot32(masked[...], row_hot(BLOCK, slot & (BLOCK - 1)), LAST_LAST)
        return carry

    lax.fori_loop(0, trips // tile, one_tile, 0)
    for step in range(trips // tile):
        tile_copy(mixed_ref, mixed_hbm, sems, step, tile).wait()
    per = rank_ref.shape[0] // members
    for source in range(members):
        group, lane = divmod(source * CAP, BLOCK)
        piece = total[group * width : (group + 1) * width, lane : lane + CAP]
        ranks = rank_ref[source * per : (source + 1) * per, :]
        spare = jnp.zeros((parts_ref.shape[1] - width - per, CAP), jnp.float32)
        parts_ref[me ^ source] = jnp.concatenate([piece, ranks, spare], axis=0).astype(jnp.bfloat16)


def weight_kernel(
    basis_ref, picked_hbm, mixed_hbm, out_ref, picked, mixed, spread, scaled, total, sems
):
    width, trips = picked.shape
    tile = spread.shape[1]
    steps = trips // tile
    moved = scaled.shape[0] // width - 1
    for step in range(steps):
        tile_copy(picked_hbm, picked, sems.at[0], step, tile).start()
        tile_copy(mixed_hbm, mixed, sems.at[1], step, tile).start()
    total[...] = jnp.zeros_like(total)

    def one_tile(step, carry):
        span = pl.ds(pl.multiple_of(step * tile, tile), tile)
        basis = basis_ref[:, span]
        tile_copy(picked_hbm, picked, sems.at[0], step, tile).wait()
        tile_copy(mixed_hbm, mixed, sems.at[1], step, tile).wait()
        feat = picked[:, span]
        spread[:width, :] = feat
        for row in range(moved, basis.shape[0]):
            at = (row - moved + 1) * width
            spread[at : at + width, :] = feat * basis[row : row + 1, :]
        grad = mixed[:, span]
        scaled[:width, :] = grad
        for row in range(moved):
            at = (row + 1) * width
            scaled[at : at + width, :] = grad * basis[row : row + 1, :]
        total[...] += dot32(spread[...], scaled[...], LAST_LAST)
        return carry

    lax.fori_loop(0, steps, one_tile, 0)
    first = [total[:width, (row + 1) * width : (row + 2) * width] for row in range(moved)]
    whole = jnp.concatenate([*first, total[width:, :width]], axis=0)
    out_ref[...] = whole.T.astype(jnp.bfloat16)


def input_kernel(grad_project_ref, down_ref, grad_new_ref, grad_in_ref):
    grad_in_ref[...] = grad_new_ref[...] + dot32(
        grad_project_ref[...], down_ref[...], FIRST_FIRST
    )


def edge_kernel(
    parts_ref,
    projected_ref,
    emb_ref,
    bil_grad_ref,
    up_grad_ref,
    grad_project_ref,
    near_ref,
    far_ref,
    flat,
):
    members = parts_ref.shape[0]
    width, edges = projected_ref.shape
    per = edges // CAP
    grad_feat = jnp.zeros((width, edges), jnp.float32)
    for source in range(members):
        part = parts_ref[source].astype(jnp.float32)
        row = jnp.concatenate([part[width + at : width + at + 1] for at in range(per)], axis=1)
        grad_feat = grad_feat + dot32(part[:width].astype(jnp.bfloat16), rank_hot(row))
    grad_project = (grad_feat * silu_slope(projected_ref[...])).astype(jnp.bfloat16)
    grad_project_ref[...] = grad_project
    down_grad = dot32(grad_project, emb_ref[...]).astype(jnp.bfloat16)
    at = 0
    for term in (down_grad, bil_grad_ref[...], up_grad_ref[...]):
        for column in range(0, term.shape[1], CAP):
            flat[at : at + width, :] = term[:, column : column + CAP]
            at += width
    me = lax.axis_index("graph")
    rows = near_ref.shape[1]
    for pair in range(members // 2):
        near_ref[pair] = flat[pl.ds(pl.multiple_of((me ^ (2 * pair)) * rows, rows), rows), :]
        far_ref[pair] = flat[pl.ds(pl.multiple_of((me ^ (2 * pair + 1)) * rows, rows), rows), :]


def share_kernel(slab_ref, *refs):
    part_refs, out_ref = refs[:-1], refs[-1]
    total = part_refs[0][...].astype(jnp.float32)
    for part_ref in part_refs[1:]:
        total = total + part_ref[...].astype(jnp.float32)
    rows = total.shape[0]
    out_ref[:rows, :] = total.astype(jnp.bfloat16)
    slab = slab_ref[...]
    out_ref[rows:, :] = slab.reshape(slab.shape[0] * slab.shape[1], CAP)


def total_kernel(factor, *refs):
    parts = [part_ref[...].astype(jnp.float32) for part_ref in refs[:-1]]
    while len(parts) > 1:
        parts = [left + right for left, right in zip(parts[::2], parts[1::2])]
    refs[-1][...] = (parts[0] * factor).astype(jnp.bfloat16)


def last_kernel(members, *refs):
    part_refs, (down_ref, bil_ref, up_ref, atom_ref, flat) = refs[:members][::-1], refs[members:]
    me = lax.axis_index("graph")
    model = atom_ref.shape[1]
    rows = flat.shape[0] // members
    held = model // members
    for place, part_ref in enumerate(part_refs):
        source = me ^ place
        flat[pl.ds(pl.multiple_of(source * rows, rows), rows), :] = part_ref[:rows, :]
        for block in range(model // CAP):
            first = rows + block * held
            atom_ref[
                pl.ds(pl.multiple_of(source * held, held), held), block * CAP : (block + 1) * CAP
            ] = part_ref[first : first + held, :].astype(jnp.float32)
    at = 0
    for out in (down_ref, bil_ref, up_ref):
        width = out.shape[0]
        for column in range(0, out.shape[1], CAP):
            out[:, column : column + CAP] = flat[at : at + width, :].astype(jnp.float32)
            at += width


HBM = pl.BlockSpec(memory_space=pltpu.HBM)
VMEM = pl.BlockSpec(memory_space=pltpu.VMEM)
SMEM = pl.BlockSpec(memory_space=pltpu.SMEM)


def hbm(value):
    return pltpu.with_memory_space_constraint(value, pltpu.HBM)


def swap(value, members, mask, axis="graph"):
    return lax.ppermute(value, axis, [(at, at ^ mask) for at in range(members)])


def scatter_near(near, far, members):
    shape = jax.ShapeDtypeStruct(near.shape[1:], near.dtype)
    sums = pl.pallas_call(
        chip_kernel,
        out_shape=[shape] * (members // 2),
        compiler_params=params(),
        name="chip_sums",
    )(near, swap(far, members, 1))
    return [sums[0]] + [swap(part, members, 2 * at) for at, part in enumerate(sums) if at > 0]


def gather_near(value, members, beside=None):
    even = [value] + [swap(value, members, mask) for mask in range(2, members, 2)]
    if beside is not None:
        back_even, beside = lax.optimization_barrier((even[::-1], beside))
        even = back_even[::-1]
    odd = [swap(piece, members, 1) for piece in even]
    return [piece for pair in zip(even, odd) for piece in pair], beside


def params(limit=VMEM_BYTES):
    return pltpu.CompilerParams(vmem_limit_bytes=limit)


def cost(flops):
    return pl.CostEstimate(flops=flops, bytes_accessed=1 << 20, transcendentals=0)


def body(
    edge_emb,
    atom_emb,
    edge_target,
    trip_in,
    trip_out,
    trip_count,
    trip_basis,
    grad_edge,
    grad_atom,
    w_down,
    w_bil,
    w_up,
    w_atom,
):
    members = lax.axis_size("graph")
    edge_rows = edge_emb[0]
    edge_dev, model = edge_rows.shape
    atom_dev = atom_emb.shape[1]
    trips = trip_in.shape[1]
    width = w_down.shape[1]
    tile = math.gcd(trips, TILE_LIMIT)
    long = math.gcd(trips, FORWARD_LIMIT)
    f32, b16 = jnp.float32, jnp.bfloat16
    shaped = jax.ShapeDtypeStruct

    down_rows = w_down.T
    bil_rows = w_bil.T
    basis = trip_basis[0]
    projected, feat = pl.pallas_call(
        feature_kernel,
        in_specs=[HBM] * 2,
        out_shape=(
            shaped((width, edge_dev), f32),
            shaped((width, edge_dev), b16),
        ),
        scratch_shapes=[
            pltpu.VMEM(edge_rows.shape, b16),
            pltpu.VMEM(down_rows.shape, b16),
            pltpu.SemaphoreType.DMA((2,)),
        ],
        compiler_params=params(),
        cost_estimate=cost(16 * edge_rows.size * width),
        name="features",
    )(hbm(edge_rows), hbm(down_rows))
    rank_rows = members * edge_dev // CAP
    staged = (trip_out, basis, bil_rows, w_up, edge_rows, edge_target)
    slot, rank, back, *kept = pl.pallas_call(
        functools.partial(index_kernel, members),
        in_specs=[HBM] * (1 + len(staged)),
        out_shape=(
            shaped(trip_in.shape, jnp.int32),
            shaped((rank_rows, CAP), f32),
            shaped(bil_rows.shape, b16),
            *[shaped(value.shape, value.dtype) for value in staged],
        ),
        scratch_shapes=[
            pltpu.VMEM(trip_in.shape, jnp.int32),
            pltpu.VMEM((CAP, trips), b16),
            pltpu.VMEM((rank_rows, CAP), f32),
            pltpu.SemaphoreType.DMA((1 + len(staged),)),
        ],
        compiler_params=params(),
        cost_estimate=cost(8 * CAP * CAP * trips),
        name="slots",
    )(*[hbm(value) for value in (trip_in, *staged)])
    feats, (slot, rank, back, *kept) = gather_near(feat, members, (slot, rank, back, *kept))

    named_rows = members * CAP // BLOCK * width
    half = shaped((members // 2, atom_dev, model), b16)
    edge_new, near, far, gathered, picked = pl.pallas_call(
        functools.partial(forward_kernel, members),
        in_specs=[SMEM] + [VMEM] * (2 + len(kept) + members),
        out_specs=(VMEM, VMEM, VMEM, VMEM, HBM),
        out_shape=(
            shaped(edge_rows.shape, b16),
            half,
            half,
            shaped((width, edge_dev), b16),
            pltpu.HBM((width, trips), b16),
        ),
        scratch_shapes=[
            pltpu.VMEM((named_rows, BLOCK), b16),
            pltpu.VMEM((edge_dev // BLOCK * width, BLOCK), f32),
            pltpu.VMEM((w_bil.shape[0], long), b16),
            pltpu.VMEM((edge_dev // BLOCK * width, long), b16),
            pltpu.VMEM((width, trips), b16),
            pltpu.SemaphoreType.DMA((trips // long,)),
        ],
        compiler_params=params(),
        cost_estimate=cost(12 * w_bil.size * trips),
        name="forward_triplets",
    )(
        trip_count,
        slot,
        rank,
        *kept,
        *feats[::-1],
    )

    atom_block = shaped((atom_dev, model), b16)
    slope = pl.pallas_call(
        slope_kernel,
        out_shape=shaped(edge_rows.shape, f32),
        compiler_params=params(),
        cost_estimate=cost(64 * edge_rows.size * width),
        name="slopes",
    )(gathered, kept[3])
    sums = scatter_near(near, far, members)
    sums, slope = lax.optimization_barrier((sums[::-1], slope))
    sums = sums[::-1]
    atom_new, pair = pl.pallas_call(
        atom_kernel,
        out_shape=(atom_block, shaped((2, atom_dev, model), b16)),
        compiler_params=params(),
        cost_estimate=cost(16 * atom_dev * w_atom.size),
        name="atoms",
    )(atom_emb[0], grad_atom[0], w_atom, *sums[::-1])
    pairs, _ = gather_near(pair, members)

    piece_rows = width + -(-(edge_dev // CAP) // 16) * 16
    grad_new, wup_term, mixed, feat_parts = pl.pallas_call(
        functools.partial(backward_kernel, members),
        in_specs=[SMEM] + [VMEM] * (11 + members),
        out_specs=(VMEM, VMEM, HBM, VMEM),
        out_shape=(
            shaped(edge_rows.shape, f32),
            shaped(w_up.shape, b16),
            pltpu.HBM((width, trips), b16),
            shaped((members, piece_rows, CAP), b16),
        ),
        scratch_shapes=[
            pltpu.VMEM((edge_dev // BLOCK * width, BLOCK), b16),
            pltpu.VMEM((w_bil.shape[0], tile), b16),
            pltpu.VMEM((named_rows, tile), b16),
            pltpu.VMEM((named_rows, BLOCK), f32),
            pltpu.VMEM((members * atom_dev, model), b16),
            pltpu.VMEM((width, trips), b16),
            pltpu.SemaphoreType.DMA((trips // tile,)),
        ],
        compiler_params=params(),
        cost_estimate=cost(12 * w_bil.size * trips),
        name="backward_triplets",
    )(
        trip_count,
        slot,
        kept[0],
        kept[1],
        rank,
        back,
        kept[3],
        gathered,
        slope,
        grad_edge[0],
        kept[5],
        w_atom,
        *pairs[::-1],
    )
    feat_parts = lax.all_to_all(feat_parts, "graph", 0, 0, tiled=True)
    wide = math.gcd(trips, 2 * tile)
    wbil_term = pl.pallas_call(
        weight_kernel,
        in_specs=[VMEM, HBM, HBM],
        out_shape=shaped((width, w_bil.shape[0]), b16),
        scratch_shapes=[
            pltpu.VMEM((width, trips), b16),
            pltpu.VMEM((width, trips), b16),
            pltpu.VMEM((w_bil.shape[0] + 2 * width - BLOCK, wide), b16),
            pltpu.VMEM((BLOCK, wide), b16),
            pltpu.VMEM((w_bil.shape[0] + 2 * width - BLOCK, BLOCK), f32),
            pltpu.SemaphoreType.DMA((2, trips // wide)),
        ],
        compiler_params=params(),
        cost_estimate=cost(8 * w_bil.size * trips),
        name="bilinear_weights",
    )(kept[1], hbm(picked), hbm(mixed))
    flat_rows = width * (2 * model + w_bil.shape[0]) // CAP
    piece = shaped((members // 2, flat_rows // members, CAP), b16)
    grad_project, near, far = pl.pallas_call(
        edge_kernel,
        out_shape=(shaped((width, edge_dev), b16), piece, piece),
        scratch_shapes=[pltpu.VMEM((flat_rows, CAP), b16)],
        compiler_params=params(),
        cost_estimate=cost(64 * edge_rows.size * width),
        name="edges",
    )(feat_parts, projected, edge_rows, wbil_term, wup_term)
    grad_in = pl.pallas_call(
        input_kernel,
        out_shape=shaped(edge_rows.shape, f32),
        compiler_params=params(),
        cost_estimate=cost(64 * edge_rows.size * width),
        name="input_grads",
    )(grad_project, down_rows, grad_new)

    slab = pl.pallas_call(
        functools.partial(slab_kernel, members),
        out_shape=shaped((model // CAP, model // members, CAP), b16),
        scratch_shapes=[
            pltpu.VMEM((members * atom_dev, model), b16),
            pltpu.VMEM((members * atom_dev, model), b16),
            pltpu.VMEM((model, model), f32),
        ],
        compiler_params=params(),
        cost_estimate=cost(16 * members * atom_dev * w_atom.size),
        name="atom_slab",
    )(*pairs)
    batches = lax.axis_size("dp")
    factor = 1.0 / math.sqrt(batches * members * edge_dev)
    share_rows = (flat_rows + model * model // CAP) // members
    flat_sums = scatter_near(near, far, members)
    flat_sums, slab, grad_in = lax.optimization_barrier((flat_sums[::-1], slab, grad_in))
    flat_sums = flat_sums[::-1]
    share = pl.pallas_call(
        share_kernel,
        out_shape=shaped((share_rows, CAP), b16),
        compiler_params=params(),
        name="share",
    )(slab, *flat_sums[::-1])
    share = pl.pallas_call(
        functools.partial(total_kernel, factor),
        out_shape=shaped((share_rows, CAP), b16),
        compiler_params=params(),
        name="total",
    )(*[swap(share, batches, mask, "dp") for mask in range(batches - 1, 0, -1)], share)
    shares, _ = gather_near(share, members)
    grad_wdown, grad_wbil, grad_wup, grad_watom = pl.pallas_call(
        functools.partial(last_kernel, members),
        out_shape=(
            shaped((width, model), f32),
            shaped((width, w_bil.shape[0]), f32),
            shaped(w_up.shape, f32),
            shaped((model, model), f32),
        ),
        scratch_shapes=[pltpu.VMEM((flat_rows, CAP), b16)],
        compiler_params=params(),
        name="weights",
    )(*shares[::-1])
    return (
        edge_new[None],
        atom_new[None],
        grad_in[None],
        grad_wdown.T,
        grad_wbil.T,
        grad_wup,
        grad_watom,
    )


def solution(mesh):
    return jax.shard_map(
        body,
        mesh=mesh,
        in_specs=(
            P("dp", "graph", None),
            P("dp", "graph", None),
            P("dp", "graph"),
            P("dp", "graph"),
            P("dp", "graph"),
            P("dp", "graph"),
            P("dp", None, "graph"),
            P("dp", "graph", None),
            P("dp", "graph", None),
            P(),
            P(),
            P(),
            P(),
        ),
        out_specs=(
            P("dp", "graph", None),
            P("dp", "graph", None),
            P("dp", "graph", None),
            P(),
            P(),
            P(),
            P(),
        ),
        check_vma=False,
    )
```

```python
import functools
import math

import jax
import jax.numpy as jnp
from jax import lax
from jax.experimental import pallas as pl
from jax.experimental.pallas import tpu as pltpu
from jax.sharding import PartitionSpec as P

ATOM_SCALE = 0.25
BLOCK = 256
CAP = 128
TILE_LIMIT = 4096
FORWARD_LIMIT = 8192
INDEX_TILE = 2048
VMEM_BYTES = 32 * 1024 * 1024

FIRST_FIRST = (((0,), (0,)), ((), ()))
LAST_LAST = (((1,), (1,)), ((), ()))


def dot32(left, right, dims=(((1,), (0,)), ((), ()))):
    return lax.dot_general(left, right, dims, preferred_element_type=jnp.float32)


def silu(value):
    return value / (1.0 + jnp.exp(-value))


def silu_slope(value):
    logistic = 1.0 / (1.0 + jnp.exp(-value))
    return logistic * (1.0 + value * (1.0 - logistic))


def row_hot(rows, index):
    iota = lax.broadcasted_iota(jnp.int32, (rows, index.shape[1]), 0)
    if rows > BLOCK:
        return (iota == index).astype(jnp.float32).astype(jnp.bfloat16)
    match = iota.astype(jnp.bfloat16) == index.astype(jnp.bfloat16)
    return jnp.where(match, jnp.bfloat16(1), jnp.bfloat16(0))


def start_copies(pairs, sems):
    copies = [
        pltpu.make_async_copy(source, target, sems.at[place])
        for place, (source, target) in enumerate(pairs)
    ]
    for copy in copies:
        copy.start()
    return copies


def tile_copy(source, target, sems, step, tile):
    span = pl.ds(pl.multiple_of(step * tile, tile), tile)
    return pltpu.make_async_copy(source.at[:, span], target.at[:, span], sems.at[step])


def feature_kernel(emb_hbm, down_hbm, projected_ref, feat_ref, emb_ref, down_ref, sems):
    for copy in start_copies(((emb_hbm, emb_ref), (down_hbm, down_ref)), sems):
        copy.wait()
    projected = dot32(down_ref[...], emb_ref[...], LAST_LAST)
    projected_ref[...] = projected
    feat_ref[...] = silu(projected).astype(jnp.bfloat16)


def index_kernel(members, in_hbm, *refs):
    held = (len(refs) - 7) // 2
    staged, (slot_ref, rank_ref, back_ref) = refs[:held], refs[held : held + 3]
    kept = refs[held + 3 : -4]
    in_ref, hots, counts, sems = refs[-4:]
    copy, *copies = start_copies(((in_hbm, in_ref), *zip(staged, kept)), sems)
    trips = in_ref.shape[1]
    rows = rank_ref.shape[0]
    turn = lax.axis_index("graph") * (rows // members * CAP)
    tile = math.gcd(trips, INDEX_TILE)
    spans = [slice(at, at + tile) for at in range(0, trips, tile)]
    counts[...] = jnp.zeros_like(counts)
    copy.wait()
    for span in spans:
        incoming = in_ref[:, span] ^ turn
        hot = row_hot(CAP, incoming & (CAP - 1))
        hots[:, span] = hot
        counts[...] += dot32(row_hot(rows, incoming // CAP), hot, LAST_LAST)
    named = (counts[...] > 0.0).astype(jnp.float32)
    per = rows // members
    ahead = (
        lax.broadcasted_iota(jnp.int32, (CAP, CAP), 0)
        < lax.broadcasted_iota(jnp.int32, (CAP, CAP), 1)
    ).astype(jnp.bfloat16)
    row = lax.broadcasted_iota(jnp.int32, (rows, rows), 0)
    other = lax.broadcasted_iota(jnp.int32, (rows, rows), 1)
    above = ((other < row) & (other // per == row // per)).astype(jnp.bfloat16)
    sums = dot32(above, named.astype(jnp.bfloat16))
    before = jnp.sum(sums, axis=1, keepdims=True)
    rank = dot32(named.astype(jnp.bfloat16), ahead) + before
    rank = jnp.where(named > 0.0, rank, -1.0)
    rank_ref[...] = rank
    lookup = rank.astype(jnp.bfloat16)
    for span in spans:
        incoming = in_ref[:, span] ^ turn
        place = incoming // CAP
        found = dot32(lookup, hots[:, span])
        iota = lax.broadcasted_iota(jnp.int32, found.shape, 0)
        found = jnp.sum(jnp.where(iota == place, found, 0.0), axis=0, keepdims=True)
        slot_ref[:, span] = (place // per) * CAP + found.astype(jnp.int32)
    for copy in copies:
        copy.wait()
    bil_ref = kept[2]
    width = bil_ref.shape[0]
    turned = bil_ref[...].astype(jnp.float32).T
    back_ref[...] = jnp.concatenate(
        [turned[at : at + width] for at in range(0, turned.shape[0], width)], axis=1
    ).astype(jnp.bfloat16)


def rank_row(rank_ref, source, per):
    return jnp.concatenate(
        [rank_ref[source * per + part : source * per + part + 1, :] for part in range(per)], axis=1
    )


def rank_hot(row):
    iota = lax.broadcasted_iota(jnp.int32, (CAP, row.shape[1]), 0).astype(jnp.float32)
    return (iota == row).astype(jnp.float32).astype(jnp.bfloat16)


def forward_kernel(
    members,
    count_ref,
    slot_ref,
    rank_ref,
    *refs,
):
    out_ref, basis_ref, bil_ref, up_ref, emb_ref, target_ref, *refs = refs
    feat_refs, refs = restored(refs[:members]), refs[members:]
    new_ref, near_ref, far_ref, gathered_ref, picked_hbm, *refs = refs
    table, total, spread, masked, picked_ref, sems = refs
    trips = slot_ref.shape[1]
    tile = spread.shape[1]
    width = bil_ref.shape[0]
    edges = emb_ref.shape[0]
    groups = table.shape[0] // width
    per = BLOCK // width
    count = count_ref[0, 0]
    total[...] = jnp.zeros_like(total)
    for source in range(members):
        row = rank_row(rank_ref, source, edges // CAP)
        chosen = dot32(feat_refs[source][...], rank_hot(row), LAST_LAST)
        group, lane = divmod(source * CAP, BLOCK)
        table[group * width : (group + 1) * width, lane : lane + CAP] = chosen.astype(jnp.bfloat16)

    def one_tile(step, carry):
        span = pl.ds(pl.multiple_of(step * tile, tile), tile)
        slot = slot_ref[:, span]
        high = slot // BLOCK
        hot = row_hot(BLOCK, slot & (BLOCK - 1))
        feat = jnp.zeros((width, tile), jnp.float32)
        for chunk in range(groups // per):
            picked = dot32(table[chunk * BLOCK : (chunk + 1) * BLOCK, :], hot)
            for part in range(per):
                feat = jnp.where(
                    high == chunk * per + part, picked[part * width : (part + 1) * width, :], feat
                )
        feat = feat.astype(jnp.bfloat16)
        picked_ref[:, span] = feat
        tile_copy(picked_ref, picked_hbm, sems, step, tile).start()
        basis = basis_ref[:, span]
        for row in range(basis.shape[0]):
            spread[row * width : (row + 1) * width, :] = feat * basis[row : row + 1, :]
        place = step * tile + lax.broadcasted_iota(jnp.int32, (1, tile), 1)
        outgoing = out_ref[:, span]
        high = jnp.where(place < count, outgoing // BLOCK, -1)
        mixed = dot32(bil_ref[...], spread[...])
        for part in range(edges // BLOCK):
            masked[part * width : (part + 1) * width, :] = jnp.where(
                high == part, mixed, 0.0
            ).astype(jnp.bfloat16)
        total[...] += dot32(masked[...], row_hot(BLOCK, outgoing & (BLOCK - 1)), LAST_LAST)
        return carry

    lax.fori_loop(0, trips // tile, one_tile, 0)
    for step in range(trips // tile):
        tile_copy(picked_ref, picked_hbm, sems, step, tile).wait()
    gathered = jnp.concatenate(
        [total[at : at + width, :] for at in range(0, total.shape[0], width)], axis=1
    ).astype(jnp.bfloat16)
    gathered_ref[...] = gathered
    update = dot32(gathered, up_ref[...], FIRST_FIRST)
    fresh = (emb_ref[...].astype(jnp.float32) + silu(update)).astype(jnp.bfloat16)
    new_ref[...] = fresh
    held = near_ref.shape[1]
    turn = lax.axis_index("graph") * held
    sums = dot32(row_hot(members * held, target_ref[...] ^ turn), fresh)
    for pair in range(members // 2):
        near_ref[pair] = sums[2 * pair * held : (2 * pair + 1) * held].astype(jnp.bfloat16)
        far_ref[pair] = sums[(2 * pair + 1) * held : (2 * pair + 2) * held].astype(jnp.bfloat16)


def chip_kernel(near_ref, far_ref, *out_refs):
    for pair, out_ref in enumerate(out_refs):
        out_ref[...] = (
            near_ref[pair].astype(jnp.float32) + far_ref[pair].astype(jnp.float32)
        ).astype(jnp.bfloat16)


def atom_kernel(emb_ref, grad_ref, weight_ref, *refs):
    part_refs, (new_ref, pair_ref) = refs[:-2], refs[-2:]
    total = part_refs[0][...].astype(jnp.float32)
    for part_ref in part_refs[1:]:
        total = total + part_ref[...].astype(jnp.float32)
    total = total.astype(jnp.bfloat16)
    pre = ATOM_SCALE * dot32(total, weight_ref[...])
    new_ref[...] = (emb_ref[...].astype(jnp.float32) + silu(pre)).astype(jnp.bfloat16)
    grad_pre = (grad_ref[...].astype(jnp.float32) * silu_slope(pre)).astype(jnp.bfloat16)
    pair_ref[0] = total
    pair_ref[1] = grad_pre


def slope_kernel(gathered_ref, up_ref, slope_ref):
    slope_ref[...] = silu_slope(dot32(gathered_ref[...], up_ref[...], FIRST_FIRST))


def slab_kernel(members, *refs):
    pair_refs, (slab_ref, sums, grads, atom_grad) = refs[:members], refs[members:]
    me = lax.axis_index("graph")
    held, model = pair_refs[0].shape[1:]
    for source, pair_ref in enumerate(pair_refs):
        sums[source * held : (source + 1) * held, :] = pair_ref[0]
        grads[source * held : (source + 1) * held, :] = pair_ref[1]
    atom_grad[...] = ATOM_SCALE * dot32(sums[...], grads[...], FIRST_FIRST)
    share = model // members
    mine = atom_grad[pl.ds(pl.multiple_of(me * share, share), share), :]
    for column in range(0, model, CAP):
        slab_ref[column // CAP] = mine[:, column : column + CAP].astype(jnp.bfloat16)


def backward_kernel(
    members,
    count_ref,
    slot_ref,
    out_ref,
    basis_ref,
    rank_ref,
    back_ref,
    up_ref,
    gathered_ref,
    slope_ref,
    grad_edge_ref,
    target_ref,
    atom_weight_ref,
    *refs,
):
    pair_refs, refs = restored(refs[:members]), refs[members:]
    grad_new_ref, up_grad_ref, mixed_hbm, parts_ref, *refs = refs
    table, spread, masked, total, grads, mixed_ref, sems = refs
    trips = slot_ref.shape[1]
    tile = spread.shape[1]
    width = back_ref.shape[0]
    edges = grad_edge_ref.shape[0]
    groups = total.shape[0] // width
    count = count_ref[0, 0]
    me = lax.axis_index("graph")
    held = pair_refs[0].shape[1]
    for source, pair_ref in enumerate(pair_refs):
        grads[source * held : (source + 1) * held, :] = pair_ref[1]
    grad_sum = (ATOM_SCALE * dot32(grads[...], atom_weight_ref[...], LAST_LAST)).astype(
        jnp.bfloat16
    )
    total[...] = jnp.zeros_like(total)
    hot = row_hot(members * held, target_ref[...] ^ (me * held))
    grad_new = grad_edge_ref[...].astype(jnp.float32) + dot32(hot, grad_sum, FIRST_FIRST)
    grad_new_ref[...] = grad_new
    grad_update = (grad_new * slope_ref[...]).astype(jnp.bfloat16)
    up_grad_ref[...] = dot32(gathered_ref[...], grad_update).astype(jnp.bfloat16)
    grad_gathered = dot32(up_ref[...], grad_update, LAST_LAST).astype(jnp.bfloat16)
    for part in range(edges // BLOCK):
        table[part * width : (part + 1) * width, :] = grad_gathered[
            :, part * BLOCK : (part + 1) * BLOCK
        ]

    def one_tile(step, carry):
        span = pl.ds(pl.multiple_of(step * tile, tile), tile)
        place = step * tile + lax.broadcasted_iota(jnp.int32, (1, tile), 1)
        outgoing = jnp.where(place < count, out_ref[:, span], -1)
        picked = dot32(table[...], row_hot(BLOCK, outgoing & (BLOCK - 1)))
        high = jnp.where(outgoing >= 0, outgoing // BLOCK, -1)
        grad = jnp.zeros((width, tile), jnp.float32)
        for part in range(edges // BLOCK):
            grad = jnp.where(high == part, picked[part * width : (part + 1) * width, :], grad)
        grad = grad.astype(jnp.bfloat16)
        mixed_ref[:, span] = grad
        tile_copy(mixed_ref, mixed_hbm, sems, step, tile).start()
        basis = basis_ref[:, span]
        for row in range(basis.shape[0]):
            spread[row * width : (row + 1) * width, :] = grad * basis[row : row + 1, :]
        feat_grad = dot32(back_ref[...], spread[...])
        slot = slot_ref[:, span]
        high_in = slot // BLOCK
        for part in range(groups):
            masked[part * width : (part + 1) * width, :] = jnp.where(
                high_in == part, feat_grad, 0.0
            ).astype(jnp.bfloat16)
        total[...] += dot32(masked[...], row_hot(BLOCK, slot & (BLOCK - 1)), LAST_LAST)
        return carry

    lax.fori_loop(0, trips // tile, one_tile, 0)
    for step in range(trips // tile):
        tile_copy(mixed_ref, mixed_hbm, sems, step, tile).wait()
    per = rank_ref.shape[0] // members
    for source in range(members):
        group, lane = divmod(source * CAP, BLOCK)
        piece = total[group * width : (group + 1) * width, lane : lane + CAP]
        ranks = rank_ref[source * per : (source + 1) * per, :]
        spare = jnp.zeros((parts_ref.shape[1] - width - per, CAP), jnp.float32)
        parts_ref[me ^ source] = jnp.concatenate([piece, ranks, spare], axis=0).astype(jnp.bfloat16)


def weight_kernel(
    basis_ref, picked_hbm, mixed_hbm, out_ref, picked, mixed, spread, scaled, total, sems
):
    width, trips = picked.shape
    tile = spread.shape[1]
    steps = trips // tile
    moved = scaled.shape[0] // width - 1
    for step in range(steps):
        tile_copy(picked_hbm, picked, sems.at[0], step, tile).start()
        tile_copy(mixed_hbm, mixed, sems.at[1], step, tile).start()
    total[...] = jnp.zeros_like(total)

    def one_tile(step, carry):
        span = pl.ds(pl.multiple_of(step * tile, tile), tile)
        basis = basis_ref[:, span]
        tile_copy(picked_hbm, picked, sems.at[0], step, tile).wait()
        tile_copy(mixed_hbm, mixed, sems.at[1], step, tile).wait()
        feat = picked[:, span]
        spread[:width, :] = feat
        for row in range(moved, basis.shape[0]):
            at = (row - moved + 1) * width
            spread[at : at + width, :] = feat * basis[row : row + 1, :]
        grad = mixed[:, span]
        scaled[:width, :] = grad
        for row in range(moved):
            at = (row + 1) * width
            scaled[at : at + width, :] = grad * basis[row : row + 1, :]
        total[...] += dot32(spread[...], scaled[...], LAST_LAST)
        return carry

    lax.fori_loop(0, steps, one_tile, 0)
    first = [total[:width, (row + 1) * width : (row + 2) * width] for row in range(moved)]
    whole = jnp.concatenate([*first, total[width:, :width]], axis=0)
    out_ref[...] = whole.T.astype(jnp.bfloat16)


def input_kernel(grad_project_ref, down_ref, grad_new_ref, grad_in_ref):
    grad_in_ref[...] = grad_new_ref[...] + dot32(
        grad_project_ref[...], down_ref[...], FIRST_FIRST
    )


def edge_kernel(
    parts_ref,
    projected_ref,
    emb_ref,
    bil_grad_ref,
    up_grad_ref,
    grad_project_ref,
    near_ref,
    far_ref,
    flat,
):
    members = parts_ref.shape[0]
    width, edges = projected_ref.shape
    per = edges // CAP
    grad_feat = jnp.zeros((width, edges), jnp.float32)
    for source in range(members):
        part = parts_ref[source].astype(jnp.float32)
        row = jnp.concatenate([part[width + at : width + at + 1] for at in range(per)], axis=1)
        grad_feat = grad_feat + dot32(part[:width].astype(jnp.bfloat16), rank_hot(row))
    grad_project = (grad_feat * silu_slope(projected_ref[...])).astype(jnp.bfloat16)
    grad_project_ref[...] = grad_project
    down_grad = dot32(grad_project, emb_ref[...]).astype(jnp.bfloat16)
    at = 0
    for term in (down_grad, bil_grad_ref[...], up_grad_ref[...]):
        for column in range(0, term.shape[1], CAP):
            flat[at : at + width, :] = term[:, column : column + CAP]
            at += width
    me = lax.axis_index("graph")
    rows = near_ref.shape[1]
    for pair in range(members // 2):
        near_ref[pair] = flat[pl.ds(pl.multiple_of((me ^ (2 * pair)) * rows, rows), rows), :]
        far_ref[pair] = flat[pl.ds(pl.multiple_of((me ^ (2 * pair + 1)) * rows, rows), rows), :]


def share_kernel(slab_ref, *refs):
    part_refs, out_ref = refs[:-1], refs[-1]
    total = part_refs[0][...].astype(jnp.float32)
    for part_ref in part_refs[1:]:
        total = total + part_ref[...].astype(jnp.float32)
    rows = total.shape[0]
    out_ref[:rows, :] = total.astype(jnp.bfloat16)
    slab = slab_ref[...]
    out_ref[rows:, :] = slab.reshape(slab.shape[0] * slab.shape[1], CAP)


def total_kernel(factor, *refs):
    parts = [part_ref[...].astype(jnp.float32) for part_ref in refs[:-1]]
    while len(parts) > 1:
        parts = [left + right for left, right in zip(parts[::2], parts[1::2])]
    refs[-1][...] = (parts[0] * factor).astype(jnp.bfloat16)


def last_kernel(members, *refs):
    part_refs, (down_ref, bil_ref, up_ref, atom_ref, flat) = restored(refs[:members]), refs[members:]
    me = lax.axis_index("graph")
    model = atom_ref.shape[1]
    rows = flat.shape[0] // members
    held = model // members
    for place, part_ref in enumerate(part_refs):
        source = me ^ place
        flat[pl.ds(pl.multiple_of(source * rows, rows), rows), :] = part_ref[:rows, :]
        for block in range(model // CAP):
            first = rows + block * held
            atom_ref[
                pl.ds(pl.multiple_of(source * held, held), held), block * CAP : (block + 1) * CAP
            ] = part_ref[first : first + held, :].astype(jnp.float32)
    at = 0
    for out in (down_ref, bil_ref, up_ref):
        width = out.shape[0]
        for column in range(0, out.shape[1], CAP):
            out[:, column : column + CAP] = flat[at : at + width, :].astype(jnp.float32)
            at += width


HBM = pl.BlockSpec(memory_space=pltpu.HBM)
VMEM = pl.BlockSpec(memory_space=pltpu.VMEM)
SMEM = pl.BlockSpec(memory_space=pltpu.SMEM)


def hbm(value):
    return pltpu.with_memory_space_constraint(value, pltpu.HBM)


def sending(count):
    falling = list(range(count))[::-1]
    return falling[1:2] + falling[:1] + falling[2:]


def places(count):
    return [2 * pair + 1 - odd for pair in sending(count // 2) for odd in range(2)]


def ordered(items):
    return [items[place] for place in places(len(items))]


def restored(items):
    found = dict(zip(places(len(items)), items))
    return [found[place] for place in range(len(items))]


def swap(value, members, mask, axis="graph"):
    return lax.ppermute(value, axis, [(at, at ^ mask) for at in range(members)])


def scatter_near(near, far, members):
    shape = jax.ShapeDtypeStruct(near.shape[1:], near.dtype)
    sums = pl.pallas_call(
        chip_kernel,
        out_shape=[shape] * (members // 2),
        compiler_params=params(),
        name="chip_sums",
    )(near, swap(far, members, 1))
    return [sums[0]] + [swap(part, members, 2 * at) for at, part in enumerate(sums) if at > 0]


def gather_near(value, members, beside=None):
    even = [value] + [swap(value, members, mask) for mask in range(2, members, 2)]
    if beside is not None:
        turn = sending(len(even))
        moved, beside = lax.optimization_barrier(([even[at] for at in turn], beside))
        even = [moved[turn.index(at)] for at in range(len(even))]
    odd = [swap(piece, members, 1) for piece in even]
    return [piece for pair in zip(even, odd) for piece in pair], beside


def params(limit=VMEM_BYTES):
    return pltpu.CompilerParams(vmem_limit_bytes=limit)


def cost(flops):
    return pl.CostEstimate(flops=flops, bytes_accessed=1 << 20, transcendentals=0)


def body(
    edge_emb,
    atom_emb,
    edge_target,
    trip_in,
    trip_out,
    trip_count,
    trip_basis,
    grad_edge,
    grad_atom,
    w_down,
    w_bil,
    w_up,
    w_atom,
):
    members = lax.axis_size("graph")
    edge_rows = edge_emb[0]
    edge_dev, model = edge_rows.shape
    atom_dev = atom_emb.shape[1]
    trips = trip_in.shape[1]
    width = w_down.shape[1]
    tile = math.gcd(trips, TILE_LIMIT)
    long = math.gcd(trips, FORWARD_LIMIT)
    f32, b16 = jnp.float32, jnp.bfloat16
    shaped = jax.ShapeDtypeStruct

    down_rows = w_down.T
    bil_rows = w_bil.T
    basis = trip_basis[0]
    projected, feat = pl.pallas_call(
        feature_kernel,
        in_specs=[HBM] * 2,
        out_shape=(
            shaped((width, edge_dev), f32),
            shaped((width, edge_dev), b16),
        ),
        scratch_shapes=[
            pltpu.VMEM(edge_rows.shape, b16),
            pltpu.VMEM(down_rows.shape, b16),
            pltpu.SemaphoreType.DMA((2,)),
        ],
        compiler_params=params(),
        cost_estimate=cost(16 * edge_rows.size * width),
        name="features",
    )(hbm(edge_rows), hbm(down_rows))
    rank_rows = members * edge_dev // CAP
    staged = (trip_out, basis, bil_rows, w_up, edge_rows, edge_target)
    slot, rank, back, *kept = pl.pallas_call(
        functools.partial(index_kernel, members),
        in_specs=[HBM] * (1 + len(staged)),
        out_shape=(
            shaped(trip_in.shape, jnp.int32),
            shaped((rank_rows, CAP), f32),
            shaped(bil_rows.shape, b16),
            *[shaped(value.shape, value.dtype) for value in staged],
        ),
        scratch_shapes=[
            pltpu.VMEM(trip_in.shape, jnp.int32),
            pltpu.VMEM((CAP, trips), b16),
            pltpu.VMEM((rank_rows, CAP), f32),
            pltpu.SemaphoreType.DMA((1 + len(staged),)),
        ],
        compiler_params=params(),
        cost_estimate=cost(8 * CAP * CAP * trips),
        name="slots",
    )(*[hbm(value) for value in (trip_in, *staged)])
    feats, (slot, rank, back, *kept) = gather_near(feat, members, (slot, rank, back, *kept))

    named_rows = members * CAP // BLOCK * width
    half = shaped((members // 2, atom_dev, model), b16)
    edge_new, near, far, gathered, picked = pl.pallas_call(
        functools.partial(forward_kernel, members),
        in_specs=[SMEM] + [VMEM] * (2 + len(kept) + members),
        out_specs=(VMEM, VMEM, VMEM, VMEM, HBM),
        out_shape=(
            shaped(edge_rows.shape, b16),
            half,
            half,
            shaped((width, edge_dev), b16),
            pltpu.HBM((width, trips), b16),
        ),
        scratch_shapes=[
            pltpu.VMEM((named_rows, BLOCK), b16),
            pltpu.VMEM((edge_dev // BLOCK * width, BLOCK), f32),
            pltpu.VMEM((w_bil.shape[0], long), b16),
            pltpu.VMEM((edge_dev // BLOCK * width, long), b16),
            pltpu.VMEM((width, trips), b16),
            pltpu.SemaphoreType.DMA((trips // long,)),
        ],
        compiler_params=params(),
        cost_estimate=cost(12 * w_bil.size * trips),
        name="forward_triplets",
    )(
        trip_count,
        slot,
        rank,
        *kept,
        *ordered(feats),
    )

    atom_block = shaped((atom_dev, model), b16)
    slope = pl.pallas_call(
        slope_kernel,
        out_shape=shaped(edge_rows.shape, f32),
        compiler_params=params(),
        cost_estimate=cost(64 * edge_rows.size * width),
        name="slopes",
    )(gathered, kept[3])
    sums = scatter_near(near, far, members)
    turn = sending(len(sums))
    moved, slope = lax.optimization_barrier(([sums[at] for at in turn], slope))
    sums = [moved[turn.index(at)] for at in range(len(sums))]
    atom_new, pair = pl.pallas_call(
        atom_kernel,
        out_shape=(atom_block, shaped((2, atom_dev, model), b16)),
        compiler_params=params(),
        cost_estimate=cost(16 * atom_dev * w_atom.size),
        name="atoms",
    )(atom_emb[0], grad_atom[0], w_atom, *[sums[at] for at in sending(len(sums))])
    pairs, _ = gather_near(pair, members)

    piece_rows = width + -(-(edge_dev // CAP) // 16) * 16
    grad_new, wup_term, mixed, feat_parts = pl.pallas_call(
        functools.partial(backward_kernel, members),
        in_specs=[SMEM] + [VMEM] * (11 + members),
        out_specs=(VMEM, VMEM, HBM, VMEM),
        out_shape=(
            shaped(edge_rows.shape, f32),
            shaped(w_up.shape, b16),
            pltpu.HBM((width, trips), b16),
            shaped((members, piece_rows, CAP), b16),
        ),
        scratch_shapes=[
            pltpu.VMEM((edge_dev // BLOCK * width, BLOCK), b16),
            pltpu.VMEM((w_bil.shape[0], tile), b16),
            pltpu.VMEM((named_rows, tile), b16),
            pltpu.VMEM((named_rows, BLOCK), f32),
            pltpu.VMEM((members * atom_dev, model), b16),
            pltpu.VMEM((width, trips), b16),
            pltpu.SemaphoreType.DMA((trips // tile,)),
        ],
        compiler_params=params(),
        cost_estimate=cost(12 * w_bil.size * trips),
        name="backward_triplets",
    )(
        trip_count,
        slot,
        kept[0],
        kept[1],
        rank,
        back,
        kept[3],
        gathered,
        slope,
        grad_edge[0],
        kept[5],
        w_atom,
        *ordered(pairs),
    )
    feat_parts = lax.all_to_all(feat_parts, "graph", 0, 0, tiled=True)
    wide = math.gcd(trips, 2 * tile)
    wbil_term = pl.pallas_call(
        weight_kernel,
        in_specs=[VMEM, HBM, HBM],
        out_shape=shaped((width, w_bil.shape[0]), b16),
        scratch_shapes=[
            pltpu.VMEM((width, trips), b16),
            pltpu.VMEM((width, trips), b16),
            pltpu.VMEM((w_bil.shape[0] + 2 * width - BLOCK, wide), b16),
            pltpu.VMEM((BLOCK, wide), b16),
            pltpu.VMEM((w_bil.shape[0] + 2 * width - BLOCK, BLOCK), f32),
            pltpu.SemaphoreType.DMA((2, trips // wide)),
        ],
        compiler_params=params(),
        cost_estimate=cost(8 * w_bil.size * trips),
        name="bilinear_weights",
    )(kept[1], hbm(picked), hbm(mixed))
    flat_rows = width * (2 * model + w_bil.shape[0]) // CAP
    piece = shaped((members // 2, flat_rows // members, CAP), b16)
    grad_project, near, far = pl.pallas_call(
        edge_kernel,
        out_shape=(shaped((width, edge_dev), b16), piece, piece),
        scratch_shapes=[pltpu.VMEM((flat_rows, CAP), b16)],
        compiler_params=params(),
        cost_estimate=cost(64 * edge_rows.size * width),
        name="edges",
    )(feat_parts, projected, edge_rows, wbil_term, wup_term)
    grad_in = pl.pallas_call(
        input_kernel,
        out_shape=shaped(edge_rows.shape, f32),
        compiler_params=params(),
        cost_estimate=cost(64 * edge_rows.size * width),
        name="input_grads",
    )(grad_project, down_rows, grad_new)

    slab = pl.pallas_call(
        functools.partial(slab_kernel, members),
        out_shape=shaped((model // CAP, model // members, CAP), b16),
        scratch_shapes=[
            pltpu.VMEM((members * atom_dev, model), b16),
            pltpu.VMEM((members * atom_dev, model), b16),
            pltpu.VMEM((model, model), f32),
        ],
        compiler_params=params(),
        cost_estimate=cost(16 * members * atom_dev * w_atom.size),
        name="atom_slab",
    )(*pairs)
    batches = lax.axis_size("dp")
    factor = 1.0 / math.sqrt(batches * members * edge_dev)
    share_rows = (flat_rows + model * model // CAP) // members
    flat_sums = scatter_near(near, far, members)
    moved, slab, grad_in = lax.optimization_barrier(
        ([flat_sums[at] for at in turn], slab, grad_in)
    )
    flat_sums = [moved[turn.index(at)] for at in range(len(sums))]
    share = pl.pallas_call(
        share_kernel,
        out_shape=shaped((share_rows, CAP), b16),
        compiler_params=params(),
        name="share",
    )(slab, *[flat_sums[at] for at in sending(len(flat_sums))])
    share = pl.pallas_call(
        functools.partial(total_kernel, factor),
        out_shape=shaped((share_rows, CAP), b16),
        compiler_params=params(),
        name="total",
    )(*[swap(share, batches, mask, "dp") for mask in range(batches - 1, 0, -1)], share)
    shares, _ = gather_near(share, members)
    grad_wdown, grad_wbil, grad_wup, grad_watom = pl.pallas_call(
        functools.partial(last_kernel, members),
        out_shape=(
            shaped((width, model), f32),
            shaped((width, w_bil.shape[0]), f32),
            shaped(w_up.shape, f32),
            shaped((model, model), f32),
        ),
        scratch_shapes=[pltpu.VMEM((flat_rows, CAP), b16)],
        compiler_params=params(),
        name="weights",
    )(*ordered(shares))
    return (
        edge_new[None],
        atom_new[None],
        grad_in[None],
        grad_wdown.T,
        grad_wbil.T,
        grad_wup,
        grad_watom,
    )


def solution(mesh):
    return jax.shard_map(
        body,
        mesh=mesh,
        in_specs=(
            P("dp", "graph", None),
            P("dp", "graph", None),
            P("dp", "graph"),
            P("dp", "graph"),
            P("dp", "graph"),
            P("dp", "graph"),
            P("dp", None, "graph"),
            P("dp", "graph", None),
            P("dp", "graph", None),
            P(),
            P(),
            P(),
            P(),
        ),
        out_specs=(
            P("dp", "graph", None),
            P("dp", "graph", None),
            P("dp", "graph", None),
            P(),
            P(),
            P(),
            P(),
        ),
        check_vma=False,
    )
```

```python
import functools
import math

import jax
import jax.numpy as jnp
from jax import lax
from jax.experimental import pallas as pl
from jax.experimental.pallas import tpu as pltpu
from jax.sharding import PartitionSpec as P

ATOM_SCALE = 0.25
BLOCK = 256
CAP = 128
TILE_LIMIT = 4096
FORWARD_LIMIT = 8192
INDEX_TILE = 2048
VMEM_BYTES = 32 * 1024 * 1024

FIRST_FIRST = (((0,), (0,)), ((), ()))
LAST_LAST = (((1,), (1,)), ((), ()))


def dot32(left, right, dims=(((1,), (0,)), ((), ()))):
    return lax.dot_general(left, right, dims, preferred_element_type=jnp.float32)


def silu(value):
    return value / (1.0 + jnp.exp(-value))


def silu_slope(value):
    logistic = 1.0 / (1.0 + jnp.exp(-value))
    return logistic * (1.0 + value * (1.0 - logistic))


def row_hot(rows, index):
    iota = lax.broadcasted_iota(jnp.int32, (rows, index.shape[1]), 0)
    if rows > BLOCK:
        return (iota == index).astype(jnp.float32).astype(jnp.bfloat16)
    match = iota.astype(jnp.bfloat16) == index.astype(jnp.bfloat16)
    return jnp.where(match, jnp.bfloat16(1), jnp.bfloat16(0))


def start_copies(pairs, sems):
    copies = [
        pltpu.make_async_copy(source, target, sems.at[place])
        for place, (source, target) in enumerate(pairs)
    ]
    for copy in copies:
        copy.start()
    return copies


def tile_copy(source, target, sems, step, tile):
    span = pl.ds(pl.multiple_of(step * tile, tile), tile)
    return pltpu.make_async_copy(source.at[:, span], target.at[:, span], sems.at[step])


def feature_kernel(emb_hbm, down_hbm, projected_ref, feat_ref, emb_ref, down_ref, sems):
    for copy in start_copies(((emb_hbm, emb_ref), (down_hbm, down_ref)), sems):
        copy.wait()
    projected = dot32(down_ref[...], emb_ref[...], LAST_LAST)
    projected_ref[...] = projected
    feat_ref[...] = silu(projected).astype(jnp.bfloat16)


def index_kernel(members, in_hbm, *refs):
    held = (len(refs) - 7) // 2
    staged, (slot_ref, rank_ref, back_ref) = refs[:held], refs[held : held + 3]
    kept = refs[held + 3 : -4]
    in_ref, hots, counts, sems = refs[-4:]
    copy, *copies = start_copies(((in_hbm, in_ref), *zip(staged, kept)), sems)
    trips = in_ref.shape[1]
    rows = rank_ref.shape[0]
    turn = lax.axis_index("graph") * (rows // members * CAP)
    tile = math.gcd(trips, INDEX_TILE)
    spans = [slice(at, at + tile) for at in range(0, trips, tile)]
    counts[...] = jnp.zeros_like(counts)
    copy.wait()
    for span in spans:
        incoming = in_ref[:, span] ^ turn
        hot = row_hot(CAP, incoming & (CAP - 1))
        hots[:, span] = hot
        counts[...] += dot32(row_hot(rows, incoming // CAP), hot, LAST_LAST)
    named = (counts[...] > 0.0).astype(jnp.float32)
    per = rows // members
    ahead = (
        lax.broadcasted_iota(jnp.int32, (CAP, CAP), 0)
        < lax.broadcasted_iota(jnp.int32, (CAP, CAP), 1)
    ).astype(jnp.bfloat16)
    row = lax.broadcasted_iota(jnp.int32, (rows, rows), 0)
    other = lax.broadcasted_iota(jnp.int32, (rows, rows), 1)
    above = ((other < row) & (other // per == row // per)).astype(jnp.bfloat16)
    sums = dot32(above, named.astype(jnp.bfloat16))
    before = jnp.sum(sums, axis=1, keepdims=True)
    rank = dot32(named.astype(jnp.bfloat16), ahead) + before
    rank = jnp.where(named > 0.0, rank, -1.0)
    rank_ref[...] = rank
    lookup = rank.astype(jnp.bfloat16)
    for span in spans:
        incoming = in_ref[:, span] ^ turn
        place = incoming // CAP
        found = dot32(lookup, hots[:, span])
        iota = lax.broadcasted_iota(jnp.int32, found.shape, 0)
        found = jnp.sum(jnp.where(iota == place, found, 0.0), axis=0, keepdims=True)
        slot_ref[:, span] = (place // per) * CAP + found.astype(jnp.int32)
    for copy in copies:
        copy.wait()
    bil_ref = kept[2]
    width = bil_ref.shape[0]
    turned = bil_ref[...].astype(jnp.float32).T
    back_ref[...] = jnp.concatenate(
        [turned[at : at + width] for at in range(0, turned.shape[0], width)], axis=1
    ).astype(jnp.bfloat16)


def rank_row(rank_ref, source, per):
    return jnp.concatenate(
        [rank_ref[source * per + part : source * per + part + 1, :] for part in range(per)], axis=1
    )


def rank_hot(row):
    iota = lax.broadcasted_iota(jnp.int32, (CAP, row.shape[1]), 0).astype(jnp.float32)
    return (iota == row).astype(jnp.float32).astype(jnp.bfloat16)


def forward_kernel(
    members,
    count_ref,
    slot_ref,
    rank_ref,
    *refs,
):
    out_ref, basis_ref, bil_ref, up_ref, emb_ref, target_ref, *refs = refs
    feat_refs, refs = restored(refs[:members]), refs[members:]
    new_ref, near_ref, far_ref, gathered_ref, picked_hbm, *refs = refs
    table, total, spread, masked, picked_ref, sems = refs
    trips = slot_ref.shape[1]
    tile = spread.shape[1]
    width = bil_ref.shape[0]
    edges = emb_ref.shape[0]
    groups = table.shape[0] // width
    per = BLOCK // width
    count = count_ref[0, 0]
    total[...] = jnp.zeros_like(total)
    for source in range(members):
        row = rank_row(rank_ref, source, edges // CAP)
        chosen = dot32(feat_refs[source][...], rank_hot(row), LAST_LAST)
        group, lane = divmod(source * CAP, BLOCK)
        table[group * width : (group + 1) * width, lane : lane + CAP] = chosen.astype(jnp.bfloat16)

    def one_tile(step, carry):
        span = pl.ds(pl.multiple_of(step * tile, tile), tile)
        slot = slot_ref[:, span]
        high = slot // BLOCK
        hot = row_hot(BLOCK, slot & (BLOCK - 1))
        feat = jnp.zeros((width, tile), jnp.float32)
        for chunk in range(groups // per):
            picked = dot32(table[chunk * BLOCK : (chunk + 1) * BLOCK, :], hot)
            for part in range(per):
                feat = jnp.where(
                    high == chunk * per + part, picked[part * width : (part + 1) * width, :], feat
                )
        feat = feat.astype(jnp.bfloat16)
        picked_ref[:, span] = feat
        tile_copy(picked_ref, picked_hbm, sems, step, tile).start()
        basis = basis_ref[:, span]
        for row in range(basis.shape[0]):
            spread[row * width : (row + 1) * width, :] = feat * basis[row : row + 1, :]
        place = step * tile + lax.broadcasted_iota(jnp.int32, (1, tile), 1)
        outgoing = out_ref[:, span]
        high = jnp.where(place < count, outgoing // BLOCK, -1)
        mixed = dot32(bil_ref[...], spread[...])
        for part in range(edges // BLOCK):
            masked[part * width : (part + 1) * width, :] = jnp.where(
                high == part, mixed, 0.0
            ).astype(jnp.bfloat16)
        total[...] += dot32(masked[...], row_hot(BLOCK, outgoing & (BLOCK - 1)), LAST_LAST)
        return carry

    lax.fori_loop(0, trips // tile, one_tile, 0)
    for step in range(trips // tile):
        tile_copy(picked_ref, picked_hbm, sems, step, tile).wait()
    gathered = jnp.concatenate(
        [total[at : at + width, :] for at in range(0, total.shape[0], width)], axis=1
    ).astype(jnp.bfloat16)
    gathered_ref[...] = gathered
    update = dot32(gathered, up_ref[...], FIRST_FIRST)
    fresh = (emb_ref[...].astype(jnp.float32) + silu(update)).astype(jnp.bfloat16)
    new_ref[...] = fresh
    held = near_ref.shape[1]
    turn = lax.axis_index("graph") * held
    sums = dot32(row_hot(members * held, target_ref[...] ^ turn), fresh)
    for pair in range(members // 2):
        near_ref[pair] = sums[2 * pair * held : (2 * pair + 1) * held].astype(jnp.bfloat16)
        far_ref[pair] = sums[(2 * pair + 1) * held : (2 * pair + 2) * held].astype(jnp.bfloat16)


def chip_kernel(near_ref, far_ref, *out_refs):
    for pair, out_ref in enumerate(out_refs):
        out_ref[...] = (
            near_ref[pair].astype(jnp.float32) + far_ref[pair].astype(jnp.float32)
        ).astype(jnp.bfloat16)


def atom_kernel(emb_ref, grad_ref, weight_ref, *refs):
    part_refs, (new_ref, pair_ref) = refs[:-2], refs[-2:]
    total = part_refs[0][...].astype(jnp.float32)
    for part_ref in part_refs[1:]:
        total = total + part_ref[...].astype(jnp.float32)
    total = total.astype(jnp.bfloat16)
    pre = ATOM_SCALE * dot32(total, weight_ref[...])
    new_ref[...] = (emb_ref[...].astype(jnp.float32) + silu(pre)).astype(jnp.bfloat16)
    grad_pre = (grad_ref[...].astype(jnp.float32) * silu_slope(pre)).astype(jnp.bfloat16)
    pair_ref[0] = total
    pair_ref[1] = grad_pre


def slope_kernel(gathered_ref, up_ref, slope_ref):
    slope_ref[...] = silu_slope(dot32(gathered_ref[...], up_ref[...], FIRST_FIRST))


def slab_kernel(members, *refs):
    pair_refs, (slab_ref, sums, grads, atom_grad) = refs[:members], refs[members:]
    me = lax.axis_index("graph")
    held, model = pair_refs[0].shape[1:]
    for source, pair_ref in enumerate(pair_refs):
        sums[source * held : (source + 1) * held, :] = pair_ref[0]
        grads[source * held : (source + 1) * held, :] = pair_ref[1]
    atom_grad[...] = ATOM_SCALE * dot32(sums[...], grads[...], FIRST_FIRST)
    share = model // members
    mine = atom_grad[pl.ds(pl.multiple_of(me * share, share), share), :]
    for column in range(0, model, CAP):
        slab_ref[column // CAP] = mine[:, column : column + CAP].astype(jnp.bfloat16)


def backward_kernel(
    members,
    count_ref,
    slot_ref,
    out_ref,
    basis_ref,
    rank_ref,
    back_ref,
    up_ref,
    gathered_ref,
    slope_ref,
    grad_edge_ref,
    target_ref,
    atom_weight_ref,
    *refs,
):
    pair_refs, refs = restored(refs[:members]), refs[members:]
    grad_new_ref, up_grad_ref, mixed_hbm, parts_ref, *refs = refs
    table, spread, masked, total, grads, mixed_ref, sems = refs
    trips = slot_ref.shape[1]
    tile = spread.shape[1]
    width = back_ref.shape[0]
    edges = grad_edge_ref.shape[0]
    groups = total.shape[0] // width
    count = count_ref[0, 0]
    me = lax.axis_index("graph")
    held = pair_refs[0].shape[1]
    for source, pair_ref in enumerate(pair_refs):
        grads[source * held : (source + 1) * held, :] = pair_ref[1]
    grad_sum = (ATOM_SCALE * dot32(grads[...], atom_weight_ref[...], LAST_LAST)).astype(
        jnp.bfloat16
    )
    total[...] = jnp.zeros_like(total)
    hot = row_hot(members * held, target_ref[...] ^ (me * held))
    grad_new = grad_edge_ref[...].astype(jnp.float32) + dot32(hot, grad_sum, FIRST_FIRST)
    grad_new_ref[...] = grad_new
    grad_update = (grad_new * slope_ref[...]).astype(jnp.bfloat16)
    up_grad_ref[...] = dot32(gathered_ref[...], grad_update).astype(jnp.bfloat16)
    grad_gathered = dot32(up_ref[...], grad_update, LAST_LAST).astype(jnp.bfloat16)
    for part in range(edges // BLOCK):
        table[part * width : (part + 1) * width, :] = grad_gathered[
            :, part * BLOCK : (part + 1) * BLOCK
        ]

    def one_tile(step, carry):
        span = pl.ds(pl.multiple_of(step * tile, tile), tile)
        place = step * tile + lax.broadcasted_iota(jnp.int32, (1, tile), 1)
        outgoing = jnp.where(place < count, out_ref[:, span], -1)
        picked = dot32(table[...], row_hot(BLOCK, outgoing & (BLOCK - 1)))
        high = jnp.where(outgoing >= 0, outgoing // BLOCK, -1)
        grad = jnp.zeros((width, tile), jnp.float32)
        for part in range(edges // BLOCK):
            grad = jnp.where(high == part, picked[part * width : (part + 1) * width, :], grad)
        grad = grad.astype(jnp.bfloat16)
        mixed_ref[:, span] = grad
        tile_copy(mixed_ref, mixed_hbm, sems, step, tile).start()
        basis = basis_ref[:, span]
        for row in range(basis.shape[0]):
            spread[row * width : (row + 1) * width, :] = grad * basis[row : row + 1, :]
        feat_grad = dot32(back_ref[...], spread[...])
        slot = slot_ref[:, span]
        high_in = slot // BLOCK
        for part in range(groups):
            masked[part * width : (part + 1) * width, :] = jnp.where(
                high_in == part, feat_grad, 0.0
            ).astype(jnp.bfloat16)
        total[...] += dot32(masked[...], row_hot(BLOCK, slot & (BLOCK - 1)), LAST_LAST)
        return carry

    lax.fori_loop(0, trips // tile, one_tile, 0)
    for step in range(trips // tile):
        tile_copy(mixed_ref, mixed_hbm, sems, step, tile).wait()
    per = rank_ref.shape[0] // members
    for source in range(members):
        group, lane = divmod(source * CAP, BLOCK)
        piece = total[group * width : (group + 1) * width, lane : lane + CAP]
        ranks = rank_ref[source * per : (source + 1) * per, :]
        spare = jnp.zeros((parts_ref.shape[1] - width - per, CAP), jnp.float32)
        parts_ref[me ^ source] = jnp.concatenate([piece, ranks, spare], axis=0).astype(jnp.bfloat16)


def weight_kernel(
    basis_ref, picked_hbm, mixed_hbm, out_ref, picked, mixed, spread, scaled, total, sems
):
    width, trips = picked.shape
    tile = spread.shape[1]
    steps = trips // tile
    moved = scaled.shape[0] // width - 1
    for step in range(steps):
        tile_copy(picked_hbm, picked, sems.at[0], step, tile).start()
        tile_copy(mixed_hbm, mixed, sems.at[1], step, tile).start()
    total[...] = jnp.zeros_like(total)

    def one_tile(step, carry):
        span = pl.ds(pl.multiple_of(step * tile, tile), tile)
        basis = basis_ref[:, span]
        tile_copy(picked_hbm, picked, sems.at[0], step, tile).wait()
        tile_copy(mixed_hbm, mixed, sems.at[1], step, tile).wait()
        feat = picked[:, span]
        spread[:width, :] = feat
        for row in range(moved, basis.shape[0]):
            at = (row - moved + 1) * width
            spread[at : at + width, :] = feat * basis[row : row + 1, :]
        grad = mixed[:, span]
        scaled[:width, :] = grad
        for row in range(moved):
            at = (row + 1) * width
            scaled[at : at + width, :] = grad * basis[row : row + 1, :]
        total[...] += dot32(spread[...], scaled[...], LAST_LAST)
        return carry

    lax.fori_loop(0, steps, one_tile, 0)
    first = [total[:width, (row + 1) * width : (row + 2) * width] for row in range(moved)]
    whole = jnp.concatenate([*first, total[width:, :width]], axis=0)
    out_ref[...] = whole.T.astype(jnp.bfloat16)


def input_kernel(grad_project_ref, down_ref, grad_new_ref, grad_in_ref):
    grad_in_ref[...] = grad_new_ref[...] + dot32(
        grad_project_ref[...], down_ref[...], FIRST_FIRST
    )


def edge_kernel(
    parts_ref,
    projected_ref,
    emb_ref,
    bil_grad_ref,
    up_grad_ref,
    grad_project_ref,
    near_ref,
    far_ref,
    flat,
):
    members = parts_ref.shape[0]
    width, edges = projected_ref.shape
    per = edges // CAP
    grad_feat = jnp.zeros((width, edges), jnp.float32)
    for source in range(members):
        part = parts_ref[source].astype(jnp.float32)
        row = jnp.concatenate([part[width + at : width + at + 1] for at in range(per)], axis=1)
        grad_feat = grad_feat + dot32(part[:width].astype(jnp.bfloat16), rank_hot(row))
    grad_project = (grad_feat * silu_slope(projected_ref[...])).astype(jnp.bfloat16)
    grad_project_ref[...] = grad_project
    down_grad = dot32(grad_project, emb_ref[...]).astype(jnp.bfloat16)
    at = 0
    for term in (down_grad, bil_grad_ref[...], up_grad_ref[...]):
        for column in range(0, term.shape[1], CAP):
            flat[at : at + width, :] = term[:, column : column + CAP]
            at += width
    me = lax.axis_index("graph")
    rows = near_ref.shape[1]
    for pair in range(members // 2):
        near_ref[pair] = flat[pl.ds(pl.multiple_of((me ^ (2 * pair)) * rows, rows), rows), :]
        far_ref[pair] = flat[pl.ds(pl.multiple_of((me ^ (2 * pair + 1)) * rows, rows), rows), :]


def share_kernel(slab_ref, *refs):
    part_refs, out_ref = refs[:-1], refs[-1]
    total = part_refs[0][...].astype(jnp.float32)
    for part_ref in part_refs[1:]:
        total = total + part_ref[...].astype(jnp.float32)
    rows = total.shape[0]
    out_ref[:rows, :] = total.astype(jnp.bfloat16)
    slab = slab_ref[...]
    out_ref[rows:, :] = slab.reshape(slab.shape[0] * slab.shape[1], CAP)


def total_kernel(factor, *refs):
    parts = [part_ref[...].astype(jnp.float32) for part_ref in refs[:-1]]
    while len(parts) > 1:
        parts = [left + right for left, right in zip(parts[::2], parts[1::2])]
    refs[-1][...] = (parts[0] * factor).astype(jnp.bfloat16)


def last_kernel(members, *refs):
    part_refs, (down_ref, bil_ref, up_ref, atom_ref, flat) = restored(refs[:members]), refs[members:]
    me = lax.axis_index("graph")
    model = atom_ref.shape[1]
    rows = flat.shape[0] // members
    held = model // members
    for place, part_ref in enumerate(part_refs):
        source = me ^ place
        flat[pl.ds(pl.multiple_of(source * rows, rows), rows), :] = part_ref[:rows, :]
        for block in range(model // CAP):
            first = rows + block * held
            atom_ref[
                pl.ds(pl.multiple_of(source * held, held), held), block * CAP : (block + 1) * CAP
            ] = part_ref[first : first + held, :].astype(jnp.float32)
    at = 0
    for out in (down_ref, bil_ref, up_ref):
        width = out.shape[0]
        for column in range(0, out.shape[1], CAP):
            out[:, column : column + CAP] = flat[at : at + width, :].astype(jnp.float32)
            at += width


HBM = pl.BlockSpec(memory_space=pltpu.HBM)
VMEM = pl.BlockSpec(memory_space=pltpu.VMEM)
SMEM = pl.BlockSpec(memory_space=pltpu.SMEM)


def hbm(value):
    return pltpu.with_memory_space_constraint(value, pltpu.HBM)


def sending(count):
    falling = list(range(count))[::-1]
    return falling[1:2] + falling[:1] + falling[2:]


def places(count):
    return [2 * pair + 1 - odd for pair in sending(count // 2) for odd in range(2)]


def ordered(items):
    return [items[place] for place in places(len(items))]


def restored(items):
    found = dict(zip(places(len(items)), items))
    return [found[place] for place in range(len(items))]


def swap(value, members, mask, axis="graph"):
    return lax.ppermute(value, axis, [(at, at ^ mask) for at in range(members)])


def scatter_near(near, far, members):
    shape = jax.ShapeDtypeStruct(near.shape[1:], near.dtype)
    sums = pl.pallas_call(
        chip_kernel,
        out_shape=[shape] * (members // 2),
        compiler_params=params(),
        name="chip_sums",
    )(near, swap(far, members, 1))
    return [sums[0]] + [swap(part, members, 2 * at) for at, part in enumerate(sums) if at > 0]


def gather_near(value, members, beside=None):
    even = [value] + [swap(value, members, mask) for mask in range(2, members, 2)]
    if beside is not None:
        turn = sending(len(even))
        moved, beside = lax.optimization_barrier(([even[at] for at in turn], beside))
        even = [moved[turn.index(at)] for at in range(len(even))]
    odd = [swap(piece, members, 1) for piece in even]
    return [piece for pair in zip(even, odd) for piece in pair], beside


def params(limit=VMEM_BYTES):
    return pltpu.CompilerParams(vmem_limit_bytes=limit)


def cost(flops):
    return pl.CostEstimate(flops=flops, bytes_accessed=1 << 20, transcendentals=0)


def body(
    edge_emb,
    atom_emb,
    edge_target,
    trip_in,
    trip_out,
    trip_count,
    trip_basis,
    grad_edge,
    grad_atom,
    w_down,
    w_bil,
    w_up,
    w_atom,
):
    members = lax.axis_size("graph")
    edge_rows = edge_emb[0]
    edge_dev, model = edge_rows.shape
    atom_dev = atom_emb.shape[1]
    trips = trip_in.shape[1]
    width = w_down.shape[1]
    tile = math.gcd(trips, TILE_LIMIT)
    long = math.gcd(trips, FORWARD_LIMIT)
    f32, b16 = jnp.float32, jnp.bfloat16
    shaped = jax.ShapeDtypeStruct

    down_rows = w_down.T
    bil_rows = w_bil.T
    basis = trip_basis[0]
    projected, feat = pl.pallas_call(
        feature_kernel,
        in_specs=[HBM] * 2,
        out_shape=(
            shaped((width, edge_dev), f32),
            shaped((width, edge_dev), b16),
        ),
        scratch_shapes=[
            pltpu.VMEM(edge_rows.shape, b16),
            pltpu.VMEM(down_rows.shape, b16),
            pltpu.SemaphoreType.DMA((2,)),
        ],
        compiler_params=params(),
        cost_estimate=cost(16 * edge_rows.size * width),
        name="features",
    )(hbm(edge_rows), hbm(down_rows))
    rank_rows = members * edge_dev // CAP
    staged = (trip_out, basis, bil_rows, w_up, edge_rows, edge_target)
    slot, rank, back, *kept = pl.pallas_call(
        functools.partial(index_kernel, members),
        in_specs=[HBM] * (1 + len(staged)),
        out_shape=(
            shaped(trip_in.shape, jnp.int32),
            shaped((rank_rows, CAP), f32),
            shaped(bil_rows.shape, b16),
            *[shaped(value.shape, value.dtype) for value in staged],
        ),
        scratch_shapes=[
            pltpu.VMEM(trip_in.shape, jnp.int32),
            pltpu.VMEM((CAP, trips), b16),
            pltpu.VMEM((rank_rows, CAP), f32),
            pltpu.SemaphoreType.DMA((1 + len(staged),)),
        ],
        compiler_params=params(),
        cost_estimate=cost(8 * CAP * CAP * trips),
        name="slots",
    )(*[hbm(value) for value in (trip_in, *staged)])
    feats, (slot, rank, back, *kept) = gather_near(feat, members, (slot, rank, back, *kept))

    named_rows = members * CAP // BLOCK * width
    half = shaped((members // 2, atom_dev, model), b16)
    edge_new, near, far, gathered, picked = pl.pallas_call(
        functools.partial(forward_kernel, members),
        in_specs=[SMEM] + [VMEM] * (2 + len(kept) + members),
        out_specs=(VMEM, VMEM, VMEM, VMEM, HBM),
        out_shape=(
            shaped(edge_rows.shape, b16),
            half,
            half,
            shaped((width, edge_dev), b16),
            pltpu.HBM((width, trips), b16),
        ),
        scratch_shapes=[
            pltpu.VMEM((named_rows, BLOCK), b16),
            pltpu.VMEM((edge_dev // BLOCK * width, BLOCK), f32),
            pltpu.VMEM((w_bil.shape[0], long), b16),
            pltpu.VMEM((edge_dev // BLOCK * width, long), b16),
            pltpu.VMEM((width, trips), b16),
            pltpu.SemaphoreType.DMA((trips // long,)),
        ],
        compiler_params=params(),
        cost_estimate=cost(12 * w_bil.size * trips),
        name="forward_triplets",
    )(
        trip_count,
        slot,
        rank,
        *kept,
        *ordered(feats),
    )

    atom_block = shaped((atom_dev, model), b16)
    slope = pl.pallas_call(
        slope_kernel,
        out_shape=shaped(edge_rows.shape, f32),
        compiler_params=params(),
        cost_estimate=cost(64 * edge_rows.size * width),
        name="slopes",
    )(gathered, kept[3])
    sums = scatter_near(near, far, members)
    turn = sending(len(sums))
    moved, slope = lax.optimization_barrier(([sums[at] for at in turn], slope))
    sums = [moved[turn.index(at)] for at in range(len(sums))]
    atom_new, pair = pl.pallas_call(
        atom_kernel,
        out_shape=(atom_block, shaped((2, atom_dev, model), b16)),
        compiler_params=params(),
        cost_estimate=cost(16 * atom_dev * w_atom.size),
        name="atoms",
    )(atom_emb[0], grad_atom[0], w_atom, *[sums[at] for at in sending(len(sums))])
    pairs, _ = gather_near(pair, members)

    piece_rows = width + -(-(edge_dev // CAP) // 16) * 16
    grad_new, wup_term, mixed, feat_parts = pl.pallas_call(
        functools.partial(backward_kernel, members),
        in_specs=[SMEM] + [VMEM] * (11 + members),
        out_specs=(VMEM, VMEM, HBM, VMEM),
        out_shape=(
            shaped(edge_rows.shape, f32),
            shaped(w_up.shape, b16),
            pltpu.HBM((width, trips), b16),
            shaped((members, piece_rows, CAP), b16),
        ),
        scratch_shapes=[
            pltpu.VMEM((edge_dev // BLOCK * width, BLOCK), b16),
            pltpu.VMEM((w_bil.shape[0], tile), b16),
            pltpu.VMEM((named_rows, tile), b16),
            pltpu.VMEM((named_rows, BLOCK), f32),
            pltpu.VMEM((members * atom_dev, model), b16),
            pltpu.VMEM((width, trips), b16),
            pltpu.SemaphoreType.DMA((trips // tile,)),
        ],
        compiler_params=params(),
        cost_estimate=cost(12 * w_bil.size * trips),
        name="backward_triplets",
    )(
        trip_count,
        slot,
        kept[0],
        kept[1],
        rank,
        back,
        kept[3],
        gathered,
        slope,
        grad_edge[0],
        kept[5],
        w_atom,
        *ordered(pairs),
    )
    feat_parts = lax.all_to_all(feat_parts, "graph", 0, 0, tiled=True)
    wide = math.gcd(trips, 2 * tile)
    wbil_term = pl.pallas_call(
        weight_kernel,
        in_specs=[VMEM, HBM, HBM],
        out_shape=shaped((width, w_bil.shape[0]), b16),
        scratch_shapes=[
            pltpu.VMEM((width, trips), b16),
            pltpu.VMEM((width, trips), b16),
            pltpu.VMEM((w_bil.shape[0] + 2 * width - BLOCK, wide), b16),
            pltpu.VMEM((BLOCK, wide), b16),
            pltpu.VMEM((w_bil.shape[0] + 2 * width - BLOCK, BLOCK), f32),
            pltpu.SemaphoreType.DMA((2, trips // wide)),
        ],
        compiler_params=params(),
        cost_estimate=cost(8 * w_bil.size * trips),
        name="bilinear_weights",
    )(kept[1], hbm(picked), hbm(mixed))
    flat_rows = width * (2 * model + w_bil.shape[0]) // CAP
    piece = shaped((members // 2, flat_rows // members, CAP), b16)
    grad_project, near, far = pl.pallas_call(
        edge_kernel,
        out_shape=(shaped((width, edge_dev), b16), piece, piece),
        scratch_shapes=[pltpu.VMEM((flat_rows, CAP), b16)],
        compiler_params=params(),
        cost_estimate=cost(64 * edge_rows.size * width),
        name="edges",
    )(feat_parts, projected, edge_rows, wbil_term, wup_term)
    grad_in = pl.pallas_call(
        input_kernel,
        out_shape=shaped(edge_rows.shape, f32),
        compiler_params=params(),
        cost_estimate=cost(64 * edge_rows.size * width),
        name="input_grads",
    )(grad_project, down_rows, grad_new)

    slab = pl.pallas_call(
        functools.partial(slab_kernel, members),
        out_shape=shaped((model // CAP, model // members, CAP), b16),
        scratch_shapes=[
            pltpu.VMEM((members * atom_dev, model), b16),
            pltpu.VMEM((members * atom_dev, model), b16),
            pltpu.VMEM((model, model), f32),
        ],
        compiler_params=params(),
        cost_estimate=cost(16 * members * atom_dev * w_atom.size),
        name="atom_slab",
    )(*pairs)
    batches = lax.axis_size("dp")
    factor = 1.0 / math.sqrt(batches * members * edge_dev)
    share_rows = (flat_rows + model * model // CAP) // members
    flat_sums = scatter_near(near, far, members)
    moved, slab, grad_in = lax.optimization_barrier(
        ([flat_sums[at] for at in turn], slab, grad_in)
    )
    flat_sums = [moved[turn.index(at)] for at in range(len(sums))]
    share = pl.pallas_call(
        share_kernel,
        out_shape=shaped((share_rows, CAP), b16),
        compiler_params=params(),
        name="share",
    )(slab, *[flat_sums[at] for at in sending(len(flat_sums))])
    share = pl.pallas_call(
        functools.partial(total_kernel, factor),
        out_shape=shaped((share_rows, CAP), b16),
        compiler_params=params(),
        name="total",
    )(*[swap(share, batches, mask, "dp") for mask in sending(batches)[:-1]], share)
    shares, _ = gather_near(share, members)
    grad_wdown, grad_wbil, grad_wup, grad_watom = pl.pallas_call(
        functools.partial(last_kernel, members),
        out_shape=(
            shaped((width, model), f32),
            shaped((width, w_bil.shape[0]), f32),
            shaped(w_up.shape, f32),
            shaped((model, model), f32),
        ),
        scratch_shapes=[pltpu.VMEM((flat_rows, CAP), b16)],
        compiler_params=params(),
        name="weights",
    )(*ordered(shares))
    return (
        edge_new[None],
        atom_new[None],
        grad_in[None],
        grad_wdown.T,
        grad_wbil.T,
        grad_wup,
        grad_watom,
    )


def solution(mesh):
    return jax.shard_map(
        body,
        mesh=mesh,
        in_specs=(
            P("dp", "graph", None),
            P("dp", "graph", None),
            P("dp", "graph"),
            P("dp", "graph"),
            P("dp", "graph"),
            P("dp", "graph"),
            P("dp", None, "graph"),
            P("dp", "graph", None),
            P("dp", "graph", None),
            P(),
            P(),
            P(),
            P(),
        ),
        out_specs=(
            P("dp", "graph", None),
            P("dp", "graph", None),
            P("dp", "graph", None),
            P(),
            P(),
            P(),
            P(),
        ),
        check_vma=False,
    )
```
